128 devices in a mesh: azim: 32 (over y, z, core), rad: 4 (over x).
Axes of the slice: x: 4, y: 4, z: 4, core: 2. Of those that a mesh axis runs over, the one named last changes fastest.
Arguments:
- prior_hydrostatic_load: float32 [256, 256, 1024], P('azim', 'rad'), may hold values from -6 to 6
- predicted_outflow_per_step: float32 [256, 256, 1024], P('azim', 'rad'), may hold values from -6 to 6
- parcel_specific_mass_recip: float32 [256, 256, 1024], P('azim', 'rad'), may hold values from 1 to 10
- melt_heat_state: float32 [256, 256, 1024], P('azim', 'rad'), may hold values from -6 to 6
- passage_parcel_label: int32 [32, 4, 4, 1024], P('azim', 'rad'), may hold values from 0 to 523775
- passage_boundary_vertex: int32 [32, 4, 4, 1024], P('azim', 'rad'), may hold values from 0 to 2047
- passage_face_share: float32 [32, 4, 4, 1024], P('azim', 'rad'), may hold values from 0.1 to 1
- passage_live_tally: int32 [32, 4, 4], P('azim', 'rad'), may hold values from 1 to 1024, as said below
- boundary_elevation_prior: float32 [8192], P('rad'), may hold values from -3 to 3
- boundary_weight_restoring: float32 [8192], P('rad'), may hold values from 0.05 to 0.5
- boundary_load_discontinuity: float32 [8192], P('rad'), may hold values from -6 to 6
- tile_approx_solve: float32 [16, 16, 512], P(None, None, 'rad'), may hold values from -0.03 to 0.28, as said below
Outputs:
- pressure: float32 [256, 256, 1024], P('azim', 'rad')
- front_height: float32 [8192], P('rad')
The draws below stay inside these ranges and needn't reach their ends.
Inputs may be any that keep to these rules, and one draw needn't show every extreme that they name: `passage_live_tally`: in every draw one group j receives 1024 live slots from every radial slab of one azimuthal sector. `tile_approx_solve`: one given matrix for each block of 16 consecutive nodes.
All inputs are finite; a program needn't handle non-finite values.
Results may differ from the reference program's by a relative error of at most 0.0003.
Values sent between devices are 32-bit elements; how exact they have to be, the bound alone decides.
No kernel may reach another device: no remote copies, remote signals or barrier semaphores. Data moves between devices by JAX's collectives and lax.ppermute only.
A program may use at most 128 MiB of HBM per device.

```python
import math
import jax
import jax.numpy as jnp
from jax import lax

CT = 8
CR = 64
MELT_ZSLICES = 1024
SWEEPS = 4
NODES = 8192
BLK = 16
ITERS = 4
CAPX = 1024
MELT_WEDGES = 256
MELT_ANNULI = 256
NODE_RAD = 2048
NBLOCK = 512
N_AZIM = 32
N_RAD = 4


def draw_predicted_outflow_per_step(key, part):
    shape = (MELT_WEDGES, MELT_ANNULI, MELT_ZSLICES)
    return jnp.clip(jax.random.normal(jax.random.fold_in(key, 3), shape, jnp.float32), -6.0, 6.0)


def draw_passage_live_tally(key, part):
    base_key = jax.random.fold_in(key, 11)
    first_key, second_key, third_key = jax.random.split(base_key, 3)
    base = jax.random.randint(first_key, (N_AZIM, N_RAD, N_RAD), CAPX // 2, CAPX + 1)
    slab = jnp.arange(N_RAD, dtype=jnp.int32)[None, :, None]
    owner_group = jnp.arange(N_RAD, dtype=jnp.int32)[None, None, :]
    divisor = 1 + slab * (1 + jnp.abs(slab - owner_group))
    counts = jnp.maximum(base // divisor, 1)
    sector = jax.random.randint(second_key, (), 0, N_AZIM)
    group = jax.random.randint(third_key, (), 0, N_RAD)
    filled = (jnp.arange(N_AZIM, dtype=jnp.int32)[:, None, None] == sector) & (owner_group == group)
    return jnp.where(filled, CAPX, counts).astype(jnp.int32)


def draw_tile_approx_solve(key, part):
    base_key = jax.random.fold_in(key, 17)
    first_key, second_key = jax.random.split(base_key, 2)
    diagonal = jax.random.uniform(first_key, (BLK, 1, NBLOCK), jnp.float32, 0.16, 0.28)
    spread = jnp.clip(0.008 * jax.random.normal(second_key, (BLK, BLK, NBLOCK), jnp.float32), -0.03, 0.03)
    places = jnp.arange(BLK, dtype=jnp.int32)
    on_diagonal = (places[:, None] == places[None, :])[:, :, None]
    return jnp.where(on_diagonal, diagonal, spread)


def with_ends(values, rng, low, top_value):
    index_at = [jax.random.randint(jax.random.fold_in(rng, axis), (), 0, length) for axis, length in enumerate(values.shape)]
    main_axis = values.shape.index(max(values.shape))
    beside = index_at[:main_axis] + [(index_at[main_axis] + 1) % values.shape[main_axis]] + index_at[main_axis + 1:]
    return values.at[tuple(index_at)].set(low).at[tuple(beside)].set(top_value)


def shard_levels(stream_key, extent, cuts, smallest, high):
    level, own = 1.0, jax.random.fold_in(stream_key, 6)
    for axis_at, blocks in cuts:
        steps = jnp.exp(jax.random.uniform(jax.random.fold_in(own, axis_at), (blocks,), jnp.float32, smallest / len(cuts), high / len(cuts)))
        level = level * jnp.repeat(steps, extent[axis_at] // blocks).reshape([-1 if axis == axis_at else 1 for axis in range(len(extent))])
    return level


def centred(rng, dims, deviation, most, cuts=(), kind=jnp.bfloat16):
    level = shard_levels(rng, dims, cuts, -0.22, 0.18) if cuts else 1.0
    entries = jax.random.normal(rng, dims, jnp.float32) * deviation * level
    return jnp.minimum(jnp.maximum(entries, -most), most).astype(kind)


def setup_inputs(seed: int = 0) -> dict:
    splits = jax.random.split(jax.random.key(seed), 13)
    prior_hydrostatic_load = centred(splits[0], (MELT_WEDGES, MELT_ANNULI, MELT_ZSLICES), 1.0, 6.0, ((0, 32), (1, 4)), jnp.float32)
    predicted_outflow_per_step = draw_predicted_outflow_per_step(jax.random.fold_in(splits[12], 71), 0)
    parcel_specific_mass_recip = jnp.clip(jnp.exp(math.log(10.0) - 2.3025851 * jax.random.uniform(splits[2], (MELT_WEDGES, MELT_ANNULI, MELT_ZSLICES), jnp.float32) ** shard_levels(splits[2], (MELT_WEDGES, MELT_ANNULI, MELT_ZSLICES), ((0, 32), (1, 4)), -0.2, 0.2)), 1.0, 10.0)
    melt_heat_state = centred(splits[3], (MELT_WEDGES, MELT_ANNULI, MELT_ZSLICES), 1.0, 6.0, ((0, 32), (1, 4)), jnp.float32)
    passage_parcel_label = with_ends(jax.random.randint(splits[4], (N_AZIM, N_RAD, N_RAD, CAPX), 0, CT * CR * (MELT_ZSLICES - 1)), jax.random.fold_in(splits[4], 1), 0, (CT * CR * (MELT_ZSLICES - 1)) - 1).astype(jnp.int32)
    passage_boundary_vertex = with_ends(jax.random.randint(splits[5], (N_AZIM, N_RAD, N_RAD, CAPX), 0, NODE_RAD), jax.random.fold_in(splits[5], 1), 0, NODE_RAD - 1).astype(jnp.int32)
    passage_face_share = jnp.clip(jnp.exp(math.log(1.0) - 2.3025851 * jax.random.uniform(splits[6], (N_AZIM, N_RAD, N_RAD, CAPX), jnp.float32) ** shard_levels(splits[6], (N_AZIM, N_RAD, N_RAD, CAPX), ((0, 32), (1, 4)), -0.2, 0.2)), 0.1, 1.0)
    passage_live_tally = draw_passage_live_tally(jax.random.fold_in(splits[12], 71), 0)
    boundary_elevation_prior = centred(splits[8], (NODES,), 0.5, 3.0, ((0, 4),), jnp.float32)
    boundary_weight_restoring = jnp.clip(jnp.exp(math.log(0.5) - 2.3025851 * jax.random.uniform(splits[9], (NODES,), jnp.float32) ** shard_levels(splits[9], (NODES,), ((0, 4),), -0.2, 0.2)), 0.05, 0.5)
    boundary_load_discontinuity = centred(splits[10], (NODES,), 1.0, 6.0, ((0, 4),), jnp.float32)
    tile_approx_solve = draw_tile_approx_solve(jax.random.fold_in(splits[12], 71), 0)
    return {"prior_hydrostatic_load": prior_hydrostatic_load, "predicted_outflow_per_step": predicted_outflow_per_step, "parcel_specific_mass_recip": parcel_specific_mass_recip, "melt_heat_state": melt_heat_state, "passage_parcel_label": passage_parcel_label, "passage_boundary_vertex": passage_boundary_vertex, "passage_face_share": passage_face_share, "passage_live_tally": passage_live_tally, "boundary_elevation_prior": boundary_elevation_prior, "boundary_weight_restoring": boundary_weight_restoring, "boundary_load_discontinuity": boundary_load_discontinuity, "tile_approx_solve": tile_approx_solve}


OMEGA = 0.9
AXIAL = 0.25
STEFAN = 1.0
SHRINK = 0.3
COUPLE = 0.2

def slab_terms(beta_slab):
    center = beta_slab[1:-1]
    theta_up = 0.5 * (center + beta_slab[2:])
    theta_down = 0.5 * (center + beta_slab[:-2])
    radial_rows = jnp.arange(MELT_ANNULI, dtype=jnp.int32)
    outer_open = (radial_rows != MELT_ANNULI - 1)[None, :, None]
    inner_open = (radial_rows != 0)[None, :, None]
    radial_out = jnp.where(outer_open, 0.5 * (center + jnp.roll(center, -1, axis=1)), 0.0)
    radial_in = jnp.where(inner_open, 0.5 * (center + jnp.roll(center, 1, axis=1)), 0.0)
    above = jnp.concatenate([center[:, :, 1:], center[:, :, -1:]], axis=2)
    below = jnp.concatenate([center[:, :, :1], center[:, :, :-1]], axis=2)
    axial_up = 0.5 * (center + above)
    bottom_open = (jnp.arange(MELT_ZSLICES, dtype=jnp.int32) != 0)[None, None, :]
    axial_down = jnp.where(bottom_open, 0.5 * (center + below), 0.0)
    radius = 0.25 * MELT_ANNULI + radial_rows.astype(jnp.float32) + 0.5
    angular = ((MELT_WEDGES / (2.0 * math.pi)) ** 2 / (radius * radius))[None, :, None]
    a_tp = theta_up * angular
    a_tm = theta_down * angular
    a_rp = radial_out * ((radius + 0.5) / radius)[None, :, None]
    a_rm = radial_in * ((radius - 0.5) / radius)[None, :, None]
    a_zp = AXIAL * axial_up
    a_zm = AXIAL * axial_down
    diagonal = a_tp + a_tm + a_rp + a_rm + a_zp + a_zm
    return (a_tp, a_tm, a_rp, a_rm, a_zp, a_zm, diagonal)

def relax(pressure, parcel_specific_mass_recip, source):
    p_wrap = jnp.concatenate([pressure[-1:], pressure, pressure[:1]], axis=0)
    b_wrap = jnp.concatenate([parcel_specific_mass_recip[-1:], parcel_specific_mass_recip, parcel_specific_mass_recip[:1]], axis=0)

    def one_sector(sector):
        start = (sector * CT).astype(jnp.int32)
        p_slab = lax.dynamic_slice_in_dim(p_wrap, start, CT + 2, 0)
        b_slab = lax.dynamic_slice_in_dim(b_wrap, start, CT + 2, 0)
        s_slab = lax.dynamic_slice_in_dim(source, start, CT, 0)
        a_tp, a_tm, a_rp, a_rm, a_zp, a_zm, diagonal = slab_terms(b_slab)
        center = p_slab[1:-1]
        zeros = jnp.zeros_like(center[:, :, :1])
        upper = jnp.concatenate([center[:, :, 1:], zeros], axis=2)
        lower = jnp.concatenate([zeros, center[:, :, :-1]], axis=2)
        beside = a_tp * p_slab[2:] + a_tm * p_slab[:-2] + a_rp * jnp.roll(center, -1, axis=1) + a_rm * jnp.roll(center, 1, axis=1) + a_zp * upper + a_zm * lower
        return (1.0 - OMEGA) * center + OMEGA * (beside - s_slab) / diagonal
    result = lax.map(one_sector, jnp.arange(N_AZIM, dtype=jnp.int32))
    return result.reshape(MELT_WEDGES, MELT_ANNULI, MELT_ZSLICES)

def reference(prior_hydrostatic_load, predicted_outflow_per_step, parcel_specific_mass_recip, melt_heat_state, passage_parcel_label, passage_boundary_vertex, passage_face_share, passage_live_tally, boundary_elevation_prior, boundary_weight_restoring, boundary_load_discontinuity, tile_approx_solve):
    column = passage_parcel_label // (MELT_ZSLICES - 1)
    axial_pos = passage_parcel_label % (MELT_ZSLICES - 1)
    sector = jnp.arange(N_AZIM, dtype=jnp.int32)[:, None, None, None]
    slab = jnp.arange(N_RAD, dtype=jnp.int32)[None, :, None, None]
    theta_index = sector * CT + column // CR
    radial_index = slab * CR + column % CR
    unrolled_location = ((theta_index * MELT_ANNULI + radial_index) * MELT_ZSLICES + axial_pos).astype(jnp.int32)
    heat_state_parcels = melt_heat_state.reshape(-1)
    heat_state_discontinuity = heat_state_parcels[unrolled_location + 1] - heat_state_parcels[unrolled_location]
    live_slots = jnp.arange(CAPX, dtype=jnp.int32)[None, None, None, :] < passage_live_tally[..., None]
    contribution = jnp.where(live_slots, passage_face_share * heat_state_discontinuity, 0.0)
    owner_group = jnp.arange(N_RAD, dtype=jnp.int32)[None, None, :, None]
    target = (owner_group * NODE_RAD + passage_boundary_vertex).astype(jnp.int32)
    node_flux = jax.ops.segment_sum(contribution.reshape(-1), target.reshape(-1), num_segments=NODES)
    front_force = boundary_load_discontinuity + COUPLE * node_flux
    height = boundary_elevation_prior
    for repeat in range(ITERS):
        padded = jnp.pad(height, 1)
        applied = (2.0 + boundary_weight_restoring) * height - padded[:-2] - padded[2:]
        residual = front_force - applied
        blocks = residual.reshape(NBLOCK, BLK).T
        update = jnp.einsum('ijb,jb->ib', tile_approx_solve, blocks, precision=lax.Precision.HIGHEST)
        height = height + update.T.reshape(NODES)
    padded = jnp.pad(height, 1)
    growth = height - boundary_elevation_prior
    front_slope = padded[2:] - padded[:-2]
    area_factor = jnp.sqrt(1.0 + front_slope[target] * front_slope[target])
    cell_term = jnp.where(live_slots, passage_face_share * (node_flux[target] - STEFAN * growth[target]) * area_factor, 0.0)
    front_source = jax.ops.segment_sum(cell_term.reshape(-1), unrolled_location.reshape(-1), num_segments=MELT_WEDGES * MELT_ANNULI * MELT_ZSLICES).reshape(MELT_WEDGES, MELT_ANNULI, MELT_ZSLICES)
    source = predicted_outflow_per_step + SHRINK * front_source
    pressure = prior_hydrostatic_load
    for repeat in range(SWEEPS):
        pressure = relax(pressure, parcel_specific_mass_recip, source)
    return (pressure, height)
```

```python
import functools
import math

import jax
import jax.numpy as jnp
from jax import lax
from jax.experimental import pallas as pl
from jax.experimental.pallas import tpu as pltpu
from jax.sharding import PartitionSpec as P

SWEEPS = 4
ITERS = 4
OMEGA = 0.9
AXIAL = 0.25
STEFAN = 1.0
SHRINK = 0.3
COUPLE = 0.2

F32 = jnp.float32
I32 = jnp.int32
BF16 = jnp.bfloat16

T, R, Z = 8, 64, 1024
H = 4
TE = T + 2 * H
RE = R + 16
RT = RE // 8
GROUPS, SLOTS, NB, BS = 4, 1024, 128, 16
UNROLL = 16


def iota(shape, dim):
    return lax.broadcasted_iota(I32, shape, dim)


def pieces(x):
    h = x.astype(BF16)
    rest = x - h.astype(F32)
    m = rest.astype(BF16)
    return h, m, (rest - m.astype(F32)).astype(BF16)


def at8(i):
    return pl.ds(pl.multiple_of(i * 8, 8), 8)


def flux_kernel(cnt, row, heat, lane, vert, share, out, diff, picked):
    def make(q, _):
        x = heat[q // 8, at8(q % 8), :]
        d = pltpu.roll(x, Z - 1, 1) - x
        for zc in range(8):
            diff[at8(q * 8 + zc), :] = d[:, zc * 128:(zc + 1) * 128]
        return 0

    lax.fori_loop(0, T * R // 8, make, 0, unroll=2)
    for j in range(GROUPS):
        def body(b, _):
            base = pl.multiple_of(b * UNROLL, UNROLL)
            for u in range(UNROLL):
                picked[pl.ds(base + u, 1), :] = diff[pl.ds(row[j, base + u], 1), :]
            return 0

        lax.fori_loop(0, (cnt[j] + UNROLL - 1) // UNROLL, body, 0)
        vals = []
        for kb in range(SLOTS // 128):
            cut = slice(kb * 128, (kb + 1) * 128)
            hit = iota((128, 128), 0) == lane[j:j + 1, cut]
            vals.append(jnp.sum(jnp.where(hit, picked[cut, :].T, 0.0), axis=0, keepdims=True))
        live = iota((1, SLOTS), 1) < cnt[j]
        val = jnp.where(live, share[j:j + 1, :] * jnp.concatenate(vals, axis=1), 0.0)
        v = vert[j:j + 1, :]
        inner = iota((BS, SLOTS), 0) == (v & (BS - 1))
        left = jnp.concatenate(
            [jnp.where(inner, p.astype(F32), 0.0).astype(BF16) for p in pieces(val)], axis=0)
        right = jnp.where(iota((NB, SLOTS), 0) == (v >> 4), 1.0, 0.0).astype(BF16)
        o = lax.dot_general(left, right, (((1,), (1,)), ((), ())), preferred_element_type=F32)
        out[j * BS:(j + 1) * BS, :] = o[:BS] + o[BS:2 * BS] + o[2 * BS:]


def front_kernel(kref, cnt, row, flux, f0, f1, f2, f3, lane, vert, share, pred,
                 src, hout, front, gtab, height, terms, *acc):
    k = kref[0]

    def zero(q, _):
        for a in acc:
            a[at8(q), :] = jnp.zeros((8, 128), F32)
        return 0

    lax.fori_loop(0, T * R, zero, 0, unroll=4)
    for s, f in enumerate((f0, f1, f2, f3)):
        front[lax.rem(k + GROUPS - s, GROUPS)] = f[...]

    def neighbours(h):
        last = jnp.concatenate([h[g][BS - 1:BS, :] for g in range(GROUPS)], axis=0)
        first = jnp.concatenate([h[g][0:1, :] for g in range(GROUPS)], axis=0)
        zrow = jnp.zeros((1, 128), F32)
        lr = pltpu.roll(last, 1, 1)
        fr = pltpu.roll(first, 127, 1)
        col = iota((GROUPS, 128), 1)
        lr = jnp.where(col == 0, jnp.concatenate([zrow, lr[:-1]], axis=0), lr)
        fr = jnp.where(col == 127, jnp.concatenate([fr[1:], zrow], axis=0), fr)
        down = [jnp.concatenate([lr[g:g + 1], h[g][:BS - 1]], axis=0) for g in range(GROUPS)]
        up = [jnp.concatenate([h[g][1:], fr[g:g + 1]], axis=0) for g in range(GROUPS)]
        return down, up

    prior = [front[g, 256:272, :] for g in range(GROUPS)]
    h = list(prior)
    for _ in range(ITERS):
        down, up = neighbours(h)
        for g in range(GROUPS):
            applied = (2.0 + front[g, 272:288, :]) * h[g] - down[g] - up[g]
            res = front[g, 288:304, :] + COUPLE * flux[g * BS:(g + 1) * BS, :] - applied
            prod = front[g, 0:256, :].reshape(BS, BS, 128) * res[None]
            h[g] = h[g] + jnp.sum(prod, axis=1)
    down, up = neighbours(h)
    for g in range(GROUPS):
        slope = up[g] - down[g]
        growth = h[g] - prior[g]
        height[g] = h[g]
        gtab[g] = (flux[g * BS:(g + 1) * BS, :] - STEFAN * growth) * jnp.sqrt(1.0 + slope * slope)
    hout[...] = height[k]
    for j in range(GROUPS):
        v = vert[j:j + 1, :]
        right = jnp.where(iota((NB, SLOTS), 0) == (v >> 4), 1.0, 0.0).astype(BF16)
        x = jnp.dot(jnp.concatenate(pieces(gtab[j]), axis=0), right, preferred_element_type=F32)
        x = x[:BS] + x[BS:2 * BS] + x[2 * BS:]
        inner = iota((BS, SLOTS), 0) == (v & (BS - 1))
        term = jnp.sum(jnp.where(inner, x, 0.0), axis=0, keepdims=True) * share[j:j + 1, :]
        term = jnp.where(iota((1, SLOTS), 1) < cnt[j], term, 0.0)
        for kb in range(SLOTS // 128):
            cut = slice(kb * 128, (kb + 1) * 128)
            hit = iota((128, 128), 0) == lane[j:j + 1, cut]
            terms[j, cut, :] = jnp.where(hit, term[:, cut], 0.0).T
    most = jnp.maximum(jnp.maximum(cnt[0], cnt[1]), jnp.maximum(cnt[2], cnt[3]))

    def add(b, _):
        for u in range(UNROLL):
            s = b * UNROLL + u
            for j in range(GROUPS):
                at = pl.ds(row[j, s], 1)
                acc[j][at, :] = acc[j][at, :] + terms[j, pl.ds(s, 1), :]
        return 0

    lax.fori_loop(0, (most + UNROLL - 1) // UNROLL, add, 0)

    def finish(q, _):
        d = q // 8
        for zc in range(8):
            a = at8(q * 8 + zc)
            s = (acc[0][a, :] + acc[1][a, :]) + (acc[2][a, :] + acc[3][a, :])
            cut = slice(zc * 128, (zc + 1) * 128)
            src[d, at8(q % 8), cut] = pred[d, at8(q % 8), cut] + SHRINK * s
        return 0

    lax.fori_loop(0, T * R // 8, finish, 0)


def place(ref, own, lo, hi, rlo, rhi, c0, c1, c2, c3):
    mid, a, b = pl.ds(H, T), pl.ds(0, H), pl.ds(H + T, H)
    rm, r0, r1 = pl.ds(8, R), pl.ds(0, 8), pl.ds(8 + R, 8)
    return [(own, ref.at[mid, rm]), (lo, ref.at[a, rm]), (hi, ref.at[b, rm]),
            (rlo, ref.at[mid, r0]), (rhi, ref.at[mid, r1]),
            (c0, ref.at[a, r0]), (c1, ref.at[a, r1]), (c2, ref.at[b, r0]), (c3, ref.at[b, r1])]


def sweep_kernel(kref, *refs):
    fields, out = refs[:27], refs[27]
    pa, pb, th, rr, zz, ww, ss, sems = refs[28:]
    k = kref[0]
    copies = []
    for n, ref in enumerate((pb, pa, ss)):
        cs = [pltpu.make_async_copy(a, b, sems.at[n, m])
              for m, (a, b) in enumerate(place(ref, *fields[9 * n:9 * n + 9]))]
        for c in cs:
            c.start()
        copies.append(cs)
    for c in copies[0]:
        c.wait()
    sub = iota((8, Z), 0)
    lane = iota((8, Z), 1)
    beta = pb

    def gidx(it):
        return k * R + (it * 8 - 8) + sub

    def radius(it):
        return 0.25 * 256 + gidx(it).astype(F32) + 0.5

    angular = (256 / (2.0 * math.pi)) ** 2

    def theta(t, _):
        for it in range(RT):
            c = slice(it * 8, it * 8 + 8)
            th[t, c, :] = (beta[t, c, :] + beta[t + 1, c, :]) * ((0.5 * angular) / radius(it))
        return 0

    lax.fori_loop(0, TE - 1, theta, 0)

    def coef(t, _):
        prev = jnp.zeros((8, Z), F32)
        nxt = beta[t, 0:8, :]
        for it in range(RT):
            c = slice(it * 8, it * 8 + 8)
            b, ra, gi = nxt, radius(it), gidx(it)
            if it + 1 < RT:
                nxt = beta[t, it * 8 + 8:it * 8 + 16, :]
            bu = jnp.where(sub == 7, pltpu.roll(nxt, 7, 0), pltpu.roll(b, 7, 0))
            face = jnp.where((gi >= 0) & (gi < 255), (0.5 * (b + bu)) * (ra + 0.5), 0.0)
            rolled = pltpu.roll(face, 1, 0)
            below = jnp.where(sub == 0, prev, rolled)
            prev = rolled
            zu = jnp.where(lane == Z - 1, b, 0.5 * (b + pltpu.roll(b, Z - 1, 1))) * (AXIAL * ra)
            zcut = jnp.where(lane == Z - 1, 0.0, zu)
            d = th[t, c, :] + th[t - 1, c, :] + face + below + zu + pltpu.roll(zcut, 1, 1)
            ww[t, c, :] = jnp.where(d > 0.0, OMEGA / jnp.where(d > 0.0, d, 1.0), 0.0)
            rr[t, c, :] = face
            zz[t, c, :] = zcut
        return 0

    lax.fori_loop(1, TE - 1, coef, 0)
    for cs in copies[1:]:
        for c in cs:
            c.wait()

    def scale(t, _):
        for it in range(RT):
            c = slice(it * 8, it * 8 + 8)
            ss[t, c, :] = ss[t, c, :] * radius(it)
        return 0

    lax.fori_loop(1, TE - 1, scale, 0)

    def sweep(old, new, t, first, last, shift, rows):
        prev = jnp.zeros((8, Z), F32)
        if first > 0:
            c = slice(first * 8 - 8, first * 8)
            prev = pltpu.roll(rr[t, c, :] * old[t, c, :], 1, 0)
        nxt = old[t, first * 8:first * 8 + 8, :]
        nroll = pltpu.roll(nxt, 7, 0)
        for it in range(first, last):
            c = slice(it * 8, it * 8 + 8)
            p, proll = nxt, nroll
            if it + 1 < RT:
                nxt = old[t, it * 8 + 8:it * 8 + 16, :]
                nroll = pltpu.roll(nxt, 7, 0)
            r, z = rr[t, c, :], zz[t, c, :]
            acc = th[t, c, :] * old[t + 1, c, :] + th[t - 1, c, :] * old[t - 1, c, :]
            acc = acc + r * jnp.where(sub == 7, nroll, proll)
            rolled = pltpu.roll(r * p, 1, 0)
            acc = acc + jnp.where(sub == 0, prev, rolled)
            prev = rolled
            acc = acc + z * pltpu.roll(p, Z - 1, 1) + pltpu.roll(z * p, 1, 1)
            o = slice(it * 8 - rows, it * 8 - rows + 8)
            new[t - shift, o, :] = (1.0 - OMEGA) * p + ww[t, c, :] * (acc - ss[t, c, :])

    bufs = (pa, pb)
    for n in range(1, SWEEPS + 1):
        old, new = bufs[(n - 1) % 2], bufs[n % 2]
        if n < SWEEPS:
            lax.fori_loop(n, TE - n, lambda t, _: (sweep(old, new, t, 0, RT, 0, 0), 0)[1], 0)
        else:
            lax.fori_loop(n, TE - n, lambda t, _: (sweep(old, out, t, 1, RT - 1, H, 8), 0)[1], 0)


def shift_pairs(dt, dk):
    pairs = []
    for a in range(32):
        for k in range(4):
            if 0 <= k + dk < 4:
                pairs.append((a * 4 + k, ((a + dt) % 32) * 4 + k + dk))
    return pairs


def halos(x):
    both = ("azim", "rad")
    send = lambda y, dt, dk: lax.ppermute(y, both, shift_pairs(dt, dk))
    a, b = x[T - H:], x[:H]
    lo, hi = send(a, 1, 0), send(b, -1, 0)
    rlo, rhi = send(x[:, R - 8:], 0, 1), send(x[:, :8], 0, -1)
    c0, c1 = send(a[:, R - 8:], 1, 1), send(a[:, :8], 1, -1)
    c2, c3 = send(b[:, R - 8:], -1, 1), send(b[:, :8], -1, -1)
    return x, lo, hi, rlo, rhi, c0, c1, c2, c3


def at(y, z, c):
    return (y % 4 * 4 + z % 4) * 2 + c


def azim_pairs(dy, dz, flip):
    return [(at(y, z, c), at(y + dy, z + dz, c ^ flip))
            for y in range(4) for z in range(4) for c in range(2)]


def total(x):
    x = x + lax.ppermute(x, "azim", azim_pairs(0, 0, 1))
    x = x + sum(lax.ppermute(x, "azim", azim_pairs(0, s, 0)) for s in (1, 2, 3))
    x = x + sum(lax.ppermute(x, "azim", azim_pairs(s, 0, 0)) for s in (1, 2, 3))
    return x + sum(lax.ppermute(x, "rad", [(i, (i + s) % 4) for i in range(4)]) for s in (1, 2, 3))


VM = pl.BlockSpec(memory_space=pltpu.VMEM)
SM = pl.BlockSpec(memory_space=pltpu.SMEM)
ANY = pl.BlockSpec(memory_space=pl.ANY)
PARAMS = pltpu.CompilerParams(vmem_limit_bytes=56 << 20)


def per_device(load, outflow, beta, heat, label, vertex, share, tally, prior, weight, jump, solve):
    label = label.reshape(GROUPS, SLOTS)
    vertex = vertex.reshape(GROUPS, SLOTS)
    share = share.reshape(GROUPS, SLOTS)
    tally = tally.reshape(GROUPS)
    hi = label >> 10
    low = hi + (label & 1023)
    carry = (low >= Z - 1).astype(I32)
    column, axial = hi + carry, low - (Z - 1) * carry
    row = ((column >> 3) << 6) + ((axial >> 7) << 3) + (column & 7)
    lane = axial & 127
    kidx = lax.axis_index("rad").astype(I32).reshape(1)

    flip = lambda v: v.reshape(NB, BS).T
    front = jnp.concatenate([solve.reshape(BS * BS, NB), flip(prior), flip(weight), flip(jump)], axis=0)
    fronts = [front] + [
        lax.ppermute(front, "rad", [(i, (i + s) % 4) for i in range(4)]) for s in (1, 2, 3)]
    beta_parts = halos(beta)
    load_parts = halos(load)

    partial = pl.pallas_call(
        flux_kernel, out_shape=jax.ShapeDtypeStruct((GROUPS * BS, NB), F32),
        in_specs=[SM, SM, VM, VM, VM, VM], out_specs=VM,
        scratch_shapes=[pltpu.VMEM((T * R * 8, 128), F32), pltpu.VMEM((SLOTS, 128), F32)],
        compiler_params=PARAMS, name="flux",
        cost_estimate=pl.CostEstimate(flops=20000000, bytes_accessed=2 << 20, transcendentals=0),
    )(tally, row, heat, lane, vertex, share)
    flux = total(partial)
    source, height = pl.pallas_call(
        front_kernel,
        out_shape=(jax.ShapeDtypeStruct((T, R, Z), F32), jax.ShapeDtypeStruct((BS, NB), F32)),
        in_specs=[SM, SM, SM] + [VM] * 9, out_specs=(VM, VM),
        scratch_shapes=[pltpu.VMEM((GROUPS, 304, NB), F32), pltpu.VMEM((GROUPS, BS, NB), F32),
                        pltpu.VMEM((GROUPS, BS, NB), F32), pltpu.VMEM((GROUPS, SLOTS, 128), F32)]
        + [pltpu.VMEM((T * R * 8, 128), F32)] * GROUPS,
        compiler_params=PARAMS, name="front",
        cost_estimate=pl.CostEstimate(flops=20000000, bytes_accessed=4 << 20, transcendentals=0),
    )(kidx, tally, row, flux, *fronts, lane, vertex, share, outflow)
    source_parts = halos(source)
    ext = pltpu.VMEM((TE, RE, Z), F32)
    pressure = pl.pallas_call(
        sweep_kernel, out_shape=jax.ShapeDtypeStruct((T, R, Z), F32),
        in_specs=[SM] + [ANY] * 27, out_specs=VM,
        scratch_shapes=[ext] * 7 + [pltpu.SemaphoreType.DMA((3, 9))],
        compiler_params=PARAMS, name="sweeps",
        cost_estimate=pl.CostEstimate(flops=40000000, bytes_accessed=16 << 20, transcendentals=0),
    )(kidx, *beta_parts, *load_parts, *source_parts)
    return pressure, height.T.reshape(NB * BS)


def solution(mesh):
    cells = P("azim", "rad", None)
    slots = P("azim", "rad", None, None)
    return jax.shard_map(
        per_device,
        mesh=mesh,
        in_specs=(cells, cells, cells, cells, slots, slots, slots, cells,
                  P("rad"), P("rad"), P("rad"), P(None, None, "rad")),
        out_specs=(cells, P("rad")),
        check_vma=False,
    )
```

```python
import functools
import math

import jax
import jax.numpy as jnp
from jax import lax
from jax.experimental import pallas as pl
from jax.experimental.pallas import tpu as pltpu
from jax.sharding import PartitionSpec as P

SWEEPS = 4
ITERS = 4
OMEGA = 0.9
AXIAL = 0.25
STEFAN = 1.0
SHRINK = 0.3
COUPLE = 0.2

F32 = jnp.float32
I32 = jnp.int32
BF16 = jnp.bfloat16

T, R, Z = 8, 64, 1024
H = 4
TE = T + 2 * H
RE = R + 8
RT = RE // 8
GROUPS, SLOTS, NB, BS = 4, 1024, 128, 16
UNROLL = 16
AZIM = ("y", "z", "core")


def iota(shape, dim):
    return lax.broadcasted_iota(I32, shape, dim)


def pieces(x):
    h = x.astype(BF16)
    rest = x - h.astype(F32)
    m = rest.astype(BF16)
    return h, m, (rest - m.astype(F32)).astype(BF16)


def at8(i):
    return pl.ds(pl.multiple_of(i * 8, 8), 8)


def flux_kernel(cnt, row, heat, lane, vert, share, out, diff, picked):
    def make(q, _):
        x = heat[q // 8, at8(q % 8), :]
        d = pltpu.roll(x, Z - 1, 1) - x
        for zc in range(8):
            diff[at8(q * 8 + zc), :] = d[:, zc * 128:(zc + 1) * 128]
        return 0

    lax.fori_loop(0, T * R // 8, make, 0, unroll=4)
    for j in range(GROUPS):
        def body(b, _):
            base = pl.multiple_of(b * UNROLL, UNROLL)
            for u in range(UNROLL):
                picked[pl.ds(base + u, 1), :] = diff[pl.ds(row[j, base + u], 1), :]
            return 0

        lax.fori_loop(0, (cnt[j] + UNROLL - 1) // UNROLL, body, 0)
        vals = []
        for kb in range(SLOTS // 128):
            cut = slice(kb * 128, (kb + 1) * 128)
            hit = iota((128, 128), 0) == lane[j:j + 1, cut]
            vals.append(jnp.sum(jnp.where(hit, picked[cut, :].T, 0.0), axis=0, keepdims=True))
        live = iota((1, SLOTS), 1) < cnt[j]
        val = jnp.where(live, share[j:j + 1, :] * jnp.concatenate(vals, axis=1), 0.0)
        v = vert[j:j + 1, :]
        inner = iota((BS, SLOTS), 0) == (v & (BS - 1))
        left = jnp.concatenate(
            [jnp.where(inner, p.astype(F32), 0.0).astype(BF16) for p in pieces(val)], axis=0)
        right = jnp.where(iota((NB, SLOTS), 0) == (v >> 4), 1.0, 0.0).astype(BF16)
        o = lax.dot_general(left, right, (((1,), (1,)), ((), ())), preferred_element_type=F32)
        out[j * BS:(j + 1) * BS, :] = o[:BS] + o[BS:2 * BS] + o[2 * BS:]


def front_kernel(kref, cnt, row, flux, f0, f1, f2, f3, lane, vert, share, pred, *refs):
    front_body(kref, cnt, row, flux, f0, f1, f2, f3, lane, vert, share, pred, *refs[5:])


def front_body(kref, cnt, row, parts, f0, f1, f2, f3, lane, vert, share, pred,
                 src, sup, sdown, srup, srdown, hout, front, gtab, height, terms, total, *acc):
    k = kref[0]
    sums = parts[0]
    for n in range(1, parts.shape[0]):
        sums = sums + parts[n]
    total[...] = sums
    flux = total

    def zero(q, _):
        for a in acc:
            a[at8(q), :] = jnp.zeros((8, 128), F32)
        return 0

    lax.fori_loop(0, T * R, zero, 0, unroll=4)
    for s, f in enumerate((f0, f1, f2, f3)):
        front[lax.rem(k + GROUPS - s, GROUPS)] = f[...]

    def neighbours(h):
        last = jnp.concatenate([h[g][BS - 1:BS, :] for g in range(GROUPS)], axis=0)
        first = jnp.concatenate([h[g][0:1, :] for g in range(GROUPS)], axis=0)
        zrow = jnp.zeros((1, 128), F32)
        lr = pltpu.roll(last, 1, 1)
        fr = pltpu.roll(first, 127, 1)
        col = iota((GROUPS, 128), 1)
        lr = jnp.where(col == 0, jnp.concatenate([zrow, lr[:-1]], axis=0), lr)
        fr = jnp.where(col == 127, jnp.concatenate([fr[1:], zrow], axis=0), fr)
        down = [jnp.concatenate([lr[g:g + 1], h[g][:BS - 1]], axis=0) for g in range(GROUPS)]
        up = [jnp.concatenate([h[g][1:], fr[g:g + 1]], axis=0) for g in range(GROUPS)]
        return down, up

    prior = [front[g, 256:272, :] for g in range(GROUPS)]
    h = list(prior)
    for _ in range(ITERS):
        down, up = neighbours(h)
        for g in range(GROUPS):
            applied = (2.0 + front[g, 272:288, :]) * h[g] - down[g] - up[g]
            res = front[g, 288:304, :] + COUPLE * flux[g * BS:(g + 1) * BS, :] - applied
            prod = front[g, 0:256, :].reshape(BS, BS, 128) * res[None]
            h[g] = h[g] + jnp.sum(prod, axis=1)
    down, up = neighbours(h)
    for g in range(GROUPS):
        slope = up[g] - down[g]
        growth = h[g] - prior[g]
        height[g] = h[g]
        gtab[g] = (flux[g * BS:(g + 1) * BS, :] - STEFAN * growth) * jnp.sqrt(1.0 + slope * slope)
    hout[...] = height[k]
    for j in range(GROUPS):
        v = vert[j:j + 1, :]
        right = jnp.where(iota((NB, SLOTS), 0) == (v >> 4), 1.0, 0.0).astype(BF16)
        x = jnp.dot(jnp.concatenate(pieces(gtab[j]), axis=0), right, preferred_element_type=F32)
        x = x[:BS] + x[BS:2 * BS] + x[2 * BS:]
        inner = iota((BS, SLOTS), 0) == (v & (BS - 1))
        term = jnp.sum(jnp.where(inner, x, 0.0), axis=0, keepdims=True) * share[j:j + 1, :]
        term = jnp.where(iota((1, SLOTS), 1) < cnt[j], term, 0.0)
        for kb in range(SLOTS // 128):
            cut = slice(kb * 128, (kb + 1) * 128)
            hit = iota((128, 128), 0) == lane[j:j + 1, cut]
            terms[j, cut, :] = jnp.where(hit, term[:, cut], 0.0).T
    most = jnp.maximum(jnp.maximum(cnt[0], cnt[1]), jnp.maximum(cnt[2], cnt[3]))

    def add(b, _):
        for u in range(UNROLL):
            s = b * UNROLL + u
            for j in range(GROUPS):
                at = pl.ds(row[j, s], 1)
                acc[j][at, :] = acc[j][at, :] + terms[j, pl.ds(s, 1), :]
        return 0

    lax.fori_loop(0, (most + UNROLL - 1) // UNROLL, add, 0)

    def finish(q, _):
        d = q // 8
        for zc in range(8):
            a = at8(q * 8 + zc)
            s = (acc[0][a, :] + acc[1][a, :]) + (acc[2][a, :] + acc[3][a, :])
            cut = slice(zc * 128, (zc + 1) * 128)
            src[d, at8(q % 8), cut] = pred[d, at8(q % 8), cut] + SHRINK * s
        return 0

    lax.fori_loop(0, T * R // 8, finish, 0)
    sup[...] = src[T - H + 1:]
    sdown[...] = src[:H - 1]
    srup[...] = src[:, R - 8:, :]
    srdown[...] = src[:, :8, :]


def pack_kernel(load, beta, up, down, rup, rdown, sems):
    copies = []
    for n, f in enumerate((load, beta)):
        copies += [(f.at[pl.ds(T - H, H)], up.at[pl.ds(n * H, H)]),
                   (f.at[pl.ds(0, H)], down.at[pl.ds(n * H, H)]),
                   (f.at[:, pl.ds(R - 8, 8)], rup.at[pl.ds(n * T, T)]),
                   (f.at[:, pl.ds(0, 8)], rdown.at[pl.ds(n * T, T)])]
    copies = [pltpu.make_async_copy(a, b, sems.at[m]) for m, (a, b) in enumerate(copies)]
    for c in copies:
        c.start()
    for c in copies:
        c.wait()


def shift_azim(x, d):
    return lax.ppermute(x, AZIM, [(i, (i + d) % 32) for i in range(32)])


def shift_rad(x, d):
    return lax.ppermute(x, "rad", [(i, i + d) for i in range(4) if 0 <= i + d < 4])


def ring_tile(from_above, from_below):
    return jnp.where(iota(from_above.shape, 1) < 4, from_above, from_below)


def wide(x):
    return jnp.concatenate([x] * (Z // 128), axis=1)


def sweep_kernel(kref, load, beta_in, lo, hi, side, clo, chi, src, slo, shi, sside, sclo, schi,
                 out, pa, pb, th, rr, zz, ww, ss, sems):
    k = kref[0]
    mid, below, above = pl.ds(H, T), pl.ds(0, H), pl.ds(H + T, H)
    below3, above3 = pl.ds(1, H - 1), pl.ds(H + T, H - 1)
    rows, ring = pl.ds(0, R), pl.ds(R, 8)

    def part(x, n, count):
        return x.at[pl.ds(n * count, count)]

    def field(ref, own, n):
        return [(own, ref.at[mid, rows]), (part(lo, n, H), ref.at[below, rows]),
                (part(hi, n, H), ref.at[above, rows]), (part(side, n, T), ref.at[mid, ring]),
                (part(clo, n, H), ref.at[below, ring]), (part(chi, n, H), ref.at[above, ring])]

    groups = [field(pb, beta_in, 1), field(pa, load, 0),
              [(src, ss.at[mid, rows]), (slo, ss.at[below3, rows]), (shi, ss.at[above3, rows]),
               (sside, ss.at[mid, ring]), (sclo, ss.at[below3, ring]), (schi, ss.at[above3, ring])]]
    copies = []
    for n, g in enumerate(groups):
        cs = [pltpu.make_async_copy(a, b, sems.at[n, m]) for m, (a, b) in enumerate(g)]
        for c in cs:
            c.start()
        copies.append(cs)
    for c in copies[0]:
        c.wait()
    sub = iota((8, Z), 0)
    top, bottom = sub == 7, sub == 0
    last_lane = iota((8, Z), 1) == Z - 1
    s8 = iota((8, 128), 0)
    beta = pb

    def gidx(it):
        return k * R + (it * 8 + s8 if it < RT - 1 else jnp.where(s8 < 4, R + s8, s8 - 8))

    def radius(it):
        return 0.25 * 256 + gidx(it).astype(F32) + 0.5

    angular = (256 / (2.0 * math.pi)) ** 2

    def cut(it):
        it = it % RT
        return slice(it * 8, it * 8 + 8)

    def coefs(it, _):
        ra, gi = radius(it), gidx(it)
        return wide((0.5 * angular) / ra), wide(jnp.where((gi >= 0) & (gi < 255), 0.5 * (ra + 0.5), 0.0)), wide(AXIAL * ra)

    for it in range(RT):
        c = cut(it)
        ang, rad, axi = coefs(it, 0)
        th[0, c, :] = (beta[0, c, :] + beta[1, c, :]) * ang

        def coef(t, _):
            b = beta[t, c, :]
            bu = jnp.where(top, pltpu.roll(beta[t, cut(it + 1), :], 7, 0), pltpu.roll(b, 7, 0))
            rr[t, c, :] = (b + bu) * rad
            th[t, c, :] = (b + beta[t + 1, c, :]) * ang
            zz[t, c, :] = jnp.where(last_lane, b, 0.5 * (b + pltpu.roll(b, Z - 1, 1))) * axi
            return 0

        lax.fori_loop(1, TE - 1, coef, 0)

    def diag(t, _):
        for it in range(RT):
            c = cut(it)
            face, z = rr[t, c, :], zz[t, c, :]
            other = jnp.where(bottom, pltpu.roll(rr[t, cut(it - 1), :], 1, 0), pltpu.roll(face, 1, 0))
            zcut = jnp.where(last_lane, 0.0, z)
            zz[t, c, :] = zcut
            d = (th[t, c, :] + th[t - 1, c, :]) + (face + other) + (z + pltpu.roll(zcut, 1, 1))
            ww[t, c, :] = OMEGA / jnp.where(d > 0.0, d, 1.0)
        return 0

    lax.fori_loop(1, TE - 1, diag, 0)
    for cs in copies[1:]:
        for c in cs:
            c.wait()
    for it in range(RT):
        c = cut(it)
        ra = wide(radius(it))

        def scale(t, _):
            ss[t, c, :] = ss[t, c, :] * ra
            return 0

        lax.fori_loop(1, TE - 1, scale, 0, unroll=2)

    def sweep(old, new, t, tiles, shift):
        prev = pltpu.roll(rr[t, cut(-1), :] * old[t, cut(-1), :], 1, 0)
        nxt = old[t, cut(0), :]
        nroll = pltpu.roll(nxt, 7, 0)
        for it in range(tiles):
            c = cut(it)
            p, proll = nxt, nroll
            nxt = old[t, cut(it + 1), :]
            nroll = pltpu.roll(nxt, 7, 0)
            r, z = rr[t, c, :], zz[t, c, :]
            acc = th[t, c, :] * old[t + 1, c, :] + th[t - 1, c, :] * old[t - 1, c, :]
            acc = acc + r * jnp.where(top, nroll, proll)
            rolled = pltpu.roll(r * p, 1, 0)
            acc = acc + jnp.where(bottom, prev, rolled)
            prev = rolled
            acc = acc + z * pltpu.roll(p, Z - 1, 1) + pltpu.roll(z * p, 1, 1)
            new[t - shift, c, :] = (1.0 - OMEGA) * p + ww[t, c, :] * (acc - ss[t, c, :])
        return 0

    bufs = (pa, pb)
    for n in range(1, SWEEPS + 1):
        old, new = bufs[(n - 1) % 2], bufs[n % 2]
        if n < SWEEPS:
            lax.fori_loop(n, TE - n, lambda t, _: sweep(old, new, t, RT, 0), 0)
        else:
            lax.fori_loop(n, TE - n, lambda t, _: sweep(old, out, t, RT - 1, H), 0)


def from_all(x, axes, count):
    return lax.all_to_all(jnp.broadcast_to(x[None], (count,) + x.shape), axes, 0, 0)


def sum_kernel(parts, *refs):
    out = refs[-1]
    s = parts[0]
    for n in range(1, parts.shape[0]):
        s = s + parts[n]
    out[...] = s


VM = pl.BlockSpec(memory_space=pltpu.VMEM)
SM = pl.BlockSpec(memory_space=pltpu.SMEM)
ANY = pl.BlockSpec(memory_space=pl.ANY)
PARAMS = pltpu.CompilerParams(vmem_limit_bytes=56 << 20)


def per_device(load, outflow, beta, heat, label, vertex, share, tally, prior, weight, jump, solve):
    label = label.reshape(GROUPS, SLOTS)
    vertex = vertex.reshape(GROUPS, SLOTS)
    share = share.reshape(GROUPS, SLOTS)
    tally = tally.reshape(GROUPS)
    hi = label >> 10
    low = hi + (label & 1023)
    carry = (low >= Z - 1).astype(I32)
    column, axial = hi + carry, low - (Z - 1) * carry
    row = ((column >> 3) << 6) + ((axial >> 7) << 3) + (column & 7)
    lane = axial & 127
    kidx = lax.axis_index("rad").astype(I32).reshape(1)

    flip = lambda v: v.reshape(NB, BS).T
    front = jnp.concatenate([solve.reshape(BS * BS, NB), flip(prior), flip(weight), flip(jump)], axis=0)
    fronts = [front] + [
        lax.ppermute(front, "rad", [(i, (i + s) % 4) for i in range(4)]) for s in (1, 2, 3)]

    plane = lambda n: jax.ShapeDtypeStruct((n, R, Z), F32)
    tile = lambda n: jax.ShapeDtypeStruct((n, 8, Z), F32)
    up, down, rup, rdown = pl.pallas_call(
        pack_kernel, out_shape=(plane(2 * H), plane(2 * H), tile(2 * T), tile(2 * T)),
        in_specs=[ANY] * 2, out_specs=(ANY,) * 4,
        scratch_shapes=[pltpu.SemaphoreType.DMA((8,))], compiler_params=PARAMS, name="pack",
    )(load, beta)
    up, down, rup, rdown, heat = lax.optimization_barrier((up, down, rup, rdown, heat))
    lo, hi = shift_azim(up, 1), shift_azim(down, -1)
    rhi, rlo = shift_rad(rdown, -1), shift_rad(rup, 1)
    side = ring_tile(rhi, rlo)
    edge = lambda s: jnp.concatenate([side[s:s + H], side[T + s:T + s + H]], axis=0)
    clo, chi = shift_azim(edge(T - H), 1), shift_azim(edge(0), -1)
    partial = pl.pallas_call(
        flux_kernel, out_shape=jax.ShapeDtypeStruct((GROUPS * BS, NB), F32),
        in_specs=[SM, SM, VM, VM, VM, VM], out_specs=VM,
        scratch_shapes=[pltpu.VMEM((T * R * 8, 128), F32), pltpu.VMEM((SLOTS, 128), F32)],
        compiler_params=PARAMS, name="flux",
        cost_estimate=pl.CostEstimate(flops=20000000, bytes_accessed=120 << 20, transcendentals=0),
    )(tally, row, heat, lane, vertex, share)
    near = pl.pallas_call(
        sum_kernel, out_shape=jax.ShapeDtypeStruct((GROUPS * BS, NB), F32),
        in_specs=[VM, ANY, ANY], out_specs=VM, compiler_params=PARAMS, name="near",
    )(from_all(partial, ("z", "core"), 8), rhi, rlo)
    flux = from_all(near, ("y", "rad"), 16)
    source, sup, sdown, srup, srdown, height = pl.pallas_call(
        front_kernel,
        out_shape=(plane(T), plane(H - 1), plane(H - 1), tile(T), tile(T),
                   jax.ShapeDtypeStruct((BS, NB), F32)),
        in_specs=[SM, SM, SM] + [VM] * 9 + [ANY] * 5, out_specs=(VM,) * 6,
        scratch_shapes=[pltpu.VMEM((GROUPS, 304, NB), F32), pltpu.VMEM((GROUPS, BS, NB), F32),
                        pltpu.VMEM((GROUPS, BS, NB), F32), pltpu.VMEM((GROUPS, SLOTS, 128), F32),
                        pltpu.VMEM((GROUPS * BS, NB), F32)]
        + [pltpu.VMEM((T * R * 8, 128), F32)] * GROUPS,
        compiler_params=PARAMS, name="front",
        cost_estimate=pl.CostEstimate(flops=1000, bytes_accessed=30 << 20, transcendentals=0),
    )(kidx, tally, row, flux, *fronts, lane, vertex, share, outflow, lo, hi, side, clo, chi)
    slo, shi = shift_azim(sup, 1), shift_azim(sdown, -1)
    sside = ring_tile(shift_rad(srdown, -1), shift_rad(srup, 1))
    sclo, schi = shift_azim(sside[T - H + 1:], 1), shift_azim(sside[:H - 1], -1)
    ext = pltpu.VMEM((TE, RE, Z), F32)
    pressure = pl.pallas_call(
        sweep_kernel, out_shape=plane(T),
        in_specs=[SM] + [ANY] * 13, out_specs=VM,
        scratch_shapes=[ext] * 7 + [pltpu.SemaphoreType.DMA((3, 6))],
        compiler_params=PARAMS, name="sweeps",
        cost_estimate=pl.CostEstimate(flops=1000, bytes_accessed=30 << 20, transcendentals=0),
    )(kidx, load, beta, lo, hi, side, clo, chi, source, slo, shi, sside, sclo, schi)
    return pressure, height.T.reshape(NB * BS)


def solution(mesh):
    fine = jax.sharding.Mesh(mesh.devices.reshape(4, 4, 2, 4), AZIM + ("rad",))
    cells = P(AZIM, "rad", None)
    slots = P(AZIM, "rad", None, None)
    return jax.shard_map(
        per_device,
        mesh=fine,
        in_specs=(cells, cells, cells, cells, slots, slots, slots, cells,
                  P("rad"), P("rad"), P("rad"), P(None, None, "rad")),
        out_specs=(cells, P("rad")),
        check_vma=False,
    )
```

```python
import functools
import math

import jax
import jax.numpy as jnp
from jax import lax
from jax.experimental import pallas as pl
from jax.experimental.pallas import tpu as pltpu
from jax.sharding import PartitionSpec as P

SWEEPS = 4
ITERS = 4
OMEGA = 0.9
AXIAL = 0.25
STEFAN = 1.0
SHRINK = 0.3
COUPLE = 0.2

F32 = jnp.float32
I32 = jnp.int32
BF16 = jnp.bfloat16

T, R, Z = 8, 64, 1024
H = 4
TE = T + 2 * H
RE = R + 8
RT = RE // 8
GROUPS, SLOTS, NB, BS = 4, 1024, 128, 16
FT = 5
UNROLL = 16
AZIM = ("y", "z", "core")


def iota(shape, dim):
    return lax.broadcasted_iota(I32, shape, dim)


def pieces(x):
    h = x.astype(BF16)
    rest = x - h.astype(F32)
    m = rest.astype(BF16)
    return h, m, (rest - m.astype(F32)).astype(BF16)


def at8(i):
    return pl.ds(pl.multiple_of(i * 8, 8), 8)


def flux_kernel(cnt, row, heat_any, lane, vert, share, out, heat, diff, picked, sems):
    loads = [pltpu.make_async_copy(heat_any.at[t], heat.at[t], sems.at[t]) for t in range(T)]
    for c in loads:
        c.start()

    for t in range(T):
        loads[t].wait()

        def make(q, _):
            x = heat[t, at8(q), :]
            d = pltpu.roll(x, Z - 1, 1) - x
            for zc in range(8):
                diff[at8((t * 8 + q) * 8 + zc), :] = d[:, zc * 128:(zc + 1) * 128]
            return 0

        lax.fori_loop(0, R // 8, make, 0, unroll=4)
    for j in range(GROUPS):
        def body(b, _):
            base = pl.multiple_of(b * UNROLL, UNROLL)
            for u in range(UNROLL):
                picked[pl.ds(base + u, 1), :] = diff[pl.ds(row[j, base + u], 1), :]
            return 0

        lax.fori_loop(0, (cnt[j] + UNROLL - 1) // UNROLL, body, 0)
        vals = []
        for kb in range(SLOTS // 128):
            cut = slice(kb * 128, (kb + 1) * 128)
            hit = iota((128, 128), 0) == lane[j:j + 1, cut]
            vals.append(jnp.sum(jnp.where(hit, picked[cut, :].T, 0.0), axis=0, keepdims=True))
        live = iota((1, SLOTS), 1) < cnt[j]
        val = jnp.where(live, share[j:j + 1, :] * jnp.concatenate(vals, axis=1), 0.0)
        v = vert[j:j + 1, :]
        inner = iota((BS, SLOTS), 0) == (v & (BS - 1))
        left = jnp.concatenate(
            [jnp.where(inner, p.astype(F32), 0.0).astype(BF16) for p in pieces(val)], axis=0)
        right = jnp.where(iota((NB, SLOTS), 0) == (v >> 4), 1.0, 0.0).astype(BF16)
        o = lax.dot_general(left, right, (((1,), (1,)), ((), ())), preferred_element_type=F32)
        o = o[:BS] + o[BS:2 * BS] + o[2 * BS:]
        for n in range(out.shape[0]):
            out[n, j * BS:(j + 1) * BS, :] = o


def front_kernel(kref, cnt, row, parts, cross, lane, vert, share, pred_any, *refs):
    front_body(kref, cnt, row, parts, cross, lane, vert, share, pred_any, *refs[5:])


def front_body(kref, cnt, row, parts, cross, lane, vert, share, pred_any, src_any, sup, sdown, srup, srdown,
               hout, front, gtab, height, terms, flux, pred, zeros, flip, sems, zsems, *acc):
    k = kref[0]
    load = pltpu.make_async_copy(pred_any, pred, sems.at[0])
    load.start()
    params_in = pltpu.make_async_copy(cross.at[:, pl.ds(2 * T, FT)], front, sems.at[6])
    params_in.start()
    zeros[...] = jnp.zeros(zeros.shape, F32)
    count = zeros.shape[0]
    clears = [pltpu.make_async_copy(zeros, a.at[pl.ds(n * count, count)], zsems.at[m, n])
              for m, a in enumerate(acc) for n in range(T * R * 8 // count)]
    for c in clears:
        c.start()
    sums = parts[0]
    for n in range(1, parts.shape[0]):
        sums = sums + parts[n]
    flux[...] = sums
    params_in.wait()

    def held(g, n):
        return jnp.concatenate([front[g, m // 8, :, m % 8 * 128:m % 8 * 128 + 128]
                                for m in (2 * n, 2 * n + 1)], axis=0)

    def neighbours(h):
        last = jnp.concatenate([h[g][BS - 1:BS, :] for g in range(GROUPS)], axis=0)
        first = jnp.concatenate([h[g][0:1, :] for g in range(GROUPS)], axis=0)
        zrow = jnp.zeros((1, 128), F32)
        lr = pltpu.roll(last, 1, 1)
        fr = pltpu.roll(first, 127, 1)
        col = iota((GROUPS, 128), 1)
        lr = jnp.where(col == 0, jnp.concatenate([zrow, lr[:-1]], axis=0), lr)
        fr = jnp.where(col == 127, jnp.concatenate([fr[1:], zrow], axis=0), fr)
        down = [jnp.concatenate([lr[g:g + 1], h[g][:BS - 1]], axis=0) for g in range(GROUPS)]
        up = [jnp.concatenate([h[g][1:], fr[g:g + 1]], axis=0) for g in range(GROUPS)]
        return down, up

    prior = [held(g, BS) for g in range(GROUPS)]
    h = list(prior)
    for _ in range(ITERS):
        down, up = neighbours(h)
        for g in range(GROUPS):
            applied = (2.0 + held(g, BS + 1)) * h[g] - down[g] - up[g]
            res = held(g, BS + 2) + COUPLE * flux[g * BS:(g + 1) * BS, :] - applied
            h[g] = h[g] + jnp.concatenate(
                [jnp.sum(held(g, i) * res, axis=0, keepdims=True) for i in range(BS)], axis=0)
    down, up = neighbours(h)
    for g in range(GROUPS):
        slope = up[g] - down[g]
        growth = h[g] - prior[g]
        height[g] = h[g]
        gtab[g] = (flux[g * BS:(g + 1) * BS, :] - STEFAN * growth) * jnp.sqrt(1.0 + slope * slope)
    for j in range(GROUPS):
        v = vert[j:j + 1, :]
        right = jnp.where(iota((NB, SLOTS), 0) == (v >> 4), 1.0, 0.0).astype(BF16)
        x = jnp.dot(jnp.concatenate(pieces(gtab[j]), axis=0), right, preferred_element_type=F32)
        x = x[:BS] + x[BS:2 * BS] + x[2 * BS:]
        inner = iota((BS, SLOTS), 0) == (v & (BS - 1))
        term = jnp.sum(jnp.where(inner, x, 0.0), axis=0, keepdims=True) * share[j:j + 1, :]
        term = jnp.where(iota((1, SLOTS), 1) < cnt[j], term, 0.0)
        for kb in range(SLOTS // 128):
            cut = slice(kb * 128, (kb + 1) * 128)
            hit = iota((128, 128), 0) == lane[j:j + 1, cut]
            terms[j, cut, :] = jnp.where(hit, term[:, cut], 0.0).T
    for c in clears:
        c.wait()
    most = jnp.maximum(jnp.maximum(cnt[0], cnt[1]), jnp.maximum(cnt[2], cnt[3]))

    def add(b, _):
        for u in range(UNROLL):
            s = b * UNROLL + u
            for j in range(GROUPS):
                at = pl.ds(row[j, s], 1)
                acc[j][at, :] = acc[j][at, :] + terms[j, pl.ds(s, 1), :]
        return 0

    lax.fori_loop(0, (most + UNROLL - 1) // UNROLL, add, 0)

    load.wait()
    src = pred
    sends = []

    def send(m, a, b):
        sends.append(pltpu.make_async_copy(a, b, sems.at[m]))
        sends[-1].start()

    for d in range(T):
        def finish(q, _):
            for zc in range(8):
                a = at8((d * 8 + q) * 8 + zc)
                s = (acc[0][a, :] + acc[1][a, :]) + (acc[2][a, :] + acc[3][a, :])
                cut = slice(zc * 128, (zc + 1) * 128)
                src[d, at8(q), cut] = pred[d, at8(q), cut] + SHRINK * s
            return 0

        lax.fori_loop(0, R // 8, finish, 0, unroll=2)
        if d == H - 2:
            send(1, src.at[pl.ds(0, H - 1)], sdown)
    send(2, src.at[pl.ds(T - H + 1, H - 1)], sup)
    send(3, src.at[:, pl.ds(R - 8, 8)], srup)
    send(4, src.at[:, pl.ds(0, 8)], srdown)
    send(5, src, src_any)
    flip[...] = jnp.concatenate([height[k], jnp.zeros((128 - BS, 128), F32)], axis=0).T
    nodes = flip[pl.ds(0, BS, stride=8), :]
    for m in range(1, 8):
        nodes = nodes + pltpu.roll(flip[pl.ds(m, BS, stride=8), :], m * BS, 1)
    hout[...] = nodes
    for c in sends:
        c.wait()


def pack_kernel(kref, load_any, beta_any, solve, prior, weight, jump, label, up, down, cross,
                row, lane, load, beta, front, flip, isems, osems, fsems):
    k = kref[0]
    loads = [pltpu.make_async_copy(a, b, isems.at[n])
             for n, (a, b) in enumerate(((load_any, load), (beta_any, beta)))]
    for c in loads:
        c.start()
    lab = label[...]
    hi = lab >> 10
    low = hi + (lab & 1023)
    carry = (low >= Z - 1).astype(I32)
    column, axial = hi + carry, low - (Z - 1) * carry
    row[...] = ((column >> 3) << 6) + ((axial >> 7) << 3) + (column & 7)
    lane[...] = axial & 127

    def keep(n, x):
        front[n // 8, :, n % 8 * 128:n % 8 * 128 + 128] = x

    for n in range(FT * 8):
        keep(n, solve[n * 8:n * 8 + 8, :] if n < BS * BS // 8 else jnp.zeros((8, 128), F32))
    for n, x in enumerate((prior, weight, jump)):
        for m in range(8):
            flip[pl.ds(m, BS, stride=8), :] = pltpu.roll(x[...], (128 - m * BS) % 128, 1)
        turned = flip[...].T
        keep(BS * BS // 8 + 2 * n, turned[:8, :])
        keep(BS * BS // 8 + 2 * n + 1, turned[8:16, :])
    sends = []
    for d in range(GROUPS):
        sends.append(pltpu.make_async_copy(front, cross.at[d, pl.ds(2 * T, FT)], fsems.at[d]))
        sends[-1].start()
    count = 0
    for n, f in enumerate((load, beta)):
        loads[n].wait()
        pairs = [(f.at[pl.ds(T - H, H)], up.at[pl.ds(n * H, H)]), (f.at[pl.ds(0, H)], down.at[pl.ds(n * H, H)])]
        for d in range(GROUPS):
            first = pl.multiple_of(jnp.where(d < k, 0, R - 8), 8)
            pairs.append((f.at[:, pl.ds(first, 8)], cross.at[d, pl.ds(n * T, T)]))
        for a, b in pairs:
            sends.append(pltpu.make_async_copy(a, b, osems.at[count]))
            sends[-1].start()
            count += 1
    for c in sends:
        c.wait()


def side_kernel(kref, cross, side, eup, edown, below, sems):
    k = kref[0]
    loads = [pltpu.make_async_copy(cross.at[jnp.minimum(k + 1, GROUPS - 1), pl.ds(0, 2 * T)], side, sems.at[0]),
             pltpu.make_async_copy(cross.at[jnp.maximum(k - 1, 0), pl.ds(0, 2 * T)], below, sems.at[1])]
    for c in loads:
        c.start()
    for c in loads:
        c.wait()
    first = iota((8, Z), 0) < 4
    for t in range(2 * T):
        above_t = jnp.where(k < GROUPS - 1, side[t], 0.0)
        below_t = jnp.where(k > 0, below[t], 0.0)
        side[t] = jnp.where(first, above_t, below_t)
    for n in range(2):
        eup[n * H:(n + 1) * H] = side[n * T + T - H:n * T + T]
        edown[n * H:(n + 1) * H] = side[n * T:n * T + H]


def shift_azim(x, d):
    return lax.ppermute(x, AZIM, [(i, (i + d) % 32) for i in range(32)])


def shift_rad(x, d):
    return lax.ppermute(x, "rad", [(i, i + d) for i in range(4) if 0 <= i + d < 4])


def ring_tile(from_above, from_below):
    return jnp.where(iota(from_above.shape, 1) < 4, from_above, from_below)


def wide(x):
    return jnp.concatenate([x] * (Z // 128), axis=1)


def sweep_kernel(kref, load, beta_in, lo, hi, side, clo, chi, src, slo, shi, sside, sclo, schi,
                 out, pa, pb, beta, th, rr, zz, ww, ss, rads, sems):
    k = kref[0]
    rows, ring = pl.ds(0, R), pl.ds(R, 8)
    half = T // 2

    def planes(own, tile_own, low, tile_low, high, tile_high, first):
        return [(low, tile_low, first, H - first), (own.at[pl.ds(0, half)], tile_own.at[pl.ds(0, half)], H, half),
                (own.at[pl.ds(half, half)], tile_own.at[pl.ds(half, half)], H + half, half),
                (high, tile_high, H + T, H - first)]

    def both(x, n, count):
        return x.at[pl.ds(n * count, count)]

    fields = [(ref, planes(own, both(side, n, T), both(lo, n, H), both(clo, n, H), both(hi, n, H), both(chi, n, H), 0))
              for ref, own, n in ((beta, beta_in, 1), (pa, load, 0))]
    fields.append((ss, planes(src, sside, slo, sclo, shi, schi, 1)))
    waits = []
    for g in range(4):
        cs = []
        for f, (ref, parts) in enumerate(fields):
            main, tile, first, count = parts[g]
            cs.append(pltpu.make_async_copy(main, ref.at[pl.ds(first, count), rows], sems.at[g, f, 0]))
            cs.append(pltpu.make_async_copy(tile, ref.at[pl.ds(first, count), ring], sems.at[g, f, 1]))
        for c in cs:
            c.start()
        waits.append(cs)
    sub, lanes = iota((8, 128), 0), iota((8, 128), 1)
    top, bottom, last_lane, first_lane = sub == 7, sub == 0, lanes == 127, lanes == 0
    angular = (256 / (2.0 * math.pi)) ** 2
    for it in range(RT):
        gi = k * R + (it * 8 + sub if it < RT - 1 else jnp.where(sub < 4, R + sub, sub - 8))
        ra = 0.25 * 256 + gi.astype(F32) + 0.5
        rads[0, it] = ra
        rads[1, it] = (0.5 * angular) / ra
        rads[2, it] = jnp.where((gi >= 0) & (gi < 255), 0.5 * (ra + 0.5), 0.0)
    nothing = jnp.zeros((8, 128), F32)
    columns = range(Z // 128)

    def cut(it):
        it = it % RT
        return slice(it * 8, it * 8 + 8)

    def vec(ref, t, it, v):
        return ref[t, cut(it), v * 128:v * 128 + 128]

    def put(ref, t, it, v, x):
        ref[t, cut(it), v * 128:v * 128 + 128] = x

    def up_row(x):
        return pltpu.roll(x, 7, 0)

    def down_row(x):
        return pltpu.roll(x, 1, 0)

    def next_lane(ref, t, it, v, cur):
        nxt = pltpu.roll(vec(ref, t, it, v + 1), 127, 1) if v + 1 < Z // 128 else cur
        return jnp.where(last_lane, nxt, cur), nxt

    def relaxed(old, t, it, v, p, pz, pu, prev, zprev, tu, td, r, z, w, s):
        acc = (tu * vec(old, t + 1, it, v) + td * vec(old, t - 1, it, v)) + r * pu
        rp = down_row(r * p)
        acc = acc + jnp.where(bottom, prev, rp)
        zu, pz = next_lane(old, t, it, v, pz)
        zp = pltpu.roll(z * p, 1, 1)
        acc = acc + (z * zu + jnp.where(first_lane, zprev, zp))
        return (1.0 - OMEGA) * p + w * (acc - s), pz, rp, zp

    def first_sweep(t, _):
        last = RT - 1
        bup = [up_row(vec(beta, t, 0, v)) for v in columns]
        pup = [up_row(vec(pa, t, 0, v)) for v in columns]
        fprev, prev = [], []
        for v in columns:
            b = vec(beta, t, last, v)
            face = (b + jnp.where(top, bup[v], up_row(b))) * rads[2, last]
            fprev.append(down_row(face))
            prev.append(down_row(face * vec(pa, t, last, v)))
        for it in range(RT):
            ra, ang, rad = rads[0, it], rads[1, it], rads[2, it]
            axi = (0.5 * AXIAL) * ra
            bz = pltpu.roll(vec(beta, t, it, 0), 127, 1)
            pz = pltpu.roll(vec(pa, t, it, 0), 127, 1)
            zfprev = zprev = nothing
            for v in columns:
                b, p = vec(beta, t, it, v), vec(pa, t, it, v)
                nb, np_ = up_row(vec(beta, t, it + 1, v)), up_row(vec(pa, t, it + 1, v))
                tu = (b + vec(beta, t + 1, it, v)) * ang
                td = vec(th, t - 1, it, v)
                r = (b + jnp.where(top, nb, bup[v])) * rad
                froll = down_row(r)
                other = jnp.where(bottom, fprev[v], froll)
                bu, bz = next_lane(beta, t, it, v, bz)
                zf = (b + bu) * axi
                z = zf
                if v == Z // 128 - 1:
                    zf = jnp.where(last_lane, 2.0 * (b * axi), zf)
                    z = jnp.where(last_lane, 0.0, zf)
                zr = pltpu.roll(z, 1, 1)
                d = (tu + td) + (r + other) + (zf + jnp.where(first_lane, zfprev, zr))
                if it == last:
                    d = jnp.where(d > 0.0, d, 1.0)
                w = pl.reciprocal(d, approx=True)
                w = w * (2.0 - d * w)
                w = (w * (2.0 - d * w)) * OMEGA
                sc = vec(ss, t, it, v) * ra
                put(th, t, it, v, tu)
                put(rr, t, it, v, r)
                put(zz, t, it, v, z)
                put(ww, t, it, v, w)
                put(ss, t, it, v, sc)
                pu = jnp.where(top, np_, pup[v])
                new, pz, prev[v], zprev = relaxed(pa, t, it, v, p, pz, pu, prev[v], zprev, tu, td, r, z, w, sc)
                put(pb, t, it, v, new)
                bup[v], pup[v], fprev[v], zfprev = nb, np_, froll, zr
        return 0

    def sweep(old, new, t, tiles, shift):
        pup = [up_row(vec(old, t, 0, v)) for v in columns]
        prev = [down_row(vec(rr, t, -1, v) * vec(old, t, -1, v)) for v in columns]
        for it in range(tiles):
            pz = pltpu.roll(vec(old, t, it, 0), 127, 1)
            zprev = nothing
            for v in columns:
                p = vec(old, t, it, v)
                np_ = up_row(vec(old, t, it + 1, v))
                pu = jnp.where(top, np_, pup[v])
                x, pz, prev[v], zprev = relaxed(
                    old, t, it, v, p, pz, pu, prev[v], zprev, vec(th, t, it, v), vec(th, t - 1, it, v),
                    vec(rr, t, it, v), vec(zz, t, it, v), vec(ww, t, it, v), vec(ss, t, it, v))
                put(new, t - shift, it, v, x)
                pup[v] = np_
        return 0

    ends = (H - 1, H + half - 1, H + T - 1, TE - 1)
    start = 1
    for g in range(4):
        for c in waits[g]:
            c.wait()
        if g == 0:
            for it in range(RT):
                th[0, cut(it), :] = (beta[0, cut(it), :] + beta[1, cut(it), :]) * wide(rads[1, it])
        lax.fori_loop(start, ends[g], first_sweep, 0)
        start = ends[g]
    lax.fori_loop(2, TE - 2, lambda t, _: sweep(pb, pa, t, RT, 0), 0)
    lax.fori_loop(3, TE - 3, lambda t, _: sweep(pa, pb, t, RT, 0), 0)
    lax.fori_loop(4, TE - 4, lambda t, _: sweep(pb, out, t, RT - 1, H), 0)


def from_all(copies, axes):
    return lax.all_to_all(copies, axes, 0, 0)


def sum_kernel(parts, *refs):
    out = refs[-1]
    s = parts[0]
    for n in range(1, parts.shape[0]):
        s = s + parts[n]
    for n in range(out.shape[0]):
        out[n] = s


VM = pl.BlockSpec(memory_space=pltpu.VMEM)
SM = pl.BlockSpec(memory_space=pltpu.SMEM)
ANY = pl.BlockSpec(memory_space=pl.ANY)


def params(mib):
    return pltpu.CompilerParams(vmem_limit_bytes=mib << 20)


def cost(us):
    return pl.CostEstimate(flops=1000, bytes_accessed=us * 3000000, transcendentals=0)


def per_device(load, outflow, beta, heat, label, vertex, share, tally, prior, weight, jump, solve):
    label = label.reshape(GROUPS, SLOTS)
    vertex = vertex.reshape(GROUPS, SLOTS)
    share = share.reshape(GROUPS, SLOTS)
    tally = tally.reshape(GROUPS)
    kidx = lax.axis_index("rad").astype(I32).reshape(1)
    nodes = lambda v: v.reshape(BS, NB)

    shape = lambda *d: jax.ShapeDtypeStruct(d, F32)
    slot = jax.ShapeDtypeStruct((GROUPS, SLOTS), I32)
    plane = lambda n: shape(n, R, Z)
    tile = lambda n: shape(n, 8, Z)
    block = pltpu.VMEM((T, R, Z), F32)
    up, down, cross, row, lane = pl.pallas_call(
        pack_kernel,
        out_shape=(plane(2 * H), plane(2 * H), shape(GROUPS, 2 * T + FT, 8, Z), slot, slot),
        in_specs=[SM] + [ANY] * 2 + [VM] * 5, out_specs=(ANY,) * 3 + (VM,) * 2,
        scratch_shapes=[block, block, pltpu.VMEM((FT, 8, Z), F32), pltpu.VMEM((128, 128), F32),
                        pltpu.SemaphoreType.DMA((2,)), pltpu.SemaphoreType.DMA((12,)),
                        pltpu.SemaphoreType.DMA((GROUPS,))],
        compiler_params=params(10), cost_estimate=cost(4), name="pack",
    )(kidx, load, beta, solve.reshape(BS * BS, NB), nodes(prior), nodes(weight), nodes(jump), label)
    lo, hi = shift_azim(up, 1), shift_azim(down, -1)
    cross = from_all(cross, "rad")

    partial = pl.pallas_call(
        flux_kernel, out_shape=shape(8, GROUPS * BS, NB),
        in_specs=[SM, SM, ANY, VM, VM, VM], out_specs=VM,
        scratch_shapes=[block, pltpu.VMEM((T * R * 8, 128), F32), pltpu.VMEM((SLOTS, 128), F32),
                        pltpu.SemaphoreType.DMA((T,))],
        compiler_params=params(12), cost_estimate=cost(10), name="flux",
    )(tally, row, heat, lane, vertex, share)
    side, eup, edown = pl.pallas_call(
        side_kernel, out_shape=(tile(2 * T), tile(2 * H), tile(2 * H)),
        in_specs=[SM, ANY], out_specs=(VM,) * 3,
        scratch_shapes=[pltpu.VMEM((2 * T, 8, Z), F32), pltpu.SemaphoreType.DMA((2,))],
        compiler_params=params(4), cost_estimate=cost(2), name="side",
    )(kidx, cross)
    clo, chi = shift_azim(eup, 1), shift_azim(edown, -1)
    near = pl.pallas_call(
        sum_kernel, out_shape=shape(16, GROUPS * BS, NB),
        in_specs=[VM, ANY], out_specs=VM, compiler_params=params(4), name="near",
    )(from_all(partial, ("z", "core")), side)
    flux = from_all(near, ("y", "rad"))
    source, sup, sdown, srup, srdown, height = pl.pallas_call(
        front_kernel,
        out_shape=(plane(T), plane(H - 1), plane(H - 1), tile(T), tile(T), shape(BS, NB)),
        in_specs=[SM, SM, SM, VM, ANY, VM, VM, VM] + [ANY] * 6, out_specs=(ANY,) * 5 + (VM,),
        scratch_shapes=[pltpu.VMEM((GROUPS, FT, 8, Z), F32),
                        pltpu.VMEM((GROUPS, BS, NB), F32), pltpu.VMEM((GROUPS, BS, NB), F32),
                        pltpu.VMEM((GROUPS, SLOTS, 128), F32), pltpu.VMEM((GROUPS * BS, NB), F32),
                        block, pltpu.VMEM((R * 8, 128), F32), pltpu.VMEM((128, 128), F32),
                        pltpu.SemaphoreType.DMA((7,)), pltpu.SemaphoreType.DMA((GROUPS, T))]
        + [pltpu.VMEM((T * R * 8, 128), F32)] * GROUPS,
        compiler_params=params(20), cost_estimate=cost(10), name="front",
    )(kidx, tally, row, flux, cross, lane, vertex, share, outflow, lo, hi, side, clo, chi)
    slo, shi = shift_azim(sup, 1), shift_azim(sdown, -1)
    sside = ring_tile(shift_rad(srdown, -1), shift_rad(srup, 1))
    sclo, schi = shift_azim(sside[T - H + 1:], 1), shift_azim(sside[:H - 1], -1)
    ext = pltpu.VMEM((TE, RE, Z), F32)
    pressure = pl.pallas_call(
        sweep_kernel, out_shape=plane(T),
        in_specs=[SM] + [ANY] * 13, out_specs=VM,
        scratch_shapes=[ext] * 8 + [pltpu.VMEM((3, RT, 8, 128), F32), pltpu.SemaphoreType.DMA((4, 3, 2))],
        compiler_params=params(46), cost_estimate=cost(20), name="sweeps",
    )(kidx, load, beta, lo, hi, side, clo, chi, source, slo, shi, sside, sclo, schi)
    return pressure, height.reshape(NB * BS)


def solution(mesh):
    fine = jax.sharding.Mesh(mesh.devices.reshape(4, 4, 2, 4), AZIM + ("rad",))
    cells = P(AZIM, "rad", None)
    slots = P(AZIM, "rad", None, None)
    return jax.shard_map(
        per_device,
        mesh=fine,
        in_specs=(cells, cells, cells, cells, slots, slots, slots, cells,
                  P("rad"), P("rad"), P("rad"), P(None, None, "rad")),
        out_specs=(cells, P("rad")),
        check_vma=False,
    )
```

```python
import functools
import math

import jax
import jax.numpy as jnp
from jax import lax
from jax.experimental import pallas as pl
from jax.experimental.pallas import tpu as pltpu
from jax.sharding import PartitionSpec as P

SWEEPS = 4
ITERS = 4
OMEGA = 0.9
AXIAL = 0.25
STEFAN = 1.0
SHRINK = 0.3
COUPLE = 0.2

F32 = jnp.float32
I32 = jnp.int32
BF16 = jnp.bfloat16

T, R, Z = 8, 64, 1024
H = 4
TE = T + 2 * H
RE = R + 8
RT = RE // 8
GROUPS, SLOTS, NB, BS = 4, 1024, 128, 16
FROWS = BS * BS + 3 * BS
UNROLL = 16
AZIM = ("y", "z", "core")


def iota(shape, dim):
    return lax.broadcasted_iota(I32, shape, dim)


def pieces(x):
    h = x.astype(BF16)
    rest = x - h.astype(F32)
    m = rest.astype(BF16)
    return h, m, (rest - m.astype(F32)).astype(BF16)


def at8(i):
    return pl.ds(pl.multiple_of(i * 8, 8), 8)


def flux_kernel(cnt, row, heat_any, lane, vert, share, out, heat, diff, picked, sems):
    loads = [pltpu.make_async_copy(heat_any.at[t], heat.at[t], sems.at[t]) for t in range(T)]
    for c in loads:
        c.start()

    for t in range(T):
        loads[t].wait()

        def make(q, _):
            x = heat[t, at8(q), :]
            d = pltpu.roll(x, Z - 1, 1) - x
            for zc in range(8):
                diff[at8((t * 8 + q) * 8 + zc), :] = d[:, zc * 128:(zc + 1) * 128]
            return 0

        lax.fori_loop(0, R // 8, make, 0, unroll=4)
    for j in range(GROUPS):
        def body(b, _):
            base = pl.multiple_of(b * UNROLL, UNROLL)
            for u in range(UNROLL):
                picked[pl.ds(base + u, 1), :] = diff[pl.ds(row[j, base + u], 1), :]
            return 0

        lax.fori_loop(0, (cnt[j] + UNROLL - 1) // UNROLL, body, 0)
        vals = []
        for kb in range(SLOTS // 128):
            cut = slice(kb * 128, (kb + 1) * 128)
            hit = iota((128, 128), 0) == lane[j:j + 1, cut]
            vals.append(jnp.sum(jnp.where(hit, picked[cut, :].T, 0.0), axis=0, keepdims=True))
        live = iota((1, SLOTS), 1) < cnt[j]
        val = jnp.where(live, share[j:j + 1, :] * jnp.concatenate(vals, axis=1), 0.0)
        v = vert[j:j + 1, :]
        inner = iota((BS, SLOTS), 0) == (v & (BS - 1))
        left = jnp.concatenate(
            [jnp.where(inner, p.astype(F32), 0.0).astype(BF16) for p in pieces(val)], axis=0)
        right = jnp.where(iota((NB, SLOTS), 0) == (v >> 4), 1.0, 0.0).astype(BF16)
        o = lax.dot_general(left, right, (((1,), (1,)), ((), ())), preferred_element_type=F32)
        o = o[:BS] + o[BS:2 * BS] + o[2 * BS:]
        for n in range(out.shape[0]):
            out[n, j * BS:(j + 1) * BS, :] = o


def front_kernel(kref, cnt, row, parts, f0, f1, f2, f3, lane, vert, share, pred_any, *refs):
    front_body(kref, cnt, row, parts, (f0, f1, f2, f3), lane, vert, share, pred_any, *refs[5:])


def front_body(kref, cnt, row, parts, fronts, lane, vert, share, pred_any, src_any, sup, sdown, srup, srdown,
               hout, front, gtab, height, terms, flux, pred, zeros, flip, sems, zsems, *acc):
    k = kref[0]
    load = pltpu.make_async_copy(pred_any, pred, sems.at[0])
    load.start()
    zeros[...] = jnp.zeros(zeros.shape, F32)
    count = zeros.shape[0]
    clears = [pltpu.make_async_copy(zeros, a.at[pl.ds(n * count, count)], zsems.at[m, n])
              for m, a in enumerate(acc) for n in range(T * R * 8 // count)]
    for c in clears:
        c.start()
    sums = parts[0]
    for n in range(1, parts.shape[0]):
        sums = sums + parts[n]
    flux[...] = sums
    for n, f in enumerate(fronts):
        front[lax.rem(k + GROUPS - n, GROUPS)] = f[...]

    def held(g, n):
        return front[g, n * BS:n * BS + BS, :]

    def neighbours(h):
        last = jnp.concatenate([h[g][BS - 1:BS, :] for g in range(GROUPS)], axis=0)
        first = jnp.concatenate([h[g][0:1, :] for g in range(GROUPS)], axis=0)
        zrow = jnp.zeros((1, 128), F32)
        lr = pltpu.roll(last, 1, 1)
        fr = pltpu.roll(first, 127, 1)
        col = iota((GROUPS, 128), 1)
        lr = jnp.where(col == 0, jnp.concatenate([zrow, lr[:-1]], axis=0), lr)
        fr = jnp.where(col == 127, jnp.concatenate([fr[1:], zrow], axis=0), fr)
        down = [jnp.concatenate([lr[g:g + 1], h[g][:BS - 1]], axis=0) for g in range(GROUPS)]
        up = [jnp.concatenate([h[g][1:], fr[g:g + 1]], axis=0) for g in range(GROUPS)]
        return down, up

    prior = [held(g, BS) for g in range(GROUPS)]
    h = list(prior)
    for _ in range(ITERS):
        down, up = neighbours(h)
        for g in range(GROUPS):
            applied = (2.0 + held(g, BS + 1)) * h[g] - down[g] - up[g]
            res = held(g, BS + 2) + COUPLE * flux[g * BS:(g + 1) * BS, :] - applied
            h[g] = h[g] + jnp.concatenate(
                [jnp.sum(held(g, i) * res, axis=0, keepdims=True) for i in range(BS)], axis=0)
    down, up = neighbours(h)
    for g in range(GROUPS):
        slope = up[g] - down[g]
        growth = h[g] - prior[g]
        height[g] = h[g]
        gtab[g] = (flux[g * BS:(g + 1) * BS, :] - STEFAN * growth) * jnp.sqrt(1.0 + slope * slope)
    for j in range(GROUPS):
        v = vert[j:j + 1, :]
        right = jnp.where(iota((NB, SLOTS), 0) == (v >> 4), 1.0, 0.0).astype(BF16)
        x = jnp.dot(jnp.concatenate(pieces(gtab[j]), axis=0), right, preferred_element_type=F32)
        x = x[:BS] + x[BS:2 * BS] + x[2 * BS:]
        inner = iota((BS, SLOTS), 0) == (v & (BS - 1))
        term = jnp.sum(jnp.where(inner, x, 0.0), axis=0, keepdims=True) * share[j:j + 1, :]
        term = jnp.where(iota((1, SLOTS), 1) < cnt[j], term, 0.0)
        for kb in range(SLOTS // 128):
            cut = slice(kb * 128, (kb + 1) * 128)
            hit = iota((128, 128), 0) == lane[j:j + 1, cut]
            terms[j, cut, :] = jnp.where(hit, term[:, cut], 0.0).T
    for c in clears:
        c.wait()
    most = jnp.maximum(jnp.maximum(cnt[0], cnt[1]), jnp.maximum(cnt[2], cnt[3]))

    def add(b, _):
        for u in range(UNROLL):
            s = b * UNROLL + u
            for j in range(GROUPS):
                at = pl.ds(row[j, s], 1)
                acc[j][at, :] = acc[j][at, :] + terms[j, pl.ds(s, 1), :]
        return 0

    lax.fori_loop(0, (most + UNROLL - 1) // UNROLL, add, 0)

    load.wait()
    src = pred
    sends = []

    def send(m, a, b):
        sends.append(pltpu.make_async_copy(a, b, sems.at[m]))
        sends[-1].start()

    for d in range(T):
        def finish(q, _):
            for zc in range(8):
                a = at8((d * 8 + q) * 8 + zc)
                s = (acc[0][a, :] + acc[1][a, :]) + (acc[2][a, :] + acc[3][a, :])
                cut = slice(zc * 128, (zc + 1) * 128)
                src[d, at8(q), cut] = pred[d, at8(q), cut] + SHRINK * s
            return 0

        lax.fori_loop(0, R // 8, finish, 0, unroll=2)
        if d == H - 2:
            send(1, src.at[pl.ds(0, H - 1)], sdown)
    send(2, src.at[pl.ds(T - H + 1, H - 1)], sup)
    send(3, src.at[:, pl.ds(R - 8, 8)], srup)
    send(4, src.at[:, pl.ds(0, 8)], srdown)
    send(5, src, src_any)
    flip[...] = jnp.concatenate([height[k], jnp.zeros((128 - BS, 128), F32)], axis=0).T
    nodes = flip[pl.ds(0, BS, stride=8), :]
    for m in range(1, 8):
        nodes = nodes + pltpu.roll(flip[pl.ds(m, BS, stride=8), :], m * BS, 1)
    hout[...] = nodes
    for c in sends:
        c.wait()


def pack_kernel(load_any, beta_any, solve, prior, weight, jump, label, up, down, rup, rdown,
                front, row, lane, load, beta, flip, isems, osems):
    loads = [pltpu.make_async_copy(a, b, isems.at[n])
             for n, (a, b) in enumerate(((load_any, load), (beta_any, beta)))]
    for c in loads:
        c.start()
    lab = label[...]
    hi = lab >> 10
    low = hi + (lab & 1023)
    carry = (low >= Z - 1).astype(I32)
    column, axial = hi + carry, low - (Z - 1) * carry
    row[...] = ((column >> 3) << 6) + ((axial >> 7) << 3) + (column & 7)
    lane[...] = axial & 127

    front[0:BS * BS, :] = solve[...]
    for n, x in enumerate((prior, weight, jump)):
        for m in range(8):
            flip[pl.ds(m, BS, stride=8), :] = pltpu.roll(x[...], (128 - m * BS) % 128, 1)
        at = BS * BS + n * BS
        front[at:at + BS, :] = flip[...].T[:BS, :]
    sends = []
    for n, f in enumerate((load, beta)):
        loads[n].wait()
        for a, b in ((f.at[pl.ds(T - H, H)], up.at[pl.ds(n * H, H)]),
                     (f.at[pl.ds(0, H)], down.at[pl.ds(n * H, H)]),
                     (f.at[:, pl.ds(R - 8, 8)], rup.at[pl.ds(n * T, T)]),
                     (f.at[:, pl.ds(0, 8)], rdown.at[pl.ds(n * T, T)])):
            sends.append(pltpu.make_async_copy(a, b, osems.at[len(sends)]))
            sends[-1].start()
    for c in sends:
        c.wait()


def side_kernel(above, below_any, side, eup, edown, below, sems):
    loads = [pltpu.make_async_copy(above, side, sems.at[0]), pltpu.make_async_copy(below_any, below, sems.at[1])]
    for c in loads:
        c.start()
    for c in loads:
        c.wait()
    first = iota((8, Z), 0) < 4
    for t in range(2 * T):
        side[t] = jnp.where(first, side[t], below[t])
    for n in range(2):
        eup[n * H:(n + 1) * H] = side[n * T + T - H:n * T + T]
        edown[n * H:(n + 1) * H] = side[n * T:n * T + H]


def shift_azim(x, d):
    return lax.ppermute(x, AZIM, [(i, (i + d) % 32) for i in range(32)])


def shift_rad(x, d):
    return lax.ppermute(x, "rad", [(i, i + d) for i in range(4) if 0 <= i + d < 4])


def ring_tile(from_above, from_below):
    return jnp.where(iota(from_above.shape, 1) < 4, from_above, from_below)


def wide(x):
    return jnp.concatenate([x] * (Z // 128), axis=1)


def sweep_kernel(kref, load, beta_in, lo, hi, side, clo, chi, src, slo, shi, sside, sclo, schi,
                 out, pa, pb, beta, th, rr, zz, ww, ss, rads, sems):
    k = kref[0]
    rows, ring = pl.ds(0, R), pl.ds(R, 8)
    half = T // 2

    def planes(own, tile_own, low, tile_low, high, tile_high, first):
        return [(low, tile_low, first, H - first), (own.at[pl.ds(0, half)], tile_own.at[pl.ds(0, half)], H, half),
                (own.at[pl.ds(half, half)], tile_own.at[pl.ds(half, half)], H + half, half),
                (high, tile_high, H + T, H - first)]

    def both(x, n, count):
        return x.at[pl.ds(n * count, count)]

    fields = [(ref, planes(own, both(side, n, T), both(lo, n, H), both(clo, n, H), both(hi, n, H), both(chi, n, H), 0))
              for ref, own, n in ((beta, beta_in, 1), (pa, load, 0))]
    fields.append((ss, planes(src, sside, slo, sclo, shi, schi, 1)))
    waits = []
    for g in range(4):
        cs = []
        for f, (ref, parts) in enumerate(fields):
            main, tile, first, count = parts[g]
            cs.append(pltpu.make_async_copy(main, ref.at[pl.ds(first, count), rows], sems.at[g, f, 0]))
            cs.append(pltpu.make_async_copy(tile, ref.at[pl.ds(first, count), ring], sems.at[g, f, 1]))
        waits.append(cs)

    def begin(g):
        for c in waits[g] if g < 4 else ():
            c.start()

    begin(0)
    begin(1)
    sub, lanes = iota((8, 128), 0), iota((8, 128), 1)
    top, bottom, last_lane, first_lane = sub == 7, sub == 0, lanes == 127, lanes == 0
    angular = (256 / (2.0 * math.pi)) ** 2
    for it in range(RT):
        gi = k * R + (it * 8 + sub if it < RT - 1 else jnp.where(sub < 4, R + sub, sub - 8))
        ra = 0.25 * 256 + gi.astype(F32) + 0.5
        rads[0, it] = ra
        rads[1, it] = (0.5 * angular) / ra
        rads[2, it] = jnp.where((gi >= 0) & (gi < 255), 0.5 * (ra + 0.5), 0.0)
    nothing = jnp.zeros((8, 128), F32)
    columns = range(Z // 128)

    def cut(it):
        it = it % RT
        return slice(it * 8, it * 8 + 8)

    def vec(ref, t, it, v):
        return ref[t, cut(it), v * 128:v * 128 + 128]

    def put(ref, t, it, v, x):
        ref[t, cut(it), v * 128:v * 128 + 128] = x

    def up_row(x):
        return pltpu.roll(x, 7, 0)

    def down_row(x):
        return pltpu.roll(x, 1, 0)

    def next_lane(ref, t, it, v, cur):
        nxt = pltpu.roll(vec(ref, t, it, v + 1), 127, 1) if v + 1 < Z // 128 else cur
        return jnp.where(last_lane, nxt, cur), nxt

    def relaxed(old, t, it, v, p, pz, pu, prev, zprev, tu, td, r, z, w, s):
        acc = (tu * vec(old, t + 1, it, v) + td * vec(old, t - 1, it, v)) + r * pu
        rp = down_row(r * p)
        acc = acc + jnp.where(bottom, prev, rp)
        zu, pz = next_lane(old, t, it, v, pz)
        zp = pltpu.roll(z * p, 1, 1)
        acc = acc + (z * zu + jnp.where(first_lane, zprev, zp))
        return (1.0 - OMEGA) * p + w * (acc - s), pz, rp, zp

    def first_sweep(t, _):
        last = RT - 1
        bup = [up_row(vec(beta, t, 0, v)) for v in columns]
        pup = [up_row(vec(pa, t, 0, v)) for v in columns]
        fprev, prev = [], []
        for v in columns:
            b = vec(beta, t, last, v)
            face = (b + jnp.where(top, bup[v], up_row(b))) * rads[2, last]
            fprev.append(down_row(face))
            prev.append(down_row(face * vec(pa, t, last, v)))
        for it in range(RT):
            ra, ang, rad = rads[0, it], rads[1, it], rads[2, it]
            axi = (0.5 * AXIAL) * ra
            bz = pltpu.roll(vec(beta, t, it, 0), 127, 1)
            pz = pltpu.roll(vec(pa, t, it, 0), 127, 1)
            zfprev = zprev = nothing
            for v in columns:
                b, p = vec(beta, t, it, v), vec(pa, t, it, v)
                nb, np_ = up_row(vec(beta, t, it + 1, v)), up_row(vec(pa, t, it + 1, v))
                tu = (b + vec(beta, t + 1, it, v)) * ang
                td = vec(th, t - 1, it, v)
                r = (b + jnp.where(top, nb, bup[v])) * rad
                froll = down_row(r)
                other = jnp.where(bottom, fprev[v], froll)
                bu, bz = next_lane(beta, t, it, v, bz)
                zf = (b + bu) * axi
                z = zf
                if v == Z // 128 - 1:
                    zf = jnp.where(last_lane, 2.0 * (b * axi), zf)
                    z = jnp.where(last_lane, 0.0, zf)
                zr = pltpu.roll(z, 1, 1)
                d = (tu + td) + (r + other) + (zf + jnp.where(first_lane, zfprev, zr))
                if it == last:
                    d = jnp.where(d > 0.0, d, 1.0)
                w = pl.reciprocal(d, approx=True)
                w = w * (2.0 - d * w)
                w = (w * (2.0 - d * w)) * OMEGA
                sc = vec(ss, t, it, v) * ra
                put(th, t, it, v, tu)
                put(rr, t, it, v, r)
                put(zz, t, it, v, z)
                put(ww, t, it, v, w)
                put(ss, t, it, v, sc)
                pu = jnp.where(top, np_, pup[v])
                new, pz, prev[v], zprev = relaxed(pa, t, it, v, p, pz, pu, prev[v], zprev, tu, td, r, z, w, sc)
                put(pb, t, it, v, new)
                bup[v], pup[v], fprev[v], zfprev = nb, np_, froll, zr
        return 0

    def sweep(old, new, t, tiles, shift):
        pup = [up_row(vec(old, t, 0, v)) for v in columns]
        prev = [down_row(vec(rr, t, -1, v) * vec(old, t, -1, v)) for v in columns]
        for it in range(tiles):
            pz = pltpu.roll(vec(old, t, it, 0), 127, 1)
            zprev = nothing
            for v in columns:
                p = vec(old, t, it, v)
                np_ = up_row(vec(old, t, it + 1, v))
                pu = jnp.where(top, np_, pup[v])
                x, pz, prev[v], zprev = relaxed(
                    old, t, it, v, p, pz, pu, prev[v], zprev, vec(th, t, it, v), vec(th, t - 1, it, v),
                    vec(rr, t, it, v), vec(zz, t, it, v), vec(ww, t, it, v), vec(ss, t, it, v))
                put(new, t - shift, it, v, x)
                pup[v] = np_
        return 0

    ends = (H - 1, H + half - 1, H + T - 1, TE - 1)
    start = 1
    for g in range(4):
        for c in waits[g]:
            c.wait()
        begin(g + 2)
        if g == 0:
            for it in range(RT):
                th[0, cut(it), :] = (beta[0, cut(it), :] + beta[1, cut(it), :]) * wide(rads[1, it])
        lax.fori_loop(start, ends[g], first_sweep, 0)
        start = ends[g]
    lax.fori_loop(2, TE - 2, lambda t, _: sweep(pb, pa, t, RT, 0), 0)
    lax.fori_loop(3, TE - 3, lambda t, _: sweep(pa, pb, t, RT, 0), 0)
    lax.fori_loop(4, TE - 4, lambda t, _: sweep(pb, out, t, RT - 1, H), 0)


def from_all(copies, axes):
    return lax.all_to_all(copies, axes, 0, 0)


def sum_kernel(parts, *refs):
    out = refs[-1]
    s = parts[0]
    for n in range(1, parts.shape[0]):
        s = s + parts[n]
    for n in range(out.shape[0]):
        out[n] = s


VM = pl.BlockSpec(memory_space=pltpu.VMEM)
SM = pl.BlockSpec(memory_space=pltpu.SMEM)
ANY = pl.BlockSpec(memory_space=pltpu.HBM)


def params(mib):
    return pltpu.CompilerParams(vmem_limit_bytes=62 << 20)


def cost(us):
    return pl.CostEstimate(flops=1000, bytes_accessed=us * 3000000, transcendentals=0)


def per_device(load, outflow, beta, heat, label, vertex, share, tally, prior, weight, jump, solve):
    label = label.reshape(GROUPS, SLOTS)
    vertex = vertex.reshape(GROUPS, SLOTS)
    share = share.reshape(GROUPS, SLOTS)
    tally = tally.reshape(GROUPS)
    kidx = lax.axis_index("rad").astype(I32).reshape(1)
    nodes = lambda v: v.reshape(BS, NB)

    shape = lambda *d: jax.ShapeDtypeStruct(d, F32)
    slot = jax.ShapeDtypeStruct((GROUPS, SLOTS), I32)
    plane = lambda n: shape(n, R, Z)
    tile = lambda n: shape(n, 8, Z)
    block = pltpu.VMEM((T, R, Z), F32)
    up, down, rup, rdown, front, row, lane = pl.pallas_call(
        pack_kernel,
        out_shape=(plane(2 * H), plane(2 * H), tile(2 * T), tile(2 * T), shape(FROWS, NB), slot, slot),
        in_specs=[ANY] * 2 + [VM] * 5, out_specs=(ANY,) * 4 + (VM,) * 3,
        scratch_shapes=[block, block, pltpu.VMEM((128, 128), F32),
                        pltpu.SemaphoreType.DMA((2,)), pltpu.SemaphoreType.DMA((8,))],
        compiler_params=params(10), cost_estimate=cost(4), name="pack",
    )(load, beta, solve.reshape(BS * BS, NB), nodes(prior), nodes(weight), nodes(jump), label)
    lo, hi = shift_azim(up, 1), shift_azim(down, -1)
    rhi, rlo = shift_rad(rdown, -1), shift_rad(rup, 1)
    fronts = [front] + [
        lax.ppermute(front, "rad", [(i, (i + s) % 4) for i in range(4)]) for s in (1, 2, 3)]

    partial = pl.pallas_call(
        flux_kernel, out_shape=shape(8, GROUPS * BS, NB),
        in_specs=[SM, SM, ANY, VM, VM, VM], out_specs=VM,
        scratch_shapes=[block, pltpu.VMEM((T * R * 8, 128), F32), pltpu.VMEM((SLOTS, 128), F32),
                        pltpu.SemaphoreType.DMA((T,))],
        compiler_params=params(12), cost_estimate=cost(10), name="flux",
    )(tally, row, heat, lane, vertex, share)
    side, eup, edown = pl.pallas_call(
        side_kernel, out_shape=(tile(2 * T), tile(2 * H), tile(2 * H)),
        in_specs=[ANY, ANY], out_specs=(VM,) * 3,
        scratch_shapes=[pltpu.VMEM((2 * T, 8, Z), F32), pltpu.SemaphoreType.DMA((2,))],
        compiler_params=params(4), cost_estimate=cost(2), name="side",
    )(rhi, rlo)
    clo, chi = shift_azim(eup, 1), shift_azim(edown, -1)
    near = pl.pallas_call(
        sum_kernel, out_shape=shape(16, GROUPS * BS, NB),
        in_specs=[VM, ANY], out_specs=VM, compiler_params=params(4), name="near",
    )(from_all(partial, ("z", "core")), side)
    flux = from_all(near, ("y", "rad"))
    source, sup, sdown, srup, srdown, height = pl.pallas_call(
        front_kernel,
        out_shape=(plane(T), plane(H - 1), plane(H - 1), tile(T), tile(T), shape(BS, NB)),
        in_specs=[SM, SM, SM] + [VM] * 8 + [ANY] * 6, out_specs=(ANY,) * 5 + (VM,),
        scratch_shapes=[pltpu.VMEM((GROUPS, FROWS, NB), F32),
                        pltpu.VMEM((GROUPS, BS, NB), F32), pltpu.VMEM((GROUPS, BS, NB), F32),
                        pltpu.VMEM((GROUPS, SLOTS, 128), F32), pltpu.VMEM((GROUPS * BS, NB), F32),
                        block, pltpu.VMEM((R * 8, 128), F32), pltpu.VMEM((128, 128), F32),
                        pltpu.SemaphoreType.DMA((6,)), pltpu.SemaphoreType.DMA((GROUPS, T))]
        + [pltpu.VMEM((T * R * 8, 128), F32)] * GROUPS,
        compiler_params=params(20), cost_estimate=cost(10), name="front",
    )(kidx, tally, row, flux, *fronts, lane, vertex, share, outflow, lo, hi, side, clo, chi)
    slo, shi = shift_azim(sup, 1), shift_azim(sdown, -1)
    sside = ring_tile(shift_rad(srdown, -1), shift_rad(srup, 1))
    sclo, schi = shift_azim(sside[T - H + 1:], 1), shift_azim(sside[:H - 1], -1)
    ext = pltpu.VMEM((TE, RE, Z), F32)
    pressure = pl.pallas_call(
        sweep_kernel, out_shape=plane(T),
        in_specs=[SM] + [ANY] * 13, out_specs=VM,
        scratch_shapes=[ext] * 8 + [pltpu.VMEM((3, RT, 8, 128), F32), pltpu.SemaphoreType.DMA((4, 3, 2))],
        compiler_params=params(46), cost_estimate=cost(20), name="sweeps",
    )(kidx, load, beta, lo, hi, side, clo, chi, source, slo, shi, sside, sclo, schi)
    return pressure, height.reshape(NB * BS)


def solution(mesh):
    fine = jax.sharding.Mesh(mesh.devices.reshape(4, 4, 2, 4), AZIM + ("rad",))
    cells = P(AZIM, "rad", None)
    slots = P(AZIM, "rad", None, None)
    return jax.shard_map(
        per_device,
        mesh=fine,
        in_specs=(cells, cells, cells, cells, slots, slots, slots, cells,
                  P("rad"), P("rad"), P("rad"), P(None, None, "rad")),
        out_specs=(cells, P("rad")),
        check_vma=False,
    )
```

```python
import functools
import math

import jax
import jax.numpy as jnp
from jax import lax
from jax.experimental import pallas as pl
from jax.experimental.pallas import tpu as pltpu
from jax.sharding import PartitionSpec as P

SWEEPS = 4
ITERS = 4
OMEGA = 0.9
AXIAL = 0.25
STEFAN = 1.0
SHRINK = 0.3
COUPLE = 0.2

F32 = jnp.float32
I32 = jnp.int32
BF16 = jnp.bfloat16

T, R, Z = 8, 64, 1024
H = 4
TE = T + 2 * H
RE = R + 8
RT = RE // 8
GROUPS, SLOTS, NB, BS = 4, 1024, 128, 16
FT = 5
UNROLL = 16
AZIM = ("y", "z", "core")


def iota(shape, dim):
    return lax.broadcasted_iota(I32, shape, dim)


def pieces(x):
    h = x.astype(BF16)
    rest = x - h.astype(F32)
    m = rest.astype(BF16)
    return h, m, (rest - m.astype(F32)).astype(BF16)


def at8(i):
    return pl.ds(pl.multiple_of(i * 8, 8), 8)


def flux_kernel(cnt, row, heat_any, lane, vert, share, out, heat, diff, picked, sems):
    loads = [pltpu.make_async_copy(heat_any.at[t], heat.at[t], sems.at[t]) for t in range(T)]
    for c in loads:
        c.start()

    for t in range(T):
        loads[t].wait()

        def make(q, _):
            x = heat[t, at8(q), :]
            d = pltpu.roll(x, Z - 1, 1) - x
            for zc in range(8):
                diff[at8((t * 8 + q) * 8 + zc), :] = d[:, zc * 128:(zc + 1) * 128]
            return 0

        lax.fori_loop(0, R // 8, make, 0, unroll=4)
    for j in range(GROUPS):
        def body(b, _):
            base = pl.multiple_of(b * UNROLL, UNROLL)
            for u in range(UNROLL):
                picked[pl.ds(base + u, 1), :] = diff[pl.ds(row[j, base + u], 1), :]
            return 0

        lax.fori_loop(0, (cnt[j] + UNROLL - 1) // UNROLL, body, 0)
        vals = []
        for kb in range(SLOTS // 128):
            cut = slice(kb * 128, (kb + 1) * 128)
            hit = iota((128, 128), 0) == lane[j:j + 1, cut]
            vals.append(jnp.sum(jnp.where(hit, picked[cut, :].T, 0.0), axis=0, keepdims=True))
        live = iota((1, SLOTS), 1) < cnt[j]
        val = jnp.where(live, share[j:j + 1, :] * jnp.concatenate(vals, axis=1), 0.0)
        v = vert[j:j + 1, :]
        inner = iota((BS, SLOTS), 0) == (v & (BS - 1))
        left = jnp.concatenate(
            [jnp.where(inner, p.astype(F32), 0.0).astype(BF16) for p in pieces(val)], axis=0)
        right = jnp.where(iota((NB, SLOTS), 0) == (v >> 4), 1.0, 0.0).astype(BF16)
        o = lax.dot_general(left, right, (((1,), (1,)), ((), ())), preferred_element_type=F32)
        o = o[:BS] + o[BS:2 * BS] + o[2 * BS:]
        for n in range(out.shape[0]):
            out[n, j * BS:(j + 1) * BS, :] = o


def front_kernel(kref, cnt, row, parts, f0, f1, f2, f3, lane, vert, share, pred_any, *refs):
    front_body(kref, cnt, row, parts, (f0, f1, f2, f3), lane, vert, share, pred_any, *refs[5:])


def front_body(kref, cnt, row, parts, fronts, lane, vert, share, pred_any, src_any, sup, sdown, srup, srdown,
               hout, front, gtab, height, terms, flux, pred, zeros, flip, sems, zsems, fsems, *acc):
    k = kref[0]
    load = pltpu.make_async_copy(pred_any, pred, sems.at[0])
    load.start()
    own, above, below, across = fronts
    copies = [(own, 0), (above.at[pl.ds(2 * T, FT)], 1), (across, 2), (below.at[pl.ds(2 * T, FT)], 3)]
    copies = [pltpu.make_async_copy(f, front.at[lax.rem(k + n, GROUPS)], fsems.at[n]) for f, n in copies]
    for c in copies:
        c.start()
    zeros[...] = jnp.zeros(zeros.shape, F32)
    count = zeros.shape[0]
    clears = [pltpu.make_async_copy(zeros, a.at[pl.ds(n * count, count)], zsems.at[m, n])
              for m, a in enumerate(acc) for n in range(T * R * 8 // count)]
    for c in clears:
        c.start()
    sums = parts[0]
    for n in range(1, parts.shape[0]):
        sums = sums + parts[n]
    flux[...] = sums
    for c in copies:
        c.wait()

    def held(g, n):
        return jnp.concatenate([front[g, m // 8, :, m % 8 * 128:m % 8 * 128 + 128]
                                for m in (2 * n, 2 * n + 1)], axis=0)

    def neighbours(h):
        last = jnp.concatenate([h[g][BS - 1:BS, :] for g in range(GROUPS)], axis=0)
        first = jnp.concatenate([h[g][0:1, :] for g in range(GROUPS)], axis=0)
        zrow = jnp.zeros((1, 128), F32)
        lr = pltpu.roll(last, 1, 1)
        fr = pltpu.roll(first, 127, 1)
        col = iota((GROUPS, 128), 1)
        lr = jnp.where(col == 0, jnp.concatenate([zrow, lr[:-1]], axis=0), lr)
        fr = jnp.where(col == 127, jnp.concatenate([fr[1:], zrow], axis=0), fr)
        down = [jnp.concatenate([lr[g:g + 1], h[g][:BS - 1]], axis=0) for g in range(GROUPS)]
        up = [jnp.concatenate([h[g][1:], fr[g:g + 1]], axis=0) for g in range(GROUPS)]
        return down, up

    prior = [held(g, BS) for g in range(GROUPS)]
    h = list(prior)
    for _ in range(ITERS):
        down, up = neighbours(h)
        for g in range(GROUPS):
            applied = (2.0 + held(g, BS + 1)) * h[g] - down[g] - up[g]
            res = held(g, BS + 2) + COUPLE * flux[g * BS:(g + 1) * BS, :] - applied
            h[g] = h[g] + jnp.concatenate(
                [jnp.sum(held(g, i) * res, axis=0, keepdims=True) for i in range(BS)], axis=0)
    down, up = neighbours(h)
    for g in range(GROUPS):
        slope = up[g] - down[g]
        growth = h[g] - prior[g]
        height[g] = h[g]
        gtab[g] = (flux[g * BS:(g + 1) * BS, :] - STEFAN * growth) * jnp.sqrt(1.0 + slope * slope)
    for j in range(GROUPS):
        v = vert[j:j + 1, :]
        right = jnp.where(iota((NB, SLOTS), 0) == (v >> 4), 1.0, 0.0).astype(BF16)
        x = jnp.dot(jnp.concatenate(pieces(gtab[j]), axis=0), right, preferred_element_type=F32)
        x = x[:BS] + x[BS:2 * BS] + x[2 * BS:]
        inner = iota((BS, SLOTS), 0) == (v & (BS - 1))
        term = jnp.sum(jnp.where(inner, x, 0.0), axis=0, keepdims=True) * share[j:j + 1, :]
        term = jnp.where(iota((1, SLOTS), 1) < cnt[j], term, 0.0)
        for kb in range(SLOTS // 128):
            cut = slice(kb * 128, (kb + 1) * 128)
            hit = iota((128, 128), 0) == lane[j:j + 1, cut]
            terms[j, cut, :] = jnp.where(hit, term[:, cut], 0.0).T
    for c in clears:
        c.wait()
    most = jnp.maximum(jnp.maximum(cnt[0], cnt[1]), jnp.maximum(cnt[2], cnt[3]))

    def add(b, _):
        for u in range(UNROLL):
            s = b * UNROLL + u
            for j in range(GROUPS):
                at = pl.ds(row[j, s], 1)
                acc[j][at, :] = acc[j][at, :] + terms[j, pl.ds(s, 1), :]
        return 0

    lax.fori_loop(0, (most + UNROLL - 1) // UNROLL, add, 0)

    load.wait()
    src = pred
    sends = []

    def send(m, a, b):
        sends.append(pltpu.make_async_copy(a, b, sems.at[m]))
        sends[-1].start()

    for d in range(T):
        def finish(q, _):
            for zc in range(8):
                a = at8((d * 8 + q) * 8 + zc)
                s = (acc[0][a, :] + acc[1][a, :]) + (acc[2][a, :] + acc[3][a, :])
                cut = slice(zc * 128, (zc + 1) * 128)
                src[d, at8(q), cut] = pred[d, at8(q), cut] + SHRINK * s
            return 0

        lax.fori_loop(0, R // 8, finish, 0, unroll=2)
        if d == H - 2:
            send(1, src.at[pl.ds(0, H - 1)], sdown)
    send(2, src.at[pl.ds(T - H + 1, H - 1)], sup)
    send(3, src.at[:, pl.ds(R - 8, 8)], srup)
    send(4, src.at[:, pl.ds(0, 8)], srdown)
    send(5, src, src_any)
    flip[...] = jnp.concatenate([height[k], jnp.zeros((128 - BS, 128), F32)], axis=0).T
    nodes = flip[pl.ds(0, BS, stride=8), :]
    for m in range(1, 8):
        nodes = nodes + pltpu.roll(flip[pl.ds(m, BS, stride=8), :], m * BS, 1)
    hout[...] = nodes
    for c in sends:
        c.wait()


def pack_kernel(load_any, beta_any, solve, prior, weight, jump, label, up, down, rup, rdown,
                front_any, row, lane, load, beta, front, flip, isems, osems, fsems):
    loads = [pltpu.make_async_copy(a, b, isems.at[n])
             for n, (a, b) in enumerate(((load_any, load), (beta_any, beta)))]
    for c in loads:
        c.start()
    lab = label[...]
    hi = lab >> 10
    low = hi + (lab & 1023)
    carry = (low >= Z - 1).astype(I32)
    column, axial = hi + carry, low - (Z - 1) * carry
    row[...] = ((column >> 3) << 6) + ((axial >> 7) << 3) + (column & 7)
    lane[...] = axial & 127


    def keep(n, x):
        front[n // 8, :, n % 8 * 128:n % 8 * 128 + 128] = x

    for n in range(FT * 8):
        keep(n, solve[n * 8:n * 8 + 8, :] if n < BS * BS // 8 else jnp.zeros((8, 128), F32))
    for n, x in enumerate((prior, weight, jump)):
        for m in range(8):
            flip[pl.ds(m, BS, stride=8), :] = pltpu.roll(x[...], (128 - m * BS) % 128, 1)
        turned = flip[...].T
        keep(BS * BS // 8 + 2 * n, turned[:8, :])
        keep(BS * BS // 8 + 2 * n + 1, turned[8:16, :])
    sends = []
    fcopies = [pltpu.make_async_copy(front, b, fsems.at[n]) for n, b in enumerate(
        (front_any, rup.at[pl.ds(2 * T, FT)], rdown.at[pl.ds(2 * T, FT)]))]
    for c in fcopies:
        c.start()
    for n, f in enumerate((load, beta)):
        loads[n].wait()
        for a, b in ((f.at[pl.ds(T - H, H)], up.at[pl.ds(n * H, H)]),
                     (f.at[pl.ds(0, H)], down.at[pl.ds(n * H, H)]),
                     (f.at[:, pl.ds(R - 8, 8)], rup.at[pl.ds(n * T, T)]),
                     (f.at[:, pl.ds(0, 8)], rdown.at[pl.ds(n * T, T)])):
            sends.append(pltpu.make_async_copy(a, b, osems.at[len(sends)]))
            sends[-1].start()
    for c in sends + fcopies:
        c.wait()


def side_kernel(kref, above, below_any, side, eup, edown, below, sems):
    loads = [pltpu.make_async_copy(above.at[pl.ds(0, 2 * T)], side, sems.at[0]),
             pltpu.make_async_copy(below_any.at[pl.ds(0, 2 * T)], below, sems.at[1])]
    for c in loads:
        c.start()
    for c in loads:
        c.wait()
    k = kref[0]
    sub = iota((8, Z), 0)
    first = (sub < 4) & (k < GROUPS - 1)
    second = (sub >= 4) & (k > 0)
    for t in range(2 * T):
        side[t] = jnp.where(first, side[t], jnp.where(second, below[t], 0.0))
    for n in range(2):
        eup[n * H:(n + 1) * H] = side[n * T + T - H:n * T + T]
        edown[n * H:(n + 1) * H] = side[n * T:n * T + H]


def shift_azim(x, d):
    return lax.ppermute(x, AZIM, [(i, (i + d) % 32) for i in range(32)])


def shift_rad(x, d):
    return lax.ppermute(x, "rad", [(i, i + d) for i in range(4) if 0 <= i + d < 4])


def ring_tile(from_above, from_below):
    return jnp.where(iota(from_above.shape, 1) < 4, from_above, from_below)


def wide(x):
    return jnp.concatenate([x] * (Z // 128), axis=1)


def sweep_kernel(kref, load, beta_in, lo, hi, side, clo, chi, src, slo, shi, sside, sclo, schi,
                 out, pa, pb, beta, th, rr, zz, ww, ss, rads, sems):
    k = kref[0]
    rows, ring = pl.ds(0, R), pl.ds(R, 8)
    half = T // 2

    def planes(own, tile_own, low, tile_low, high, tile_high, first):
        return [(low, tile_low, first, H - first), (own.at[pl.ds(0, half)], tile_own.at[pl.ds(0, half)], H, half),
                (own.at[pl.ds(half, half)], tile_own.at[pl.ds(half, half)], H + half, half),
                (high, tile_high, H + T, H - first)]

    def both(x, n, count):
        return x.at[pl.ds(n * count, count)]

    fields = [(ref, planes(own, both(side, n, T), both(lo, n, H), both(clo, n, H), both(hi, n, H), both(chi, n, H), 0))
              for ref, own, n in ((beta, beta_in, 1), (pa, load, 0))]
    fields.append((ss, planes(src, sside, slo, sclo, shi, schi, 1)))
    waits = []
    for g in range(4):
        cs = []
        for f, (ref, parts) in enumerate(fields):
            main, tile, first, count = parts[g]
            cs.append(pltpu.make_async_copy(main, ref.at[pl.ds(first, count), rows], sems.at[g, f, 0]))
            cs.append(pltpu.make_async_copy(tile, ref.at[pl.ds(first, count), ring], sems.at[g, f, 1]))
        waits.append(cs)

    def begin(g):
        for c in waits[g] if g < 4 else ():
            c.start()

    begin(0)
    begin(1)
    sub, lanes = iota((8, 128), 0), iota((8, 128), 1)
    top, bottom, last_lane, first_lane = sub == 7, sub == 0, lanes == 127, lanes == 0
    angular = (256 / (2.0 * math.pi)) ** 2
    for it in range(RT):
        gi = k * R + (it * 8 + sub if it < RT - 1 else jnp.where(sub < 4, R + sub, sub - 8))
        ra = 0.25 * 256 + gi.astype(F32) + 0.5
        rads[0, it] = ra
        rads[1, it] = (0.5 * angular) / ra
        rads[2, it] = jnp.where((gi >= 0) & (gi < 255), 0.5 * (ra + 0.5), 0.0)
    nothing = jnp.zeros((8, 128), F32)
    columns = range(Z // 128)

    def cut(it):
        it = it % RT
        return slice(it * 8, it * 8 + 8)

    def vec(ref, t, it, v):
        return ref[t, cut(it), v * 128:v * 128 + 128]

    def put(ref, t, it, v, x):
        ref[t, cut(it), v * 128:v * 128 + 128] = x

    def up_row(x):
        return pltpu.roll(x, 7, 0)

    def down_row(x):
        return pltpu.roll(x, 1, 0)

    def next_lane(ref, t, it, v, cur):
        nxt = pltpu.roll(vec(ref, t, it, v + 1), 127, 1) if v + 1 < Z // 128 else cur
        return jnp.where(last_lane, nxt, cur), nxt

    def relaxed(old, t, it, v, p, pz, pu, prev, zprev, tu, td, r, z, w, s):
        acc = (tu * vec(old, t + 1, it, v) + td * vec(old, t - 1, it, v)) + r * pu
        rp = down_row(r * p)
        acc = acc + jnp.where(bottom, prev, rp)
        zu, pz = next_lane(old, t, it, v, pz)
        zp = pltpu.roll(z * p, 1, 1)
        acc = acc + (z * zu + jnp.where(first_lane, zprev, zp))
        return (1.0 - OMEGA) * p + w * (acc - s), pz, rp, zp

    def first_sweep(t, _):
        last = RT - 1
        bup = [up_row(vec(beta, t, 0, v)) for v in columns]
        pup = [up_row(vec(pa, t, 0, v)) for v in columns]
        fprev, prev = [], []
        for v in columns:
            b = vec(beta, t, last, v)
            face = (b + jnp.where(top, bup[v], up_row(b))) * rads[2, last]
            fprev.append(down_row(face))
            prev.append(down_row(face * vec(pa, t, last, v)))
        for it in range(RT):
            ra, ang, rad = rads[0, it], rads[1, it], rads[2, it]
            axi = (0.5 * AXIAL) * ra
            bz = pltpu.roll(vec(beta, t, it, 0), 127, 1)
            pz = pltpu.roll(vec(pa, t, it, 0), 127, 1)
            zfprev = zprev = nothing
            for v in columns:
                b, p = vec(beta, t, it, v), vec(pa, t, it, v)
                nb, np_ = up_row(vec(beta, t, it + 1, v)), up_row(vec(pa, t, it + 1, v))
                tu = (b + vec(beta, t + 1, it, v)) * ang
                td = vec(th, t - 1, it, v)
                r = (b + jnp.where(top, nb, bup[v])) * rad
                froll = down_row(r)
                other = jnp.where(bottom, fprev[v], froll)
                bu, bz = next_lane(beta, t, it, v, bz)
                zf = (b + bu) * axi
                z = zf
                if v == Z // 128 - 1:
                    zf = jnp.where(last_lane, 2.0 * (b * axi), zf)
                    z = jnp.where(last_lane, 0.0, zf)
                zr = pltpu.roll(z, 1, 1)
                d = (tu + td) + (r + other) + (zf + jnp.where(first_lane, zfprev, zr))
                if it == last:
                    d = jnp.where(d > 0.0, d, 1.0)
                w = pl.reciprocal(d, approx=True)
                w = w * (2.0 - d * w)
                w = (w * (2.0 - d * w)) * OMEGA
                sc = vec(ss, t, it, v) * ra
                put(th, t, it, v, tu)
                put(rr, t, it, v, r)
                put(zz, t, it, v, z)
                put(ww, t, it, v, w)
                put(ss, t, it, v, sc)
                pu = jnp.where(top, np_, pup[v])
                new, pz, prev[v], zprev = relaxed(pa, t, it, v, p, pz, pu, prev[v], zprev, tu, td, r, z, w, sc)
                put(pb, t, it, v, new)
                bup[v], pup[v], fprev[v], zfprev = nb, np_, froll, zr
        return 0

    def sweep(old, new, t, tiles, shift):
        pup = [up_row(vec(old, t, 0, v)) for v in columns]
        prev = [down_row(vec(rr, t, -1, v) * vec(old, t, -1, v)) for v in columns]
        for it in range(tiles):
            pz = pltpu.roll(vec(old, t, it, 0), 127, 1)
            zprev = nothing
            for v in columns:
                p = vec(old, t, it, v)
                np_ = up_row(vec(old, t, it + 1, v))
                pu = jnp.where(top, np_, pup[v])
                x, pz, prev[v], zprev = relaxed(
                    old, t, it, v, p, pz, pu, prev[v], zprev, vec(th, t, it, v), vec(th, t - 1, it, v),
                    vec(rr, t, it, v), vec(zz, t, it, v), vec(ww, t, it, v), vec(ss, t, it, v))
                put(new, t - shift, it, v, x)
                pup[v] = np_
        return 0

    ends = (H - 1, H + half - 1, H + T - 1, TE - 1)
    start = 1
    for g in range(4):
        for c in waits[g]:
            c.wait()
        begin(g + 2)
        if g == 0:
            for it in range(RT):
                th[0, cut(it), :] = (beta[0, cut(it), :] + beta[1, cut(it), :]) * wide(rads[1, it])
        lax.fori_loop(start, ends[g], first_sweep, 0)
        start = ends[g]
    lax.fori_loop(2, TE - 2, lambda t, _: sweep(pb, pa, t, RT, 0), 0)
    lax.fori_loop(3, TE - 3, lambda t, _: sweep(pa, pb, t, RT, 0), 0)
    lax.fori_loop(4, TE - 4, lambda t, _: sweep(pb, out, t, RT - 1, H), 0)


def from_all(copies, axes):
    return lax.all_to_all(copies, axes, 0, 0)


def sum_kernel(parts, *refs):
    out = refs[-1]
    s = parts[0]
    for n in range(1, parts.shape[0]):
        s = s + parts[n]
    for n in range(out.shape[0]):
        out[n] = s


VM = pl.BlockSpec(memory_space=pltpu.VMEM)
SM = pl.BlockSpec(memory_space=pltpu.SMEM)
ANY = pl.BlockSpec(memory_space=pltpu.HBM)


def params(mib):
    return pltpu.CompilerParams(vmem_limit_bytes=62 << 20)


def cost(us):
    return pl.CostEstimate(flops=1000, bytes_accessed=us * 3000000, transcendentals=0)


def per_device(load, outflow, beta, heat, label, vertex, share, tally, prior, weight, jump, solve):
    label = label.reshape(GROUPS, SLOTS)
    vertex = vertex.reshape(GROUPS, SLOTS)
    share = share.reshape(GROUPS, SLOTS)
    tally = tally.reshape(GROUPS)
    kidx = lax.axis_index("rad").astype(I32).reshape(1)
    nodes = lambda v: v.reshape(BS, NB)

    shape = lambda *d: jax.ShapeDtypeStruct(d, F32)
    slot = jax.ShapeDtypeStruct((GROUPS, SLOTS), I32)
    plane = lambda n: shape(n, R, Z)
    tile = lambda n: shape(n, 8, Z)
    block = pltpu.VMEM((T, R, Z), F32)
    up, down, rup, rdown, front, row, lane = pl.pallas_call(
        pack_kernel,
        out_shape=(plane(2 * H), plane(2 * H), tile(2 * T + FT), tile(2 * T + FT), tile(FT), slot, slot),
        in_specs=[ANY] * 2 + [VM] * 5, out_specs=(ANY,) * 5 + (VM,) * 2,
        scratch_shapes=[block, block, pltpu.VMEM((FT, 8, Z), F32), pltpu.VMEM((128, 128), F32),
                        pltpu.SemaphoreType.DMA((2,)), pltpu.SemaphoreType.DMA((8,)), pltpu.SemaphoreType.DMA((3,))],
        compiler_params=params(10), cost_estimate=cost(4), name="pack",
    )(load, beta, solve.reshape(BS * BS, NB), nodes(prior), nodes(weight), nodes(jump), label)
    lo, hi = shift_azim(up, 1), shift_azim(down, -1)
    ring = lambda x, d: lax.ppermute(x, "rad", [(i, (i + d) % 4) for i in range(4)])
    rhi, rlo, across = ring(rdown, -1), ring(rup, 1), ring(front, 2)

    partial = pl.pallas_call(
        flux_kernel, out_shape=shape(8, GROUPS * BS, NB),
        in_specs=[SM, SM, ANY, VM, VM, VM], out_specs=VM,
        scratch_shapes=[block, pltpu.VMEM((T * R * 8, 128), F32), pltpu.VMEM((SLOTS, 128), F32),
                        pltpu.SemaphoreType.DMA((T,))],
        compiler_params=params(12), cost_estimate=cost(10), name="flux",
    )(tally, row, heat, lane, vertex, share)
    side, eup, edown = pl.pallas_call(
        side_kernel, out_shape=(tile(2 * T), tile(2 * H), tile(2 * H)),
        in_specs=[SM, ANY, ANY], out_specs=(VM,) * 3,
        scratch_shapes=[pltpu.VMEM((2 * T, 8, Z), F32), pltpu.SemaphoreType.DMA((2,))],
        compiler_params=params(4), cost_estimate=cost(2), name="side",
    )(kidx, rhi, rlo)
    clo, chi = shift_azim(eup, 1), shift_azim(edown, -1)
    near = pl.pallas_call(
        sum_kernel, out_shape=shape(16, GROUPS * BS, NB),
        in_specs=[VM, ANY, ANY], out_specs=VM, compiler_params=params(4), name="near",
    )(from_all(partial, ("z", "core")), side, across)
    flux = from_all(near, ("y", "rad"))
    source, sup, sdown, srup, srdown, height = pl.pallas_call(
        front_kernel,
        out_shape=(plane(T), plane(H - 1), plane(H - 1), tile(T), tile(T), shape(BS, NB)),
        in_specs=[SM, SM, SM, VM] + [ANY] * 4 + [VM] * 3 + [ANY] * 6, out_specs=(ANY,) * 5 + (VM,),
        scratch_shapes=[pltpu.VMEM((GROUPS, FT, 8, Z), F32),
                        pltpu.VMEM((GROUPS, BS, NB), F32), pltpu.VMEM((GROUPS, BS, NB), F32),
                        pltpu.VMEM((GROUPS, SLOTS, 128), F32), pltpu.VMEM((GROUPS * BS, NB), F32),
                        block, pltpu.VMEM((R * 8, 128), F32), pltpu.VMEM((128, 128), F32),
                        pltpu.SemaphoreType.DMA((6,)), pltpu.SemaphoreType.DMA((GROUPS, T)),
                        pltpu.SemaphoreType.DMA((GROUPS,))]
        + [pltpu.VMEM((T * R * 8, 128), F32)] * GROUPS,
        compiler_params=params(20), cost_estimate=cost(10), name="front",
    )(kidx, tally, row, flux, front, rhi, rlo, across, lane, vertex, share, outflow, lo, hi, side, clo, chi)
    slo, shi = shift_azim(sup, 1), shift_azim(sdown, -1)
    sside = ring_tile(shift_rad(srdown, -1), shift_rad(srup, 1))
    sclo, schi = shift_azim(sside[T - H + 1:], 1), shift_azim(sside[:H - 1], -1)
    ext = pltpu.VMEM((TE, RE, Z), F32)
    pressure = pl.pallas_call(
        sweep_kernel, out_shape=plane(T),
        in_specs=[SM] + [ANY] * 13, out_specs=VM,
        scratch_shapes=[ext] * 8 + [pltpu.VMEM((3, RT, 8, 128), F32), pltpu.SemaphoreType.DMA((4, 3, 2))],
        compiler_params=params(46), cost_estimate=cost(20), name="sweeps",
    )(kidx, load, beta, lo, hi, side, clo, chi, source, slo, shi, sside, sclo, schi)
    return pressure, height.reshape(NB * BS)


def solution(mesh):
    fine = jax.sharding.Mesh(mesh.devices.reshape(4, 4, 2, 4), AZIM + ("rad",))
    cells = P(AZIM, "rad", None)
    slots = P(AZIM, "rad", None, None)
    return jax.shard_map(
        per_device,
        mesh=fine,
        in_specs=(cells, cells, cells, cells, slots, slots, slots, cells,
                  P("rad"), P("rad"), P("rad"), P(None, None, "rad")),
        out_specs=(cells, P("rad")),
        check_vma=False,
    )
```

```python
import functools
import math

import jax
import jax.numpy as jnp
from jax import lax
from jax.experimental import pallas as pl
from jax.experimental.pallas import tpu as pltpu
from jax.sharding import PartitionSpec as P

SWEEPS = 4
ITERS = 4
OMEGA = 0.9
AXIAL = 0.25
STEFAN = 1.0
SHRINK = 0.3
COUPLE = 0.2

F32 = jnp.float32
I32 = jnp.int32
BF16 = jnp.bfloat16

T, R, Z = 8, 64, 1024
H = 4
TE = T + 2 * H
RE = R + 8
RT = RE // 8
GROUPS, SLOTS, NB, BS = 4, 1024, 128, 16
FT = 5
UNROLL = 16
AZIM = ("y", "z", "core")


def iota(shape, dim):
    return lax.broadcasted_iota(I32, shape, dim)


def pieces(x):
    h = x.astype(BF16)
    rest = x - h.astype(F32)
    m = rest.astype(BF16)
    return h, m, (rest - m.astype(F32)).astype(BF16)


def at8(i):
    return pl.ds(pl.multiple_of(i * 8, 8), 8)


def flux_kernel(cnt, row, heat_any, lane, vert, share, out, heat, diff, picked, sems):
    loads = [pltpu.make_async_copy(heat_any.at[t], heat.at[t], sems.at[t]) for t in range(T)]
    for c in loads:
        c.start()

    for t in range(T):
        loads[t].wait()

        def make(q, _):
            x = heat[t, at8(q), :]
            d = pltpu.roll(x, Z - 1, 1) - x
            for zc in range(8):
                diff[at8((t * 8 + q) * 8 + zc), :] = d[:, zc * 128:(zc + 1) * 128]
            return 0

        lax.fori_loop(0, R // 8, make, 0, unroll=4)
    for j in range(GROUPS):
        def body(b, _):
            base = pl.multiple_of(b * UNROLL, UNROLL)
            for u in range(UNROLL):
                picked[pl.ds(base + u, 1), :] = diff[pl.ds(row[j, base + u], 1), :]
            return 0

        lax.fori_loop(0, (cnt[j] + UNROLL - 1) // UNROLL, body, 0)
        vals = []
        for kb in range(SLOTS // 128):
            cut = slice(kb * 128, (kb + 1) * 128)
            hit = iota((128, 128), 0) == lane[j:j + 1, cut]
            vals.append(jnp.sum(jnp.where(hit, picked[cut, :].T, 0.0), axis=0, keepdims=True))
        live = iota((1, SLOTS), 1) < cnt[j]
        val = jnp.where(live, share[j:j + 1, :] * jnp.concatenate(vals, axis=1), 0.0)
        v = vert[j:j + 1, :]
        inner = iota((BS, SLOTS), 0) == (v & (BS - 1))
        left = jnp.concatenate(
            [jnp.where(inner, p.astype(F32), 0.0).astype(BF16) for p in pieces(val)], axis=0)
        right = jnp.where(iota((NB, SLOTS), 0) == (v >> 4), 1.0, 0.0).astype(BF16)
        o = lax.dot_general(left, right, (((1,), (1,)), ((), ())), preferred_element_type=F32)
        o = o[:BS] + o[BS:2 * BS] + o[2 * BS:]
        for n in range(out.shape[0]):
            out[n, j * BS:(j + 1) * BS, :] = o


def front_kernel(kref, cnt, row, parts, f0, f1, f2, f3, lane, vert, share, pred_any, *refs):
    front_body(kref, cnt, row, parts, (f0, f1, f2, f3), lane, vert, share, pred_any, *refs[6:])


def front_body(kref, cnt, row, parts, fronts, lane, vert, share, pred_any, src_any, sup, sdown, srup, srdown,
               hout, front, gtab, height, terms, flux, pred, zeros, flip, sems, zsems, fsems, *acc):
    k = kref[0]
    load = pltpu.make_async_copy(pred_any, pred, sems.at[0])
    load.start()
    own, above, below, across = fronts
    copies = [(own, 0), (above.at[pl.ds(2 * T, FT)], 1), (across, 2), (below.at[pl.ds(2 * T, FT)], 3)]
    copies = [pltpu.make_async_copy(f, front.at[lax.rem(k + n, GROUPS)], fsems.at[n]) for f, n in copies]
    for c in copies:
        c.start()
    zeros[...] = jnp.zeros(zeros.shape, F32)
    count = zeros.shape[0]
    clears = [pltpu.make_async_copy(zeros, a.at[pl.ds(n * count, count)], zsems.at[m, n])
              for m, a in enumerate(acc) for n in range(T * R * 8 // count)]
    for c in clears:
        c.start()
    sums = parts[0]
    for n in range(1, parts.shape[0]):
        sums = sums + parts[n]
    flux[...] = sums
    for c in copies:
        c.wait()

    def held(g, n):
        return jnp.concatenate([front[g, m // 8, :, m % 8 * 128:m % 8 * 128 + 128]
                                for m in (2 * n, 2 * n + 1)], axis=0)

    def neighbours(h):
        last = jnp.concatenate([h[g][BS - 1:BS, :] for g in range(GROUPS)], axis=0)
        first = jnp.concatenate([h[g][0:1, :] for g in range(GROUPS)], axis=0)
        zrow = jnp.zeros((1, 128), F32)
        lr = pltpu.roll(last, 1, 1)
        fr = pltpu.roll(first, 127, 1)
        col = iota((GROUPS, 128), 1)
        lr = jnp.where(col == 0, jnp.concatenate([zrow, lr[:-1]], axis=0), lr)
        fr = jnp.where(col == 127, jnp.concatenate([fr[1:], zrow], axis=0), fr)
        down = [jnp.concatenate([lr[g:g + 1], h[g][:BS - 1]], axis=0) for g in range(GROUPS)]
        up = [jnp.concatenate([h[g][1:], fr[g:g + 1]], axis=0) for g in range(GROUPS)]
        return down, up

    prior = [held(g, BS) for g in range(GROUPS)]
    h = list(prior)
    for _ in range(ITERS):
        down, up = neighbours(h)
        for g in range(GROUPS):
            applied = (2.0 + held(g, BS + 1)) * h[g] - down[g] - up[g]
            res = held(g, BS + 2) + COUPLE * flux[g * BS:(g + 1) * BS, :] - applied
            h[g] = h[g] + jnp.concatenate(
                [jnp.sum(held(g, i) * res, axis=0, keepdims=True) for i in range(BS)], axis=0)
    down, up = neighbours(h)
    for g in range(GROUPS):
        slope = up[g] - down[g]
        growth = h[g] - prior[g]
        height[g] = h[g]
        gtab[g] = (flux[g * BS:(g + 1) * BS, :] - STEFAN * growth) * jnp.sqrt(1.0 + slope * slope)
    for j in range(GROUPS):
        v = vert[j:j + 1, :]
        right = jnp.where(iota((NB, SLOTS), 0) == (v >> 4), 1.0, 0.0).astype(BF16)
        x = jnp.dot(jnp.concatenate(pieces(gtab[j]), axis=0), right, preferred_element_type=F32)
        x = x[:BS] + x[BS:2 * BS] + x[2 * BS:]
        inner = iota((BS, SLOTS), 0) == (v & (BS - 1))
        term = jnp.sum(jnp.where(inner, x, 0.0), axis=0, keepdims=True) * share[j:j + 1, :]
        term = jnp.where(iota((1, SLOTS), 1) < cnt[j], term, 0.0)
        for kb in range(SLOTS // 128):
            cut = slice(kb * 128, (kb + 1) * 128)
            hit = iota((128, 128), 0) == lane[j:j + 1, cut]
            terms[j, cut, :] = jnp.where(hit, term[:, cut], 0.0).T
    for c in clears:
        c.wait()
    most = jnp.maximum(jnp.maximum(cnt[0], cnt[1]), jnp.maximum(cnt[2], cnt[3]))

    def add(b, _):
        for u in range(UNROLL):
            s = b * UNROLL + u
            for j in range(GROUPS):
                at = pl.ds(row[j, s], 1)
                acc[j][at, :] = acc[j][at, :] + terms[j, pl.ds(s, 1), :]
        return 0

    lax.fori_loop(0, (most + UNROLL - 1) // UNROLL, add, 0)

    load.wait()
    src = pred
    sends = []

    def send(m, a, b):
        sends.append(pltpu.make_async_copy(a, b, sems.at[m]))
        sends[-1].start()

    for d in range(T):
        def finish(q, _):
            for zc in range(8):
                a = at8((d * 8 + q) * 8 + zc)
                s = (acc[0][a, :] + acc[1][a, :]) + (acc[2][a, :] + acc[3][a, :])
                cut = slice(zc * 128, (zc + 1) * 128)
                src[d, at8(q), cut] = pred[d, at8(q), cut] + SHRINK * s
            return 0

        lax.fori_loop(0, R // 8, finish, 0, unroll=2)
        if d == H - 2:
            send(1, src.at[pl.ds(0, H - 1)], sdown)
    send(2, src.at[pl.ds(T - H + 1, H - 1)], sup)
    send(3, src.at[:, pl.ds(R - 8, 8)], srup)
    send(4, src.at[:, pl.ds(0, 8)], srdown)
    send(5, src, src_any)
    flip[...] = jnp.concatenate([height[k], jnp.zeros((128 - BS, 128), F32)], axis=0).T
    nodes = flip[pl.ds(0, BS, stride=8), :]
    for m in range(1, 8):
        nodes = nodes + pltpu.roll(flip[pl.ds(m, BS, stride=8), :], m * BS, 1)
    hout[...] = nodes
    for c in sends:
        c.wait()


def pack_kernel(load_any, beta_any, solve, prior, weight, jump, label, up, down, rup, rdown,
                front_any, row, lane, load, beta, front, flip, isems, osems, fsems):
    loads = [pltpu.make_async_copy(a, b, isems.at[n])
             for n, (a, b) in enumerate(((load_any, load), (beta_any, beta)))]
    for c in loads:
        c.start()
    lab = label[...]
    hi = lab >> 10
    low = hi + (lab & 1023)
    carry = (low >= Z - 1).astype(I32)
    column, axial = hi + carry, low - (Z - 1) * carry
    row[...] = ((column >> 3) << 6) + ((axial >> 7) << 3) + (column & 7)
    lane[...] = axial & 127


    def keep(n, x):
        front[n // 8, :, n % 8 * 128:n % 8 * 128 + 128] = x

    for n in range(FT * 8):
        keep(n, solve[n * 8:n * 8 + 8, :] if n < BS * BS // 8 else jnp.zeros((8, 128), F32))
    for n, x in enumerate((prior, weight, jump)):
        for m in range(8):
            flip[pl.ds(m, BS, stride=8), :] = pltpu.roll(x[...], (128 - m * BS) % 128, 1)
        turned = flip[...].T
        keep(BS * BS // 8 + 2 * n, turned[:8, :])
        keep(BS * BS // 8 + 2 * n + 1, turned[8:16, :])
    sends = []
    fcopies = [pltpu.make_async_copy(front, b, fsems.at[n]) for n, b in enumerate(
        (front_any, rup.at[pl.ds(2 * T, FT)], rdown.at[pl.ds(2 * T, FT)]))]
    for c in fcopies:
        c.start()
    for n, f in enumerate((load, beta)):
        loads[n].wait()
        for a, b in ((f.at[pl.ds(T - H, H)], up.at[pl.ds(n * H, H)]),
                     (f.at[pl.ds(0, H)], down.at[pl.ds(n * H, H)]),
                     (f.at[:, pl.ds(R - 8, 8)], rup.at[pl.ds(n * T, T)]),
                     (f.at[:, pl.ds(0, 8)], rdown.at[pl.ds(n * T, T)])):
            sends.append(pltpu.make_async_copy(a, b, osems.at[len(sends)]))
            sends[-1].start()
    for c in sends + fcopies:
        c.wait()


def side_kernel(kref, above, below_any, side, eup, edown, below, sems):
    loads = [pltpu.make_async_copy(above.at[pl.ds(0, 2 * T)], side, sems.at[0]),
             pltpu.make_async_copy(below_any.at[pl.ds(0, 2 * T)], below, sems.at[1])]
    for c in loads:
        c.start()
    for c in loads:
        c.wait()
    k = kref[0]
    sub = iota((8, Z), 0)
    first = (sub < 4) & (k < GROUPS - 1)
    second = (sub >= 4) & (k > 0)
    for t in range(2 * T):
        side[t] = jnp.where(first, side[t], jnp.where(second, below[t], 0.0))
    for n in range(2):
        eup[n * H:(n + 1) * H] = side[n * T + T - H:n * T + T]
        edown[n * H:(n + 1) * H] = side[n * T:n * T + H]


def shift_azim(x, d):
    return lax.ppermute(x, AZIM, [(i, (i + d) % 32) for i in range(32)])


def shift_rad(x, d):
    return lax.ppermute(x, "rad", [(i, i + d) for i in range(4) if 0 <= i + d < 4])


def ring_kernel(above, below, unread, side, eup, edown):
    side[...] = jnp.where(iota((T, 8, Z), 1) < 4, above[...], below[...])
    eup[...] = side[T - H + 1:]
    edown[...] = side[:H - 1]


nothing = lambda: jnp.zeros((8, 128), F32)
columns = range(Z // 128)


def cut(it):
    it = it % RT
    return slice(it * 8, it * 8 + 8)


def vec(ref, t, it, v):
    return ref[t, cut(it), v * 128:v * 128 + 128]


def put(ref, t, it, v, x):
    ref[t, cut(it), v * 128:v * 128 + 128] = x


def up_row(x):
    return pltpu.roll(x, 7, 0)


def down_row(x):
    return pltpu.roll(x, 1, 0)


def next_lane(ref, t, it, v, cur):
    nxt = pltpu.roll(vec(ref, t, it, v + 1), 127, 1) if v + 1 < Z // 128 else cur
    return jnp.where(iota((8, 128), 1) == 127, nxt, cur), nxt


def ring_rows(k, it):
    sub = iota((8, 128), 0)
    return k * R + (it * 8 + sub if it < RT - 1 else jnp.where(sub < 4, R + sub, sub - 8))


def radii(k, it):
    return 0.25 * 256 + ring_rows(k, it).astype(F32) + 0.5


def relaxed(old, t, it, v, p, pz, pu, prev, zprev, tu, td, r, z, w):
    acc = (tu * vec(old, t + 1, it, v) + td * vec(old, t - 1, it, v)) + r * pu
    rp = down_row(r * p)
    acc = acc + jnp.where(iota((8, 128), 0) == 0, prev, rp)
    zu, pz = next_lane(old, t, it, v, pz)
    zp = pltpu.roll(z * p, 1, 1)
    acc = acc + (z * zu + jnp.where(iota((8, 128), 1) == 0, zprev, zp))
    return (1.0 - OMEGA) * p + w * acc, pz, rp, zp


PARTS = ((1, 6), (7, 4), (11, 4))


def coef_kernel(first, count, kref, load, beta_in, lo, hi, side, clo, chi,
                h_out, w_out, r_out, z_out, t_out, pa, beta, hh, ww, rr, zz, th, rads, sems, osems):
    k = kref[0]
    rows, ring = pl.ds(0, R), pl.ds(R, 8)
    copies = []
    begin, end = first - 1, first + count + 1
    for f, (ref, own, n) in enumerate(((beta, beta_in, 1), (pa, load, 0))):
        spans = ((max(begin, 0), min(end, H), lo, clo, n * H, 0, n * H),
                 (max(begin, H), min(end, H + T), own, side, 0, H, n * T),
                 (max(begin, H + T), min(end, TE), hi, chi, n * H, H + T, n * H))
        for m, (x, y, main, tile, base, origin, tbase) in enumerate(spans):
            if x < y:
                copies.append(pltpu.make_async_copy(
                    main.at[pl.ds(base + x - origin, y - x)], ref.at[pl.ds(x - begin, y - x), rows], sems.at[f, m, 0]))
                copies.append(pltpu.make_async_copy(
                    tile.at[pl.ds(tbase + x - origin, y - x)], ref.at[pl.ds(x - begin, y - x), ring], sems.at[f, m, 1]))
    for c in copies:
        c.start()
    lanes = iota((8, 128), 1)
    top, bottom, last_lane, first_lane = iota((8, 128), 0) == 7, iota((8, 128), 0) == 0, lanes == 127, lanes == 0
    angular = (256 / (2.0 * math.pi)) ** 2
    for it in range(RT):
        ra, gi = radii(k, it), ring_rows(k, it)
        rads[0, it] = (0.5 * AXIAL) * ra
        rads[1, it] = (0.5 * angular) / ra
        rads[2, it] = jnp.where((gi >= 0) & (gi < 255), 0.5 * (ra + 0.5), 0.0)
    for c in copies:
        c.wait()
    for it in range(RT):
        for v in columns:
            put(th, 0, it, v, (vec(beta, 0, it, v) + vec(beta, 1, it, v)) * rads[1, it])

    def plane(t, _):
        o = t - 1
        last = RT - 1
        bup = [up_row(vec(beta, t, 0, v)) for v in columns]
        pup = [up_row(vec(pa, t, 0, v)) for v in columns]
        fprev, prev = [], []
        for v in columns:
            b = vec(beta, t, last, v)
            face = (b + jnp.where(top, bup[v], up_row(b))) * rads[2, last]
            fprev.append(down_row(face))
            prev.append(down_row(face * vec(pa, t, last, v)))
        for it in range(RT):
            axi, ang, rad = rads[0, it], rads[1, it], rads[2, it]
            bz = pltpu.roll(vec(beta, t, it, 0), 127, 1)
            pz = pltpu.roll(vec(pa, t, it, 0), 127, 1)
            zfprev = zprev = nothing()
            for v in columns:
                b, p = vec(beta, t, it, v), vec(pa, t, it, v)
                nb, np_ = up_row(vec(beta, t, it + 1, v)), up_row(vec(pa, t, it + 1, v))
                tu = (b + vec(beta, t + 1, it, v)) * ang
                td = vec(th, t - 1, it, v)
                r = (b + jnp.where(top, nb, bup[v])) * rad
                froll = down_row(r)
                other = jnp.where(bottom, fprev[v], froll)
                bu, bz = next_lane(beta, t, it, v, bz)
                zf = (b + bu) * axi
                z = zf
                if v == Z // 128 - 1:
                    zf = jnp.where(last_lane, 2.0 * (b * axi), zf)
                    z = jnp.where(last_lane, 0.0, zf)
                zr = pltpu.roll(z, 1, 1)
                d = (tu + td) + (r + other) + (zf + jnp.where(first_lane, zfprev, zr))
                if it == last:
                    d = jnp.where(d > 0.0, d, 1.0)
                w = pl.reciprocal(d, approx=True)
                w = w * (2.0 - d * w)
                w = (w * (2.0 - d * w)) * OMEGA
                put(th, t, it, v, tu)
                put(rr, o, it, v, r)
                put(zz, o, it, v, z)
                put(ww, o, it, v, w)
                pu = jnp.where(top, np_, pup[v])
                new, pz, prev[v], zprev = relaxed(pa, t, it, v, p, pz, pu, prev[v], zprev, tu, td, r, z, w)
                put(hh, o, it, v, new)
                bup[v], pup[v], fprev[v], zfprev = nb, np_, froll, zr
        for c in results(o):
            c.start()
        return 0

    def results(o):
        pairs = ((hh.at[o], h_out.at[o]), (ww.at[o], w_out.at[o]), (rr.at[o], r_out.at[o]),
                 (zz.at[o], z_out.at[o]), (th.at[o + 1], t_out.at[o]))
        return [pltpu.make_async_copy(a, b, osems.at[m, o]) for m, (a, b) in enumerate(pairs)]

    lax.fori_loop(1, count + 1, plane, 0)
    for o in range(count):
        for c in results(o):
            c.wait()


def sweep_kernel(kref, *refs):
    given, (src, slo, shi, sside, sclo, schi, out_any) = refs[:15], refs[15:22]
    pa, pb, th, rr, zz, ww, ss, out, sems, osems = refs[22:]
    k = kref[0]
    rows, ring = pl.ds(0, R), pl.ds(R, 8)
    waits = []
    for g, (first, count) in enumerate(PARTS):
        cs = []

        def fetch(a, b):
            cs.append(pltpu.make_async_copy(a, b, sems.at[g, len(cs)]))

        for a, ref in zip(given[5 * g:5 * g + 2], (pb, ww)):
            fetch(a, ref.at[pl.ds(first, count)])
        for x, y, main, tile, origin in ((first, min(first + count, H), slo, sclo, 1),
                                         (max(first, H), min(first + count, H + T), src, sside, H),
                                         (max(first, H + T), first + count, shi, schi, H + T)):
            if x < y:
                fetch(main.at[pl.ds(x - origin, y - x)], ss.at[pl.ds(x, y - x), rows])
                fetch(tile.at[pl.ds(x - origin, y - x)], ss.at[pl.ds(x, y - x), ring])
        for a, ref in zip(given[5 * g + 2:5 * g + 5], (rr, zz, th)):
            fetch(a, ref.at[pl.ds(first, count)])
        waits.append(cs)

    def begin(g):
        for c in waits[g] if g < len(PARTS) else ():
            c.start()

    def add_source(t, _):
        for it in range(RT):
            ra = radii(k, it)
            for v in columns:
                s = vec(ww, t, it, v) * (vec(ss, t, it, v) * ra)
                put(ss, t, it, v, s)
                put(pb, t, it, v, vec(pb, t, it, v) - s)
        return 0

    def sweep(old, new, t, tiles, shift):
        pup = [up_row(vec(old, t, 0, v)) for v in columns]
        prev = [down_row(vec(rr, t, -1, v) * vec(old, t, -1, v)) for v in columns]
        for it in range(tiles):
            pz = pltpu.roll(vec(old, t, it, 0), 127, 1)
            zprev = nothing()
            for v in columns:
                p = vec(old, t, it, v)
                np_ = up_row(vec(old, t, it + 1, v))
                pu = jnp.where(iota((8, 128), 0) == 7, np_, pup[v])
                x, pz, prev[v], zprev = relaxed(
                    old, t, it, v, p, pz, pu, prev[v], zprev, vec(th, t, it, v), vec(th, t - 1, it, v),
                    vec(rr, t, it, v), vec(zz, t, it, v), vec(ww, t, it, v))
                put(new, t - shift, it, v, x - vec(ss, t, it, v))
                pup[v] = np_
        return 0

    begin(0)
    begin(1)
    start = 2
    for g, (first, count) in enumerate(PARTS):
        for c in waits[g]:
            c.wait()
        begin(g + 2)
        lax.fori_loop(first, first + count, add_source, 0)
        lax.fori_loop(start, first + count - 1, lambda t, _: sweep(pb, pa, t, RT, 0), 0)
        start = first + count - 1
    lax.fori_loop(3, TE - 3, lambda t, _: sweep(pa, pb, t, RT, 0), 0)

    def final(t, _):
        sweep(pb, out, t, RT - 1, H)
        pltpu.make_async_copy(out.at[t - H], out_any.at[t - H], osems.at[t - H]).start()
        return 0

    lax.fori_loop(4, TE - 4, final, 0)
    for t in range(T):
        pltpu.make_async_copy(out.at[t], out_any.at[t], osems.at[t]).wait()


def from_all(copies, axes):
    return lax.all_to_all(copies, axes, 0, 0)


def sum_kernel(parts, *refs):
    out = refs[-1]
    s = parts[0]
    for n in range(1, parts.shape[0]):
        s = s + parts[n]
    for n in range(out.shape[0]):
        out[n] = s


VM = pl.BlockSpec(memory_space=pltpu.VMEM)
SM = pl.BlockSpec(memory_space=pltpu.SMEM)
ANY = pl.BlockSpec(memory_space=pltpu.HBM)


def params(mib):
    return pltpu.CompilerParams(vmem_limit_bytes=62 << 20)


def cost(us):
    return pl.CostEstimate(flops=1000, bytes_accessed=us * 3000000, transcendentals=0)


def per_device(load, outflow, beta, heat, label, vertex, share, tally, prior, weight, jump, solve):
    label = label.reshape(GROUPS, SLOTS)
    vertex = vertex.reshape(GROUPS, SLOTS)
    share = share.reshape(GROUPS, SLOTS)
    tally = tally.reshape(GROUPS)
    kidx = lax.axis_index("rad").astype(I32).reshape(1)
    nodes = lambda v: v.reshape(BS, NB)

    shape = lambda *d: jax.ShapeDtypeStruct(d, F32)
    slot = jax.ShapeDtypeStruct((GROUPS, SLOTS), I32)
    plane = lambda n: shape(n, R, Z)
    tile = lambda n: shape(n, 8, Z)
    block = pltpu.VMEM((T, R, Z), F32)
    up, down, rup, rdown, front, row, lane = pl.pallas_call(
        pack_kernel,
        out_shape=(plane(2 * H), plane(2 * H), tile(2 * T + FT), tile(2 * T + FT), tile(FT), slot, slot),
        in_specs=[ANY] * 2 + [VM] * 5, out_specs=(ANY,) * 5 + (VM,) * 2,
        scratch_shapes=[block, block, pltpu.VMEM((FT, 8, Z), F32), pltpu.VMEM((128, 128), F32),
                        pltpu.SemaphoreType.DMA((2,)), pltpu.SemaphoreType.DMA((8,)), pltpu.SemaphoreType.DMA((3,))],
        compiler_params=params(10), cost_estimate=cost(4), name="pack",
    )(load, beta, solve.reshape(BS * BS, NB), nodes(prior), nodes(weight), nodes(jump), label)
    lo, hi = shift_azim(up, 1), shift_azim(down, -1)
    ring = lambda x, d: lax.ppermute(x, "rad", [(i, (i + d) % 4) for i in range(4)])
    rhi, rlo, across = ring(rdown, -1), ring(rup, 1), ring(front, 2)

    partial = pl.pallas_call(
        flux_kernel, out_shape=shape(8, GROUPS * BS, NB),
        in_specs=[SM, SM, ANY, VM, VM, VM], out_specs=VM,
        scratch_shapes=[block, pltpu.VMEM((T * R * 8, 128), F32), pltpu.VMEM((SLOTS, 128), F32),
                        pltpu.SemaphoreType.DMA((T,))],
        compiler_params=params(12), cost_estimate=cost(10), name="flux",
    )(tally, row, heat, lane, vertex, share)
    side, eup, edown = pl.pallas_call(
        side_kernel, out_shape=(tile(2 * T), tile(2 * H), tile(2 * H)),
        in_specs=[SM, ANY, ANY], out_specs=(VM,) * 3,
        scratch_shapes=[pltpu.VMEM((2 * T, 8, Z), F32), pltpu.SemaphoreType.DMA((2,))],
        compiler_params=params(4), cost_estimate=cost(2), name="side",
    )(kidx, rhi, rlo)
    clo, chi = shift_azim(eup, 1), shift_azim(edown, -1)
    near = pl.pallas_call(
        sum_kernel, out_shape=shape(16, GROUPS * BS, NB),
        in_specs=[VM, ANY, ANY], out_specs=VM, compiler_params=params(4), name="near",
    )(from_all(partial, ("z", "core")), side, across)
    def coefficients(first, count):
        ext = lambda n: pltpu.VMEM((n, RE, Z), F32)
        return pl.pallas_call(
            functools.partial(coef_kernel, first, count), out_shape=(shape(count, RE, Z),) * 5,
            in_specs=[SM] + [ANY] * 7, out_specs=(ANY,) * 5,
            scratch_shapes=[ext(count + 2)] * 2 + [ext(count)] * 4 + [ext(count + 1), pltpu.VMEM((3, RT, 8, 128), F32),
                            pltpu.SemaphoreType.DMA((2, 3, 2)), pltpu.SemaphoreType.DMA((5, count))],
            compiler_params=params(40), cost_estimate=cost(1 + count), name="coef",
        )(kidx, load, beta, lo, hi, side, clo, chi)

    given = [coefficients(first, count) for first, count in PARTS]
    flux = from_all(near, ("y", "rad"))
    source, sup, sdown, srup, srdown, height = pl.pallas_call(
        front_kernel,
        out_shape=(plane(T), plane(H - 1), plane(H - 1), tile(T), tile(T), shape(BS, NB)),
        in_specs=[SM, SM, SM, VM] + [ANY] * 4 + [VM] * 3 + [ANY] * 7, out_specs=(ANY,) * 5 + (VM,),
        scratch_shapes=[pltpu.VMEM((GROUPS, FT, 8, Z), F32),
                        pltpu.VMEM((GROUPS, BS, NB), F32), pltpu.VMEM((GROUPS, BS, NB), F32),
                        pltpu.VMEM((GROUPS, SLOTS, 128), F32), pltpu.VMEM((GROUPS * BS, NB), F32),
                        block, pltpu.VMEM((R * 8, 128), F32), pltpu.VMEM((128, 128), F32),
                        pltpu.SemaphoreType.DMA((6,)), pltpu.SemaphoreType.DMA((GROUPS, T)),
                        pltpu.SemaphoreType.DMA((GROUPS,))]
        + [pltpu.VMEM((T * R * 8, 128), F32)] * GROUPS,
        compiler_params=params(20), cost_estimate=cost(10), name="front",
    )(kidx, tally, row, flux, front, rhi, rlo, across, lane, vertex, share, outflow, lo, hi, side, clo, chi, given[0][0])
    slo, shi = shift_azim(sup, 1), shift_azim(sdown, -1)
    sside, seup, sedown = pl.pallas_call(
        ring_kernel, out_shape=(tile(T), tile(H - 1), tile(H - 1)),
        in_specs=[VM, VM, ANY], out_specs=(VM,) * 3, compiler_params=params(4), cost_estimate=cost(1), name="ring",
    )(shift_rad(srdown, -1), shift_rad(srup, 1), given[1][0])
    sclo, schi = shift_azim(seup, 1), shift_azim(sedown, -1)
    ext = pltpu.VMEM((TE, RE, Z), F32)
    pressure = pl.pallas_call(
        sweep_kernel, out_shape=plane(T),
        in_specs=[SM] + [ANY] * 21, out_specs=ANY,
        scratch_shapes=[ext] * 7 + [block, pltpu.SemaphoreType.DMA((len(PARTS), 9)), pltpu.SemaphoreType.DMA((T,))],
        compiler_params=params(46), cost_estimate=cost(20), name="sweeps",
    )(kidx, *[x for part in given for x in part], source, slo, shi, sside, sclo, schi)
    return pressure, height.reshape(NB * BS)


def solution(mesh):
    fine = jax.sharding.Mesh(mesh.devices.reshape(4, 4, 2, 4), AZIM + ("rad",))
    cells = P(AZIM, "rad", None)
    slots = P(AZIM, "rad", None, None)
    return jax.shard_map(
        per_device,
        mesh=fine,
        in_specs=(cells, cells, cells, cells, slots, slots, slots, cells,
                  P("rad"), P("rad"), P("rad"), P(None, None, "rad")),
        out_specs=(cells, P("rad")),
        check_vma=False,
    )
```

```python
import functools
import math

import jax
import jax.numpy as jnp
from jax import lax
from jax.experimental import pallas as pl
from jax.experimental.pallas import tpu as pltpu
from jax.sharding import PartitionSpec as P

SWEEPS = 4
ITERS = 4
OMEGA = 0.9
AXIAL = 0.25
STEFAN = 1.0
SHRINK = 0.3
COUPLE = 0.2

F32 = jnp.float32
I32 = jnp.int32
BF16 = jnp.bfloat16

T, R, Z = 8, 64, 1024
H = 4
TE = T + 2 * H
RE = R + 8
RT = RE // 8
GROUPS, SLOTS, NB, BS = 4, 1024, 128, 16
FT = 5
UNROLL = 16
AZIM = ("y", "z", "core")


def iota(shape, dim):
    return lax.broadcasted_iota(I32, shape, dim)


def pieces(x):
    h = x.astype(BF16)
    rest = x - h.astype(F32)
    m = rest.astype(BF16)
    return h, m, (rest - m.astype(F32)).astype(BF16)


def at8(i):
    return pl.ds(pl.multiple_of(i * 8, 8), 8)


def flux_kernel(cnt, heat_any, label, vert, share, load_any, beta_any, solve, prior, weight, jump,
                out, row_out, lane, up, down, rup, rdown, front_any,
                heat, diff, picked, row, load, beta, front, flip, sems, isems, osems, fsems):
    loads = [pltpu.make_async_copy(heat_any.at[t], heat.at[t], sems.at[t]) for t in range(T)]
    fields = [pltpu.make_async_copy(a, b, isems.at[n])
              for n, (a, b) in enumerate(((load_any, load), (beta_any, beta)))]
    for c in loads + fields:
        c.start()
    lab = label[...]
    hi = lab >> 10
    low = hi + (lab & 1023)
    carry = (low >= Z - 1).astype(I32)
    column, axial = hi + carry, low - (Z - 1) * carry
    row_out[...] = ((column >> 3) << 6) + ((axial >> 7) << 3) + (column & 7)
    lane[...] = axial & 127
    index = pltpu.make_async_copy(row_out, row, isems.at[2])
    index.start()

    def keep(n, x):
        front[n // 8, :, n % 8 * 128:n % 8 * 128 + 128] = x

    for n in range(FT * 8):
        keep(n, solve[n * 8:n * 8 + 8, :] if n < BS * BS // 8 else jnp.zeros((8, 128), F32))
    for n, x in enumerate((prior, weight, jump)):
        for m in range(8):
            flip[pl.ds(m, BS, stride=8), :] = pltpu.roll(x[...], (128 - m * BS) % 128, 1)
        turned = flip[...].T
        keep(BS * BS // 8 + 2 * n, turned[:8, :])
        keep(BS * BS // 8 + 2 * n + 1, turned[8:16, :])
    sends = [pltpu.make_async_copy(front, b, fsems.at[n]) for n, b in enumerate(
        (front_any, rup.at[pl.ds(2 * T, FT)], rdown.at[pl.ds(2 * T, FT)]))]
    for c in sends:
        c.start()
    for t in range(T):
        loads[t].wait()

        def make(q, _):
            x = heat[t, at8(q), :]
            d = pltpu.roll(x, Z - 1, 1) - x
            for zc in range(8):
                diff[at8((t * 8 + q) * 8 + zc), :] = d[:, zc * 128:(zc + 1) * 128]
            return 0

        lax.fori_loop(0, R // 8, make, 0, unroll=4)
    for n, f in enumerate((load, beta)):
        fields[n].wait()
        for m, (a, b) in enumerate(((f.at[pl.ds(T - H, H)], up.at[pl.ds(n * H, H)]),
                                    (f.at[pl.ds(0, H)], down.at[pl.ds(n * H, H)]),
                                    (f.at[:, pl.ds(R - 8, 8)], rup.at[pl.ds(n * T, T)]),
                                    (f.at[:, pl.ds(0, 8)], rdown.at[pl.ds(n * T, T)]))):
            sends.append(pltpu.make_async_copy(a, b, osems.at[4 * n + m]))
            sends[-1].start()
    index.wait()
    for j in range(GROUPS):
        def body(b, _):
            base = pl.multiple_of(b * UNROLL, UNROLL)
            for u in range(UNROLL):
                picked[pl.ds(base + u, 1), :] = diff[pl.ds(row[j, base + u], 1), :]
            return 0

        lax.fori_loop(0, (cnt[j] + UNROLL - 1) // UNROLL, body, 0)
        vals = []
        for kb in range(SLOTS // 128):
            cut = slice(kb * 128, (kb + 1) * 128)
            hit = iota((128, 128), 0) == lane[j:j + 1, cut]
            vals.append(jnp.sum(jnp.where(hit, picked[cut, :].T, 0.0), axis=0, keepdims=True))
        live = iota((1, SLOTS), 1) < cnt[j]
        val = jnp.where(live, share[j:j + 1, :] * jnp.concatenate(vals, axis=1), 0.0)
        v = vert[j:j + 1, :]
        inner = iota((BS, SLOTS), 0) == (v & (BS - 1))
        left = jnp.concatenate(
            [jnp.where(inner, p.astype(F32), 0.0).astype(BF16) for p in pieces(val)], axis=0)
        right = jnp.where(iota((NB, SLOTS), 0) == (v >> 4), 1.0, 0.0).astype(BF16)
        o = lax.dot_general(left, right, (((1,), (1,)), ((), ())), preferred_element_type=F32)
        o = o[:BS] + o[BS:2 * BS] + o[2 * BS:]
        for n in range(out.shape[0]):
            out[n, j * BS:(j + 1) * BS, :] = o
    for c in sends:
        c.wait()


def front_kernel(kref, cnt, row, parts, f0, f1, f2, f3, lane, vert, share, pred_any, *refs):
    front_body(kref, cnt, row, parts, (f0, f1, f2, f3), lane, vert, share, pred_any, *refs[5:])


def front_body(kref, cnt, row, parts, fronts, lane, vert, share, pred_any, src_any, sup, sdown, srup, srdown,
               hout, front, gtab, height, terms, flux, pred, zeros, flip, sems, zsems, fsems, *acc):
    k = kref[0]
    load = pltpu.make_async_copy(pred_any, pred, sems.at[0])
    load.start()
    own, above, below, across = fronts
    copies = [(own, 0), (above.at[pl.ds(2 * T, FT)], 1), (across, 2), (below.at[pl.ds(2 * T, FT)], 3)]
    copies = [pltpu.make_async_copy(f, front.at[lax.rem(k + n, GROUPS)], fsems.at[n]) for f, n in copies]
    for c in copies:
        c.start()
    zeros[...] = jnp.zeros(zeros.shape, F32)
    count = zeros.shape[0]
    clears = [pltpu.make_async_copy(zeros, a.at[pl.ds(n * count, count)], zsems.at[m, n])
              for m, a in enumerate(acc) for n in range(T * R * 8 // count)]
    for c in clears:
        c.start()
    sums = parts[0]
    for n in range(1, parts.shape[0]):
        sums = sums + parts[n]
    flux[...] = sums
    for c in copies:
        c.wait()

    def held(g, n):
        return jnp.concatenate([front[g, m // 8, :, m % 8 * 128:m % 8 * 128 + 128]
                                for m in (2 * n, 2 * n + 1)], axis=0)

    def neighbours(h):
        last = jnp.concatenate([h[g][BS - 1:BS, :] for g in range(GROUPS)], axis=0)
        first = jnp.concatenate([h[g][0:1, :] for g in range(GROUPS)], axis=0)
        zrow = jnp.zeros((1, 128), F32)
        lr = pltpu.roll(last, 1, 1)
        fr = pltpu.roll(first, 127, 1)
        col = iota((GROUPS, 128), 1)
        lr = jnp.where(col == 0, jnp.concatenate([zrow, lr[:-1]], axis=0), lr)
        fr = jnp.where(col == 127, jnp.concatenate([fr[1:], zrow], axis=0), fr)
        down = [jnp.concatenate([lr[g:g + 1], h[g][:BS - 1]], axis=0) for g in range(GROUPS)]
        up = [jnp.concatenate([h[g][1:], fr[g:g + 1]], axis=0) for g in range(GROUPS)]
        return down, up

    prior = [held(g, BS) for g in range(GROUPS)]
    h = list(prior)
    for _ in range(ITERS):
        down, up = neighbours(h)
        for g in range(GROUPS):
            applied = (2.0 + held(g, BS + 1)) * h[g] - down[g] - up[g]
            res = held(g, BS + 2) + COUPLE * flux[g * BS:(g + 1) * BS, :] - applied
            h[g] = h[g] + jnp.concatenate(
                [jnp.sum(held(g, i) * res, axis=0, keepdims=True) for i in range(BS)], axis=0)
    down, up = neighbours(h)
    for g in range(GROUPS):
        slope = up[g] - down[g]
        growth = h[g] - prior[g]
        height[g] = h[g]
        gtab[g] = (flux[g * BS:(g + 1) * BS, :] - STEFAN * growth) * jnp.sqrt(1.0 + slope * slope)
    for j in range(GROUPS):
        v = vert[j:j + 1, :]
        right = jnp.where(iota((NB, SLOTS), 0) == (v >> 4), 1.0, 0.0).astype(BF16)
        x = jnp.dot(jnp.concatenate(pieces(gtab[j]), axis=0), right, preferred_element_type=F32)
        x = x[:BS] + x[BS:2 * BS] + x[2 * BS:]
        inner = iota((BS, SLOTS), 0) == (v & (BS - 1))
        term = jnp.sum(jnp.where(inner, x, 0.0), axis=0, keepdims=True) * share[j:j + 1, :]
        term = jnp.where(iota((1, SLOTS), 1) < cnt[j], term, 0.0)
        for kb in range(SLOTS // 128):
            cut = slice(kb * 128, (kb + 1) * 128)
            hit = iota((128, 128), 0) == lane[j:j + 1, cut]
            terms[j, cut, :] = jnp.where(hit, term[:, cut], 0.0).T
    for c in clears:
        c.wait()
    most = jnp.maximum(jnp.maximum(cnt[0], cnt[1]), jnp.maximum(cnt[2], cnt[3]))

    def add(b, _):
        for u in range(UNROLL):
            s = b * UNROLL + u
            for j in range(GROUPS):
                at = pl.ds(row[j, s], 1)
                acc[j][at, :] = acc[j][at, :] + terms[j, pl.ds(s, 1), :]
        return 0

    lax.fori_loop(0, (most + UNROLL - 1) // UNROLL, add, 0)

    load.wait()
    src = pred
    sends = []

    def send(m, a, b):
        sends.append(pltpu.make_async_copy(a, b, sems.at[m]))
        sends[-1].start()

    for d in range(T):
        def finish(q, _):
            for zc in range(8):
                a = at8((d * 8 + q) * 8 + zc)
                s = (acc[0][a, :] + acc[1][a, :]) + (acc[2][a, :] + acc[3][a, :])
                cut = slice(zc * 128, (zc + 1) * 128)
                src[d, at8(q), cut] = pred[d, at8(q), cut] + SHRINK * s
            return 0

        lax.fori_loop(0, R // 8, finish, 0, unroll=2)
        if d == H - 2:
            send(1, src.at[pl.ds(0, H - 1)], sdown)
    send(2, src.at[pl.ds(T - H + 1, H - 1)], sup)
    send(3, src.at[:, pl.ds(R - 8, 8)], srup)
    send(4, src.at[:, pl.ds(0, 8)], srdown)
    send(5, src, src_any)
    flip[...] = jnp.concatenate([height[k], jnp.zeros((128 - BS, 128), F32)], axis=0).T
    nodes = flip[pl.ds(0, BS, stride=8), :]
    for m in range(1, 8):
        nodes = nodes + pltpu.roll(flip[pl.ds(m, BS, stride=8), :], m * BS, 1)
    hout[...] = nodes
    for c in sends:
        c.wait()


def side_kernel(kref, above, below_any, side, eup, edown, below, sems):
    loads = [pltpu.make_async_copy(above.at[pl.ds(0, 2 * T)], side, sems.at[0]),
             pltpu.make_async_copy(below_any.at[pl.ds(0, 2 * T)], below, sems.at[1])]
    for c in loads:
        c.start()
    for c in loads:
        c.wait()
    k = kref[0]
    sub = iota((8, Z), 0)
    first = (sub < 4) & (k < GROUPS - 1)
    second = (sub >= 4) & (k > 0)
    for t in range(2 * T):
        side[t] = jnp.where(first, side[t], jnp.where(second, below[t], 0.0))
    for n in range(2):
        eup[n * H:(n + 1) * H] = side[n * T + T - H:n * T + T]
        edown[n * H:(n + 1) * H] = side[n * T:n * T + H]


def shift_azim(x, d):
    return lax.ppermute(x, AZIM, [(i, (i + d) % 32) for i in range(32)])


def shift_rad(x, d):
    return lax.ppermute(x, "rad", [(i, i + d) for i in range(4) if 0 <= i + d < 4])


def ring_tile(from_above, from_below):
    return jnp.where(iota(from_above.shape, 1) < 4, from_above, from_below)


def wide(x):
    return jnp.concatenate([x] * (Z // 128), axis=1)


def sweep_kernel(kref, load, beta_in, lo, hi, side, clo, chi, src, slo, shi, sside, sclo, schi,
                 out_any, pa, pb, beta, th, rr, zz, ww, ss, rads, out, sems, osems):
    k = kref[0]
    rows, ring = pl.ds(0, R), pl.ds(R, 8)
    half = T // 2

    def planes(own, tile_own, low, tile_low, high, tile_high, first):
        return [(low, tile_low, first, H - first), (own.at[pl.ds(0, half)], tile_own.at[pl.ds(0, half)], H, half),
                (own.at[pl.ds(half, half)], tile_own.at[pl.ds(half, half)], H + half, half),
                (high, tile_high, H + T, H - first)]

    def both(x, n, count):
        return x.at[pl.ds(n * count, count)]

    fields = [(ref, planes(own, both(side, n, T), both(lo, n, H), both(clo, n, H), both(hi, n, H), both(chi, n, H), 0))
              for ref, own, n in ((beta, beta_in, 1), (pa, load, 0))]
    fields.append((ss, planes(src, sside, slo, sclo, shi, schi, 1)))
    waits = []
    for g in range(4):
        cs = []
        for f, (ref, parts) in enumerate(fields):
            main, tile, first, count = parts[g]
            cs.append(pltpu.make_async_copy(main, ref.at[pl.ds(first, count), rows], sems.at[g, f, 0]))
            cs.append(pltpu.make_async_copy(tile, ref.at[pl.ds(first, count), ring], sems.at[g, f, 1]))
        waits.append(cs)

    def begin(g):
        for c in waits[g] if g < 4 else ():
            c.start()

    begin(0)
    begin(1)
    sub, lanes = iota((8, 128), 0), iota((8, 128), 1)
    top, bottom, last_lane, first_lane = sub == 7, sub == 0, lanes == 127, lanes == 0
    angular = (256 / (2.0 * math.pi)) ** 2
    for it in range(RT):
        gi = k * R + (it * 8 + sub if it < RT - 1 else jnp.where(sub < 4, R + sub, sub - 8))
        ra = 0.25 * 256 + gi.astype(F32) + 0.5
        rads[0, it] = ra
        rads[1, it] = (0.5 * angular) / ra
        rads[2, it] = jnp.where((gi >= 0) & (gi < 255), 0.5 * (ra + 0.5), 0.0)
    nothing = jnp.zeros((8, 128), F32)
    columns = range(Z // 128)

    def cut(it):
        it = it % RT
        return slice(it * 8, it * 8 + 8)

    def vec(ref, t, it, v):
        return ref[t, cut(it), v * 128:v * 128 + 128]

    def put(ref, t, it, v, x):
        ref[t, cut(it), v * 128:v * 128 + 128] = x

    def up_row(x):
        return pltpu.roll(x, 7, 0)

    def down_row(x):
        return pltpu.roll(x, 1, 0)

    def next_lane(ref, t, it, v, cur):
        nxt = pltpu.roll(vec(ref, t, it, v + 1), 127, 1) if v + 1 < Z // 128 else cur
        return jnp.where(last_lane, nxt, cur), nxt

    def relaxed(old, t, it, v, p, pz, pu, prev, zprev, tu, td, r, z, w, s):
        acc = (tu * vec(old, t + 1, it, v) + td * vec(old, t - 1, it, v)) + r * pu
        rp = down_row(r * p)
        acc = acc + jnp.where(bottom, prev, rp)
        zu, pz = next_lane(old, t, it, v, pz)
        zp = pltpu.roll(z * p, 1, 1)
        acc = acc + (z * zu + jnp.where(first_lane, zprev, zp))
        return (1.0 - OMEGA) * p + w * (acc - s), pz, rp, zp

    def first_sweep(t, _):
        last = RT - 1
        bup = [up_row(vec(beta, t, 0, v)) for v in columns]
        pup = [up_row(vec(pa, t, 0, v)) for v in columns]
        fprev, prev = [], []
        for v in columns:
            b = vec(beta, t, last, v)
            face = (b + jnp.where(top, bup[v], up_row(b))) * rads[2, last]
            fprev.append(down_row(face))
            prev.append(down_row(face * vec(pa, t, last, v)))
        for it in range(RT):
            ra, ang, rad = rads[0, it], rads[1, it], rads[2, it]
            axi = (0.5 * AXIAL) * ra
            bz = pltpu.roll(vec(beta, t, it, 0), 127, 1)
            pz = pltpu.roll(vec(pa, t, it, 0), 127, 1)
            zfprev = zprev = nothing
            for v in columns:
                b, p = vec(beta, t, it, v), vec(pa, t, it, v)
                nb, np_ = up_row(vec(beta, t, it + 1, v)), up_row(vec(pa, t, it + 1, v))
                tu = (b + vec(beta, t + 1, it, v)) * ang
                td = vec(th, t - 1, it, v)
                r = (b + jnp.where(top, nb, bup[v])) * rad
                froll = down_row(r)
                other = jnp.where(bottom, fprev[v], froll)
                bu, bz = next_lane(beta, t, it, v, bz)
                zf = (b + bu) * axi
                z = zf
                if v == Z // 128 - 1:
                    zf = jnp.where(last_lane, 2.0 * (b * axi), zf)
                    z = jnp.where(last_lane, 0.0, zf)
                zr = pltpu.roll(z, 1, 1)
                d = (tu + td) + (r + other) + (zf + jnp.where(first_lane, zfprev, zr))
                if it == last:
                    d = jnp.where(d > 0.0, d, 1.0)
                w = pl.reciprocal(d, approx=True)
                w = w * (2.0 - d * w)
                w = (w * (2.0 - d * w)) * OMEGA
                sc = vec(ss, t, it, v) * ra
                put(th, t, it, v, tu)
                put(rr, t, it, v, r)
                put(zz, t, it, v, z)
                put(ww, t, it, v, w)
                put(ss, t, it, v, sc)
                pu = jnp.where(top, np_, pup[v])
                new, pz, prev[v], zprev = relaxed(pa, t, it, v, p, pz, pu, prev[v], zprev, tu, td, r, z, w, sc)
                put(pb, t, it, v, new)
                bup[v], pup[v], fprev[v], zfprev = nb, np_, froll, zr
        return 0

    def sweep(old, new, t, tiles, shift):
        pup = [up_row(vec(old, t, 0, v)) for v in columns]
        prev = [down_row(vec(rr, t, -1, v) * vec(old, t, -1, v)) for v in columns]
        for it in range(tiles):
            pz = pltpu.roll(vec(old, t, it, 0), 127, 1)
            zprev = nothing
            for v in columns:
                p = vec(old, t, it, v)
                np_ = up_row(vec(old, t, it + 1, v))
                pu = jnp.where(top, np_, pup[v])
                x, pz, prev[v], zprev = relaxed(
                    old, t, it, v, p, pz, pu, prev[v], zprev, vec(th, t, it, v), vec(th, t - 1, it, v),
                    vec(rr, t, it, v), vec(zz, t, it, v), vec(ww, t, it, v), vec(ss, t, it, v))
                put(new, t - shift, it, v, x)
                pup[v] = np_
        return 0

    ends = (H - 1, H + half - 1, H + T - 1, TE - 1)
    start = 1
    for g in range(4):
        for c in waits[g]:
            c.wait()
        begin(g + 2)
        if g == 0:
            for it in range(RT):
                th[0, cut(it), :] = (beta[0, cut(it), :] + beta[1, cut(it), :]) * wide(rads[1, it])
        lax.fori_loop(start, ends[g], first_sweep, 0)
        start = ends[g]
    lax.fori_loop(2, TE - 2, lambda t, _: sweep(pb, pa, t, RT, 0), 0)
    lax.fori_loop(3, TE - 3, lambda t, _: sweep(pa, pb, t, RT, 0), 0)

    def final(t, _):
        sweep(pb, out, t, RT - 1, H)
        pltpu.make_async_copy(out.at[t - H], out_any.at[t - H], osems.at[t - H]).start()
        return 0

    lax.fori_loop(4, TE - 4, final, 0)
    for t in range(T):
        pltpu.make_async_copy(out.at[t], out_any.at[t], osems.at[t]).wait()


def from_all(copies, axes):
    return lax.all_to_all(copies, axes, 0, 0)


def sum_kernel(parts, *refs):
    out = refs[-1]
    s = parts[0]
    for n in range(1, parts.shape[0]):
        s = s + parts[n]
    for n in range(out.shape[0]):
        out[n] = s


VM = pl.BlockSpec(memory_space=pltpu.VMEM)
SM = pl.BlockSpec(memory_space=pltpu.SMEM)
ANY = pl.BlockSpec(memory_space=pltpu.HBM)


def params(mib):
    return pltpu.CompilerParams(vmem_limit_bytes=62 << 20)


def cost(us):
    return pl.CostEstimate(flops=1000, bytes_accessed=us * 3000000, transcendentals=0)


def per_device(load, outflow, beta, heat, label, vertex, share, tally, prior, weight, jump, solve):
    label = label.reshape(GROUPS, SLOTS)
    vertex = vertex.reshape(GROUPS, SLOTS)
    share = share.reshape(GROUPS, SLOTS)
    tally = tally.reshape(GROUPS)
    kidx = lax.axis_index("rad").astype(I32).reshape(1)
    nodes = lambda v: v.reshape(BS, NB)

    shape = lambda *d: jax.ShapeDtypeStruct(d, F32)
    slot = jax.ShapeDtypeStruct((GROUPS, SLOTS), I32)
    plane = lambda n: shape(n, R, Z)
    tile = lambda n: shape(n, 8, Z)
    block = pltpu.VMEM((T, R, Z), F32)
    partial, row, lane, up, down, rup, rdown, front = pl.pallas_call(
        flux_kernel,
        out_shape=(shape(8, GROUPS * BS, NB), slot, slot, plane(2 * H), plane(2 * H),
                   tile(2 * T + FT), tile(2 * T + FT), tile(FT)),
        in_specs=[SM, ANY, VM, VM, VM, ANY, ANY] + [VM] * 4, out_specs=(VM,) * 3 + (ANY,) * 5,
        scratch_shapes=[block, pltpu.VMEM((T * R * 8, 128), F32), pltpu.VMEM((SLOTS, 128), F32),
                        pltpu.SMEM((GROUPS, SLOTS), I32), block, block, pltpu.VMEM((FT, 8, Z), F32),
                        pltpu.VMEM((128, 128), F32), pltpu.SemaphoreType.DMA((T,)), pltpu.SemaphoreType.DMA((3,)),
                        pltpu.SemaphoreType.DMA((8,)), pltpu.SemaphoreType.DMA((3,))],
        compiler_params=params(20), cost_estimate=cost(10), name="flux",
    )(tally, heat, label, vertex, share, load, beta, solve.reshape(BS * BS, NB), nodes(prior), nodes(weight), nodes(jump))
    lo, hi = shift_azim(up, 1), shift_azim(down, -1)
    ring = lambda x, d: lax.ppermute(x, "rad", [(i, (i + d) % 4) for i in range(4)])
    rhi, rlo, across = ring(rdown, -1), ring(rup, 1), ring(front, 2)

    side, eup, edown = pl.pallas_call(
        side_kernel, out_shape=(tile(2 * T), tile(2 * H), tile(2 * H)),
        in_specs=[SM, ANY, ANY], out_specs=(VM,) * 3,
        scratch_shapes=[pltpu.VMEM((2 * T, 8, Z), F32), pltpu.SemaphoreType.DMA((2,))],
        compiler_params=params(4), cost_estimate=cost(2), name="side",
    )(kidx, rhi, rlo)
    clo, chi = shift_azim(eup, 1), shift_azim(edown, -1)
    near = pl.pallas_call(
        sum_kernel, out_shape=shape(16, GROUPS * BS, NB),
        in_specs=[VM, ANY, ANY], out_specs=VM, compiler_params=params(4), name="near",
    )(from_all(partial, ("z", "core")), side, across)
    flux = from_all(near, ("y", "rad"))
    source, sup, sdown, srup, srdown, height = pl.pallas_call(
        front_kernel,
        out_shape=(plane(T), plane(H - 1), plane(H - 1), tile(T), tile(T), shape(BS, NB)),
        in_specs=[SM, SM, SM, VM] + [ANY] * 4 + [VM] * 3 + [ANY] * 6, out_specs=(ANY,) * 5 + (VM,),
        scratch_shapes=[pltpu.VMEM((GROUPS, FT, 8, Z), F32),
                        pltpu.VMEM((GROUPS, BS, NB), F32), pltpu.VMEM((GROUPS, BS, NB), F32),
                        pltpu.VMEM((GROUPS, SLOTS, 128), F32), pltpu.VMEM((GROUPS * BS, NB), F32),
                        block, pltpu.VMEM((R * 8, 128), F32), pltpu.VMEM((128, 128), F32),
                        pltpu.SemaphoreType.DMA((6,)), pltpu.SemaphoreType.DMA((GROUPS, T)),
                        pltpu.SemaphoreType.DMA((GROUPS,))]
        + [pltpu.VMEM((T * R * 8, 128), F32)] * GROUPS,
        compiler_params=params(20), cost_estimate=cost(10), name="front",
    )(kidx, tally, row, flux, front, rhi, rlo, across, lane, vertex, share, outflow, lo, hi, side, clo, chi)
    slo, shi = shift_azim(sup, 1), shift_azim(sdown, -1)
    sside = ring_tile(shift_rad(srdown, -1), shift_rad(srup, 1))
    sclo, schi = shift_azim(sside[T - H + 1:], 1), shift_azim(sside[:H - 1], -1)
    ext = pltpu.VMEM((TE, RE, Z), F32)
    pressure = pl.pallas_call(
        sweep_kernel, out_shape=plane(T),
        in_specs=[SM] + [ANY] * 13, out_specs=ANY,
        scratch_shapes=[ext] * 8 + [pltpu.VMEM((3, RT, 8, 128), F32), block, pltpu.SemaphoreType.DMA((4, 3, 2)),
                        pltpu.SemaphoreType.DMA((T,))],
        compiler_params=params(46), cost_estimate=cost(20), name="sweeps",
    )(kidx, load, beta, lo, hi, side, clo, chi, source, slo, shi, sside, sclo, schi)
    return pressure, height.reshape(NB * BS)


def solution(mesh):
    fine = jax.sharding.Mesh(mesh.devices.reshape(4, 4, 2, 4), AZIM + ("rad",))
    cells = P(AZIM, "rad", None)
    slots = P(AZIM, "rad", None, None)
    return jax.shard_map(
        per_device,
        mesh=fine,
        in_specs=(cells, cells, cells, cells, slots, slots, slots, cells,
                  P("rad"), P("rad"), P("rad"), P(None, None, "rad")),
        out_specs=(cells, P("rad")),
        check_vma=False,
    )
```

```python
import functools
import math

import jax
import jax.numpy as jnp
from jax import lax
from jax.experimental import pallas as pl
from jax.experimental.pallas import tpu as pltpu
from jax.sharding import PartitionSpec as P

SWEEPS = 4
ITERS = 4
OMEGA = 0.9
AXIAL = 0.25
STEFAN = 1.0
SHRINK = 0.3
COUPLE = 0.2

F32 = jnp.float32
I32 = jnp.int32
BF16 = jnp.bfloat16

T, R, Z = 8, 64, 1024
H = 4
TE = T + 2 * H
RE = R + 8
RT = RE // 8
GROUPS, SLOTS, NB, BS = 4, 1024, 128, 16
FT = 5
UNROLL = 16
AZIM = ("y", "z", "core")


def iota(shape, dim):
    return lax.broadcasted_iota(I32, shape, dim)


def pieces(x):
    h = x.astype(BF16)
    rest = x - h.astype(F32)
    m = rest.astype(BF16)
    return h, m, (rest - m.astype(F32)).astype(BF16)


def at8(i):
    return pl.ds(pl.multiple_of(i * 8, 8), 8)


def flux_kernel(cnt, row, heat_any, lane, vert, share, out, heat, diff, picked, vals, sems):
    loads = [pltpu.make_async_copy(heat_any.at[t], heat.at[t], sems.at[t]) for t in range(T)]
    for c in loads:
        c.start()

    picked[...] = jnp.zeros((128, 128), F32)
    vals[...] = jnp.zeros((8, SLOTS), F32)
    for t in range(T):
        loads[t].wait()

        def make(q, _):
            x = heat[t, at8(q), :]
            d = pltpu.roll(x, Z - 1, 1) - x
            for zc in range(8):
                diff[at8((t * 8 + q) * 8 + zc), :] = d[:, zc * 128:(zc + 1) * 128]
            return 0

        lax.fori_loop(0, R // 8, make, 0, unroll=4)
    for j in range(GROUPS):
        blocks = (cnt[j] + 127) // 128

        def pick(b, rows):
            at = pl.ds(pl.multiple_of(jnp.maximum(b, 0) * 128, 128), 128)
            hit = iota((128, 128), 0) == lane[j:j + 1, at]
            vals[0:1, at] = jnp.sum(jnp.where(hit, rows.T, 0.0), axis=0, keepdims=True)

        def body(b, _):
            rows = picked[...]
            base = b * 128
            for u in range(128):
                picked[u:u + 1, :] = diff[pl.ds(row[j, base + u], 1), :]
            pick(b - 1, rows)
            return 0

        lax.fori_loop(0, blocks, body, 0)
        pick(blocks - 1, picked[...])
        live = iota((1, SLOTS), 1) < cnt[j]
        val = jnp.where(live, share[j:j + 1, :] * vals[0:1, :], 0.0)
        v = vert[j:j + 1, :]
        inner = iota((BS, SLOTS), 0) == (v & (BS - 1))
        left = jnp.concatenate(
            [jnp.where(inner, p.astype(F32), 0.0).astype(BF16) for p in pieces(val)], axis=0)
        right = jnp.where(iota((NB, SLOTS), 0) == (v >> 4), 1.0, 0.0).astype(BF16)
        o = lax.dot_general(left, right, (((1,), (1,)), ((), ())), preferred_element_type=F32)
        o = o[:BS] + o[BS:2 * BS] + o[2 * BS:]
        for n in range(out.shape[0]):
            out[n, j * BS:(j + 1) * BS, :] = o


def front_kernel(kref, cnt, row, parts, f0, f1, f2, f3, lane, vert, share, pred_any, *refs):
    front_body(kref, cnt, row, parts, (f0, f1, f2, f3), lane, vert, share, pred_any, *refs[5:])


def front_body(kref, cnt, row, parts, fronts, lane, vert, share, pred_any, src_any, sup, sdown, srup, srdown,
               hout, front, gtab, height, terms, flux, pred, zeros, flip, sems, zsems, fsems, osems, *acc):
    k = kref[0]
    load = pltpu.make_async_copy(pred_any, pred, sems.at[0])
    load.start()
    own, above, below, across = fronts
    copies = [(own, 0), (above.at[pl.ds(2 * T, FT)], 1), (across, 2), (below.at[pl.ds(2 * T, FT)], 3)]
    copies = [pltpu.make_async_copy(f, front.at[lax.rem(k + n, GROUPS)], fsems.at[n]) for f, n in copies]
    for c in copies:
        c.start()
    zeros[...] = jnp.zeros(zeros.shape, F32)
    count = zeros.shape[0]
    clears = [pltpu.make_async_copy(zeros, a.at[pl.ds(n * count, count)], zsems.at[m, n])
              for m, a in enumerate(acc) for n in range(T * R * 8 // count)]
    for c in clears:
        c.start()
    sums = parts[0]
    for n in range(1, parts.shape[0]):
        sums = sums + parts[n]
    flux[...] = sums
    for c in copies:
        c.wait()

    def held(g, n):
        return jnp.concatenate([front[g, m // 8, :, m % 8 * 128:m % 8 * 128 + 128]
                                for m in (2 * n, 2 * n + 1)], axis=0)

    def neighbours(h):
        last = jnp.concatenate([h[g][BS - 1:BS, :] for g in range(GROUPS)], axis=0)
        first = jnp.concatenate([h[g][0:1, :] for g in range(GROUPS)], axis=0)
        zrow = jnp.zeros((1, 128), F32)
        lr = pltpu.roll(last, 1, 1)
        fr = pltpu.roll(first, 127, 1)
        col = iota((GROUPS, 128), 1)
        lr = jnp.where(col == 0, jnp.concatenate([zrow, lr[:-1]], axis=0), lr)
        fr = jnp.where(col == 127, jnp.concatenate([fr[1:], zrow], axis=0), fr)
        down = [jnp.concatenate([lr[g:g + 1], h[g][:BS - 1]], axis=0) for g in range(GROUPS)]
        up = [jnp.concatenate([h[g][1:], fr[g:g + 1]], axis=0) for g in range(GROUPS)]
        return down, up

    prior = [held(g, BS) for g in range(GROUPS)]
    h = list(prior)
    for _ in range(ITERS):
        down, up = neighbours(h)
        for g in range(GROUPS):
            applied = (2.0 + held(g, BS + 1)) * h[g] - down[g] - up[g]
            res = held(g, BS + 2) + COUPLE * flux[g * BS:(g + 1) * BS, :] - applied
            h[g] = h[g] + jnp.concatenate(
                [jnp.sum(held(g, i) * res, axis=0, keepdims=True) for i in range(BS)], axis=0)
    down, up = neighbours(h)
    for g in range(GROUPS):
        slope = up[g] - down[g]
        growth = h[g] - prior[g]
        height[g] = h[g]
        gtab[g] = (flux[g * BS:(g + 1) * BS, :] - STEFAN * growth) * jnp.sqrt(1.0 + slope * slope)
    for j in range(GROUPS):
        v = vert[j:j + 1, :]
        right = jnp.where(iota((NB, SLOTS), 0) == (v >> 4), 1.0, 0.0).astype(BF16)
        x = jnp.dot(jnp.concatenate(pieces(gtab[j]), axis=0), right, preferred_element_type=F32)
        x = x[:BS] + x[BS:2 * BS] + x[2 * BS:]
        inner = iota((BS, SLOTS), 0) == (v & (BS - 1))
        term = jnp.sum(jnp.where(inner, x, 0.0), axis=0, keepdims=True) * share[j:j + 1, :]
        term = jnp.where(iota((1, SLOTS), 1) < cnt[j], term, 0.0)
        for kb in range(SLOTS // 128):
            cut = slice(kb * 128, (kb + 1) * 128)
            hit = iota((128, 128), 0) == lane[j:j + 1, cut]
            terms[j, cut, :] = jnp.where(hit, term[:, cut], 0.0).T
    for c in clears:
        c.wait()
    most = jnp.maximum(jnp.maximum(cnt[0], cnt[1]), jnp.maximum(cnt[2], cnt[3]))

    def add(b, _):
        for u in range(UNROLL):
            s = b * UNROLL + u
            for j in range(GROUPS):
                at = pl.ds(row[j, s], 1)
                acc[j][at, :] = acc[j][at, :] + terms[j, pl.ds(s, 1), :]
        return 0

    lax.fori_loop(0, (most + UNROLL - 1) // UNROLL, add, 0)

    load.wait()
    src = pred
    sends = []

    def send(m, n, a, b):
        sends.append(pltpu.make_async_copy(a, b, osems.at[m, n]))
        sends[-1].start()

    for n, d in enumerate((0, 1, 2, 5, 6, 7, 3, 4)):
        def finish(q, _):
            for zc in range(8):
                a = at8((d * 8 + q) * 8 + zc)
                s = (acc[0][a, :] + acc[1][a, :]) + (acc[2][a, :] + acc[3][a, :])
                cut = slice(zc * 128, (zc + 1) * 128)
                src[d, at8(q), cut] = pred[d, at8(q), cut] + SHRINK * s
            return 0

        lax.fori_loop(0, R // 8, finish, 0, unroll=2)
        if d < H - 1:
            send(0, n, src.at[d], sdown.at[d])
        if d >= T - H + 1:
            send(0, n, src.at[d], sup.at[d - (T - H + 1)])
        send(1, n, src.at[d, pl.ds(R - 8, 8)], srup.at[d])
        send(2, n, src.at[d, pl.ds(0, 8)], srdown.at[d])
        send(3, n, src.at[d], src_any.at[d])
    flip[...] = jnp.concatenate([height[k], jnp.zeros((128 - BS, 128), F32)], axis=0).T
    nodes = flip[pl.ds(0, BS, stride=8), :]
    for m in range(1, 8):
        nodes = nodes + pltpu.roll(flip[pl.ds(m, BS, stride=8), :], m * BS, 1)
    hout[...] = nodes
    for c in sends:
        c.wait()


def pack_kernel(load_any, beta_any, solve, prior, weight, jump, label, up, down, rup, rdown,
                front_any, row, lane, load, beta, front, flip, isems, osems, fsems):
    loads = [pltpu.make_async_copy(a, b, isems.at[n])
             for n, (a, b) in enumerate(((load_any, load), (beta_any, beta)))]
    for c in loads:
        c.start()
    lab = label[...]
    hi = lab >> 10
    low = hi + (lab & 1023)
    carry = (low >= Z - 1).astype(I32)
    column, axial = hi + carry, low - (Z - 1) * carry
    row[...] = ((column >> 3) << 6) + ((axial >> 7) << 3) + (column & 7)
    lane[...] = axial & 127


    def keep(n, x):
        front[n // 8, :, n % 8 * 128:n % 8 * 128 + 128] = x

    for n in range(FT * 8):
        keep(n, solve[n * 8:n * 8 + 8, :] if n < BS * BS // 8 else jnp.zeros((8, 128), F32))
    for n, x in enumerate((prior, weight, jump)):
        for m in range(8):
            flip[pl.ds(m, BS, stride=8), :] = pltpu.roll(x[...], (128 - m * BS) % 128, 1)
        turned = flip[...].T
        keep(BS * BS // 8 + 2 * n, turned[:8, :])
        keep(BS * BS // 8 + 2 * n + 1, turned[8:16, :])
    sends = []
    fcopies = [pltpu.make_async_copy(front, b, fsems.at[n]) for n, b in enumerate(
        (front_any, rup.at[pl.ds(2 * T, FT)], rdown.at[pl.ds(2 * T, FT)]))]
    for c in fcopies:
        c.start()
    for n, f in enumerate((load, beta)):
        loads[n].wait()
        for a, b in ((f.at[pl.ds(T - H, H)], up.at[pl.ds(n * H, H)]),
                     (f.at[pl.ds(0, H)], down.at[pl.ds(n * H, H)]),
                     (f.at[:, pl.ds(R - 8, 8)], rup.at[pl.ds(n * T, T)]),
                     (f.at[:, pl.ds(0, 8)], rdown.at[pl.ds(n * T, T)])):
            sends.append(pltpu.make_async_copy(a, b, osems.at[len(sends)]))
            sends[-1].start()
    for c in sends + fcopies:
        c.wait()


def side_kernel(kref, above, below_any, side, eup, edown, below, sems):
    loads = [pltpu.make_async_copy(above.at[pl.ds(0, 2 * T)], side, sems.at[0]),
             pltpu.make_async_copy(below_any.at[pl.ds(0, 2 * T)], below, sems.at[1])]
    for c in loads:
        c.start()
    for c in loads:
        c.wait()
    k = kref[0]
    sub = iota((8, Z), 0)
    first = (sub < 4) & (k < GROUPS - 1)
    second = (sub >= 4) & (k > 0)
    for t in range(2 * T):
        side[t] = jnp.where(first, side[t], jnp.where(second, below[t], 0.0))
    for n in range(2):
        eup[n * H:(n + 1) * H] = side[n * T + T - H:n * T + T]
        edown[n * H:(n + 1) * H] = side[n * T:n * T + H]


def shift_azim(x, d):
    return lax.ppermute(x, AZIM, [(i, (i + d) % 32) for i in range(32)])


def shift_rad(x, d):
    return lax.ppermute(x, "rad", [(i, i + d) for i in range(4) if 0 <= i + d < 4])


def ring_tile(from_above, from_below):
    return jnp.where(iota(from_above.shape, 1) < 4, from_above, from_below)


def wide(x):
    return jnp.concatenate([x] * (Z // 128), axis=1)


def sweep_kernel(kref, load, beta_in, lo, hi, side, clo, chi, src, slo, shi, sside, sclo, schi,
                 out_any, pa, pb, beta, th, rr, zz, ww, ss, rads, out, sems, osems):
    k = kref[0]
    rows, ring = pl.ds(0, R), pl.ds(R, 8)
    half = T // 2

    def planes(own, tile_own, low, tile_low, high, tile_high, first):
        return [(low, tile_low, first, H - first), (own.at[pl.ds(0, half)], tile_own.at[pl.ds(0, half)], H, half),
                (own.at[pl.ds(half, half)], tile_own.at[pl.ds(half, half)], H + half, half),
                (high, tile_high, H + T, H - first)]

    def both(x, n, count):
        return x.at[pl.ds(n * count, count)]

    fields = [(ref, planes(own, both(side, n, T), both(lo, n, H), both(clo, n, H), both(hi, n, H), both(chi, n, H), 0))
              for ref, own, n in ((beta, beta_in, 1), (pa, load, 0))]
    fields.append((ss, planes(src, sside, slo, sclo, shi, schi, 1)))
    waits = []
    for g in range(4):
        cs = []
        for f, (ref, parts) in enumerate(fields):
            main, tile, first, count = parts[g]
            cs.append(pltpu.make_async_copy(main, ref.at[pl.ds(first, count), rows], sems.at[g, f, 0]))
            cs.append(pltpu.make_async_copy(tile, ref.at[pl.ds(first, count), ring], sems.at[g, f, 1]))
        waits.append(cs)

    def begin(g):
        for c in waits[g] if g < 4 else ():
            c.start()

    begin(0)
    begin(1)
    sub, lanes = iota((8, 128), 0), iota((8, 128), 1)
    top, bottom, last_lane, first_lane = sub == 7, sub == 0, lanes == 127, lanes == 0
    angular = (256 / (2.0 * math.pi)) ** 2
    for it in range(RT):
        gi = k * R + (it * 8 + sub if it < RT - 1 else jnp.where(sub < 4, R + sub, sub - 8))
        ra = 0.25 * 256 + gi.astype(F32) + 0.5
        rads[0, it] = ra
        rads[1, it] = (0.5 * angular) / ra
        rads[2, it] = jnp.where((gi >= 0) & (gi < 255), 0.5 * (ra + 0.5), 0.0)
    nothing = jnp.zeros((8, 128), F32)
    columns = range(Z // 128)

    def cut(it):
        it = it % RT
        return slice(it * 8, it * 8 + 8)

    def vec(ref, t, it, v):
        return ref[t, cut(it), v * 128:v * 128 + 128]

    def put(ref, t, it, v, x):
        ref[t, cut(it), v * 128:v * 128 + 128] = x

    def up_row(x):
        return pltpu.roll(x, 7, 0)

    def down_row(x):
        return pltpu.roll(x, 1, 0)

    def next_lane(row, v, cur):
        nxt = pltpu.roll(row[v + 1], 127, 1) if v + 1 < Z // 128 else cur
        return jnp.where(last_lane, nxt, cur), nxt

    def relaxed(old, row, t, it, v, p, pz, pu, prev, zprev, tu, td, r, z, w, s):
        acc = (tu * vec(old, t + 1, it, v) + td * vec(old, t - 1, it, v)) + r * pu
        rp = down_row(r * p)
        acc = acc + jnp.where(bottom, prev, rp)
        zu, pz = next_lane(row, v, pz)
        zp = pltpu.roll(z * p, 1, 1)
        acc = acc + (z * zu + jnp.where(first_lane, zprev, zp))
        return (1.0 - OMEGA) * p + w * (acc - s), pz, rp, zp

    def first_sweep(t, _):
        last = RT - 1
        bc = [vec(beta, t, 0, v) for v in columns]
        pc = [vec(pa, t, 0, v) for v in columns]
        fprev, prev = [], []
        for v in columns:
            b = vec(beta, t, last, v)
            face = (b + jnp.where(top, up_row(bc[v]), up_row(b))) * rads[2, last]
            fprev.append(down_row(face))
            prev.append(down_row(face * vec(pa, t, last, v)))
        for it in range(RT):
            ra, ang, rad = rads[0, it], rads[1, it], rads[2, it]
            axi = (0.5 * AXIAL) * ra
            bz = pltpu.roll(bc[0], 127, 1)
            pz = pltpu.roll(pc[0], 127, 1)
            zfprev = zprev = nothing
            for v in columns:
                b, p = bc[v], pc[v]
                nb, np_ = vec(beta, t, it + 1, v), vec(pa, t, it + 1, v)
                tu = (b + vec(beta, t + 1, it, v)) * ang
                td = vec(th, t - 1, it, v)
                r = (b + jnp.where(top, up_row(nb), up_row(b))) * rad
                froll = down_row(r)
                other = jnp.where(bottom, fprev[v], froll)
                bu, bz = next_lane(bc, v, bz)
                zf = (b + bu) * axi
                z = zf
                if v == Z // 128 - 1:
                    zf = jnp.where(last_lane, 2.0 * (b * axi), zf)
                    z = jnp.where(last_lane, 0.0, zf)
                zr = pltpu.roll(z, 1, 1)
                d = (tu + td) + (r + other) + (zf + jnp.where(first_lane, zfprev, zr))
                if it == last:
                    d = jnp.where(d > 0.0, d, 1.0)
                w = pl.reciprocal(d, approx=True)
                w = w * (2.0 - d * w)
                w = (w * (2.0 - d * w)) * OMEGA
                sc = vec(ss, t, it, v) * ra
                put(th, t, it, v, tu)
                put(rr, t, it, v, r)
                put(zz, t, it, v, z)
                put(ww, t, it, v, w)
                put(ss, t, it, v, sc)
                pu = jnp.where(top, up_row(np_), up_row(p))
                new, pz, prev[v], zprev = relaxed(pa, pc, t, it, v, p, pz, pu, prev[v], zprev, tu, td, r, z, w, sc)
                put(pb, t, it, v, new)
                bc[v], pc[v], fprev[v], zfprev = nb, np_, froll, zr
        return 0

    def sweep(old, new, t, tiles, shift):
        pc = [vec(old, t, 0, v) for v in columns]
        pup = [up_row(p) for p in pc]
        prev = [down_row(vec(rr, t, -1, v) * vec(old, t, -1, v)) for v in columns]
        for it in range(tiles):
            pz = pltpu.roll(pc[0], 127, 1)
            zprev = nothing
            for v in columns:
                p = pc[v]
                np_ = vec(old, t, it + 1, v)
                nup = up_row(np_)
                pu = jnp.where(top, nup, pup[v])
                x, pz, prev[v], zprev = relaxed(
                    old, pc, t, it, v, p, pz, pu, prev[v], zprev, vec(th, t, it, v), vec(th, t - 1, it, v),
                    vec(rr, t, it, v), vec(zz, t, it, v), vec(ww, t, it, v), vec(ss, t, it, v))
                put(new, t - shift, it, v, x)
                pc[v], pup[v] = np_, nup
        return 0

    ends = (H - 1, H + half - 1, H + T - 1, TE - 1)
    start = 1
    for g in range(4):
        for c in waits[g]:
            c.wait()
        begin(g + 2)
        if g == 0:
            for it in range(RT):
                th[0, cut(it), :] = (beta[0, cut(it), :] + beta[1, cut(it), :]) * wide(rads[1, it])
        lax.fori_loop(start, ends[g], first_sweep, 0)
        start = ends[g]
    lax.fori_loop(2, TE - 2, lambda t, _: sweep(pb, pa, t, RT, 0), 0)
    lax.fori_loop(3, TE - 3, lambda t, _: sweep(pa, pb, t, RT, 0), 0)

    def final(t, _):
        sweep(pb, out, t, RT - 1, H)
        pltpu.make_async_copy(out.at[t - H], out_any.at[t - H], osems.at[t - H]).start()
        return 0

    lax.fori_loop(4, TE - 4, final, 0)
    for t in range(T):
        pltpu.make_async_copy(out.at[t], out_any.at[t], osems.at[t]).wait()


def from_all(copies, axes):
    return lax.all_to_all(copies, axes, 0, 0)


def sum_kernel(parts, *refs):
    out = refs[-1]
    s = parts[0]
    for n in range(1, parts.shape[0]):
        s = s + parts[n]
    for n in range(out.shape[0]):
        out[n] = s


VM = pl.BlockSpec(memory_space=pltpu.VMEM)
SM = pl.BlockSpec(memory_space=pltpu.SMEM)
ANY = pl.BlockSpec(memory_space=pltpu.HBM)


def params(mib):
    return pltpu.CompilerParams(vmem_limit_bytes=62 << 20)


def cost(us):
    return pl.CostEstimate(flops=1000, bytes_accessed=us * 3000000, transcendentals=0)


def per_device(load, outflow, beta, heat, label, vertex, share, tally, prior, weight, jump, solve):
    label = label.reshape(GROUPS, SLOTS)
    vertex = vertex.reshape(GROUPS, SLOTS)
    share = share.reshape(GROUPS, SLOTS)
    tally = tally.reshape(GROUPS)
    kidx = lax.axis_index("rad").astype(I32).reshape(1)
    nodes = lambda v: v.reshape(BS, NB)

    shape = lambda *d: jax.ShapeDtypeStruct(d, F32)
    slot = jax.ShapeDtypeStruct((GROUPS, SLOTS), I32)
    plane = lambda n: shape(n, R, Z)
    tile = lambda n: shape(n, 8, Z)
    block = pltpu.VMEM((T, R, Z), F32)
    up, down, rup, rdown, front, row, lane = pl.pallas_call(
        pack_kernel,
        out_shape=(plane(2 * H), plane(2 * H), tile(2 * T + FT), tile(2 * T + FT), tile(FT), slot, slot),
        in_specs=[ANY] * 2 + [VM] * 5, out_specs=(ANY,) * 5 + (VM,) * 2,
        scratch_shapes=[block, block, pltpu.VMEM((FT, 8, Z), F32), pltpu.VMEM((128, 128), F32),
                        pltpu.SemaphoreType.DMA((2,)), pltpu.SemaphoreType.DMA((8,)), pltpu.SemaphoreType.DMA((3,))],
        compiler_params=params(10), cost_estimate=cost(4), name="pack",
    )(load, beta, solve.reshape(BS * BS, NB), nodes(prior), nodes(weight), nodes(jump), label)
    lo, hi = shift_azim(up, 1), shift_azim(down, -1)
    ring = lambda x, d: lax.ppermute(x, "rad", [(i, (i + d) % 4) for i in range(4)])
    rhi, rlo, across = ring(rdown, -1), ring(rup, 1), ring(front, 2)

    partial = pl.pallas_call(
        flux_kernel, out_shape=shape(8, GROUPS * BS, NB),
        in_specs=[SM, SM, ANY, VM, VM, VM], out_specs=VM,
        scratch_shapes=[block, pltpu.VMEM((T * R * 8, 128), F32), pltpu.VMEM((128, 128), F32),
                        pltpu.VMEM((8, SLOTS), F32),
                        pltpu.SemaphoreType.DMA((T,))],
        compiler_params=params(12), cost_estimate=cost(10), name="flux",
    )(tally, row, heat, lane, vertex, share)
    side, eup, edown = pl.pallas_call(
        side_kernel, out_shape=(tile(2 * T), tile(2 * H), tile(2 * H)),
        in_specs=[SM, ANY, ANY], out_specs=(VM,) * 3,
        scratch_shapes=[pltpu.VMEM((2 * T, 8, Z), F32), pltpu.SemaphoreType.DMA((2,))],
        compiler_params=params(4), cost_estimate=cost(2), name="side",
    )(kidx, rhi, rlo)
    clo, chi = shift_azim(eup, 1), shift_azim(edown, -1)
    near = pl.pallas_call(
        sum_kernel, out_shape=shape(16, GROUPS * BS, NB),
        in_specs=[VM, ANY, ANY], out_specs=VM, compiler_params=params(4), name="near",
    )(from_all(partial, ("z", "core")), side, across)
    flux = from_all(near, ("y", "rad"))
    source, sup, sdown, srup, srdown, height = pl.pallas_call(
        front_kernel,
        out_shape=(plane(T), plane(H - 1), plane(H - 1), tile(T), tile(T), shape(BS, NB)),
        in_specs=[SM, SM, SM, VM] + [ANY] * 4 + [VM] * 3 + [ANY] * 6, out_specs=(ANY,) * 5 + (VM,),
        scratch_shapes=[pltpu.VMEM((GROUPS, FT, 8, Z), F32),
                        pltpu.VMEM((GROUPS, BS, NB), F32), pltpu.VMEM((GROUPS, BS, NB), F32),
                        pltpu.VMEM((GROUPS, SLOTS, 128), F32), pltpu.VMEM((GROUPS * BS, NB), F32),
                        block, pltpu.VMEM((R * 8, 128), F32), pltpu.VMEM((128, 128), F32),
                        pltpu.SemaphoreType.DMA((1,)), pltpu.SemaphoreType.DMA((GROUPS, T)),
                        pltpu.SemaphoreType.DMA((GROUPS,)), pltpu.SemaphoreType.DMA((4, T))]
        + [pltpu.VMEM((T * R * 8, 128), F32)] * GROUPS,
        compiler_params=params(20), cost_estimate=cost(10), name="front",
    )(kidx, tally, row, flux, front, rhi, rlo, across, lane, vertex, share, outflow, lo, hi, side, clo, chi)
    slo, shi = shift_azim(sup, 1), shift_azim(sdown, -1)
    sside = ring_tile(shift_rad(srdown, -1), shift_rad(srup, 1))
    sclo, schi = shift_azim(sside[T - H + 1:], 1), shift_azim(sside[:H - 1], -1)
    ext = pltpu.VMEM((TE, RE, Z), F32)
    pressure = pl.pallas_call(
        sweep_kernel, out_shape=plane(T),
        in_specs=[SM] + [ANY] * 13, out_specs=ANY,
        scratch_shapes=[ext] * 8 + [pltpu.VMEM((3, RT, 8, 128), F32), block, pltpu.SemaphoreType.DMA((4, 3, 2)),
                        pltpu.SemaphoreType.DMA((T,))],
        compiler_params=params(46), cost_estimate=cost(20), name="sweeps",
    )(kidx, load, beta, lo, hi, side, clo, chi, source, slo, shi, sside, sclo, schi)
    return pressure, height.reshape(NB * BS)


def solution(mesh):
    fine = jax.sharding.Mesh(mesh.devices.reshape(4, 4, 2, 4), AZIM + ("rad",))
    cells = P(AZIM, "rad", None)
    slots = P(AZIM, "rad", None, None)
    return jax.shard_map(
        per_device,
        mesh=fine,
        in_specs=(cells, cells, cells, cells, slots, slots, slots, cells,
                  P("rad"), P("rad"), P("rad"), P(None, None, "rad")),
        out_specs=(cells, P("rad")),
        check_vma=False,
    )
```
